256 devices in a mesh: table: 8 (over y, core), seq: 8 (over z), tensor: 4 (over x).
Axes of the slice: x: 4, y: 4, z: 8, core: 2. Of those that a mesh axis runs over, the one named last changes fastest.
Arguments:
- table: bfloat16 [131072, 512], P(('table', 'seq'), 'tensor'), may hold values from -6 to 6
- owner: int32 [65536, 1], P(('table', 'seq')), may hold values from 0 to 63; in each aligned block of 1024 rows (0 to 1023, 1024 to 2047, ...) at most 24 rows name the same one
- local_row: int32 [65536], P(('table', 'seq')), may hold values from 0 to 2047
- segment_ids: int32 [64, 1024], P(('table', 'seq')), may hold values from 0 to 3, never falling along the last dimension, each value on 1 to 512 neighbouring positions
- proj_in: bfloat16 [4, 512, 512], P(None, None, 'tensor'), may hold values from -0.25 to 0.25
- proj_out: bfloat16 [512, 512], P('tensor'), may hold values from -0.25 to 0.25
- grad_out: bfloat16 [65536, 512], P(('table', 'seq'), 'tensor'), may hold values from -6 to 6
Outputs:
- layer_out: bfloat16 [65536, 512], P(('table', 'seq'), 'tensor')
- table_grad: float32 [131072, 512], P(('table', 'seq'), 'tensor')
- proj_in_grad: float32 [4, 512, 512], P(None, None, 'tensor')
- proj_out_grad: float32 [512, 512], P('tensor')
The draws below stay inside these ranges and needn't reach their ends.
Inputs may be any that keep to these rules, and one draw needn't show every extreme that they name: Among the events of one owner block, each owner is named at most 24 times, a bound that some block reaches. `segment_ids`: within a row, ids never fall; each history has 1 to 512 events, one exactly 512.
All inputs are finite; a program needn't handle non-finite values.
Results may differ from the reference program's by a relative error of at most 0.02.
Values may be sent and summed in bfloat16 or wider, within the bound.
No kernel may reach another device: no remote copies, remote signals or barrier semaphores. Data moves between devices by JAX's collectives and lax.ppermute only.
A program may use at most 64 MiB of HBM per device.

```python
import math
import jax
import jax.numpy as jnp
import numpy as np
from jax import lax

D = 512
HD = 128
HH = 512
TOK_DEV = 1024
SEQ_DEV = 4
SEQ_MOST = 512
ROWS_DEV = 2048
N_OWN = 64
CAP = 24
TOKENS = 65536
ROWS = 131072
N_TENSOR = 4


def touch_ends(drawn, stream_key, low, high):
    shape = drawn.shape
    index_at = [jax.random.randint(jax.random.fold_in(stream_key, axis), (), 0, shape[axis]) for axis in range(len(shape))]
    drawn = drawn.at[tuple(index_at)].set(low)
    longest = shape.index(max(shape))
    index_at[longest] = (index_at[longest] + 1) % shape[longest]
    return drawn.at[tuple(index_at)].set(high)


def block_scale(own_key, dims, shards, smallest, top_value):
    gain, own = 1.0, jax.random.fold_in(own_key, 6)
    for axis_at, blocks in shards:
        draws = jnp.exp(jax.random.uniform(jax.random.fold_in(own, axis_at), (blocks,), jnp.float32, smallest / len(shards), top_value / len(shards)))
        gain = gain * jnp.repeat(draws, dims[axis_at] // blocks).reshape([-1 if axis == axis_at else 1 for axis in range(len(dims))])
    return gain


def profile(number_of, total, limit, skew):
    loads = [(1 << 20) // math.isqrt(rank ** skew) + 1 for rank in range(2, number_of + 1)]
    rest, counts = total - limit - (number_of - 1), [1] * (number_of - 1)
    while rest > 0:
        candidates = [i for i in range(number_of - 1) if counts[i] < limit]
        whole, remaining = sum([loads[i] for i in candidates]), rest
        for i in candidates:
            extra = min(limit - counts[i], max(1, remaining * loads[i] // whole), rest)
            counts[i] = counts[i] + extra
            rest = rest - extra
    return np.array([limit] + counts)


def ragged(stream_key, amount, total, bound, slope):
    if amount == 2:
        one = jax.random.randint(stream_key, (), max(1, total - bound), min(bound, total - 1) + 1)
        return jnp.stack([one, total - one])
    lengths = jnp.asarray(profile(amount, total, bound, slope), jnp.int32)
    couples = (amount - 1) // 2
    donor, taker = lengths[1:1 + 2 * couples:2], lengths[2:2 + 2 * couples:2]
    margin = jnp.minimum(donor - 1, bound - taker)
    passed = jax.random.randint(jax.random.fold_in(stream_key, 1), (couples,), 0, 1 << 20) % (margin + 1)
    lengths = lengths.at[1:1 + 2 * couples:2].set(donor - passed).at[2:2 + 2 * couples:2].set(taker + passed)
    return lengths[jax.random.permutation(jax.random.fold_in(stream_key, 2), amount)]


def routed_block(own_key, own, number, rows, count, top, most, lean):
    order = jax.random.permutation(own_key, count)
    heavy_load, ordinary = portions_of(count, rows * top, most, lean, True), portions_of(count, rows * top, most, lean, False)
    places = jnp.arange(count)

    def named(lengths, offset_by):
        used = int((lengths > 0).sum())
        fixed = max(1, used // 4)
        passed = fixed + (places - fixed + offset_by * (used - fixed)) % max(1, count - fixed)
        return jnp.zeros((count,), jnp.int32).at[order[jnp.where(places < fixed, places, passed)]].set(jnp.asarray(lengths, jnp.int32))

    lengths = jnp.where(number % 4 == 0, named(heavy_load, number // 4), named(ordinary, number - number // 4 - 1))
    mixed = jax.random.permutation(jax.random.fold_in(own, 3), count)
    donor, receiver = mixed[0:count // 2 * 2:2], mixed[1:count // 2 * 2:2]
    slack = jnp.minimum(lengths[donor] - 1, most - lengths[receiver]) // 2
    slack = jnp.where((donor == order[0]) | (receiver == order[0]) | (lengths[receiver] == 0), 0, jnp.maximum(slack, 0))
    passed = jax.random.randint(jax.random.fold_in(own, 4), (count // 2,), 0, 1 << 20) % (slack + 1)
    lengths = lengths.at[donor].add(-passed).at[receiver].add(passed)
    members = jnp.searchsorted(jnp.cumsum(lengths), jnp.arange(rows * top), side="right").astype(jnp.int32)
    listing = members.reshape(top, rows).T
    listing = listing[jax.random.permutation(jax.random.fold_in(own, 1), rows)]
    offset_by = jax.random.randint(jax.random.fold_in(own, 2), (rows, 1), 0, top)
    return jnp.take_along_axis(listing, (jnp.arange(top)[None, :] + offset_by) % top, axis=1)


def portions_of(amount, total, bound, lean, full):
    weights = [(1 << 20) // math.isqrt(grade ** lean) + 1 for grade in range(1, amount + 1)]
    largest = bound if full else min(bound, max(-(-total // amount), total * weights[0] // sum(weights)))
    least = 1 if total - largest >= amount - 1 else 0
    counts, surplus = [largest] + [least] * (amount - 1), total - largest - least * (amount - 1)
    while surplus > 0:
        candidates = [i for i in range(1, amount) if counts[i] < largest] or [i for i in range(1, amount) if counts[i] < bound]
        pool, remaining = sum([weights[i] for i in candidates]), surplus
        for i in candidates:
            more = min(bound - counts[i], max(1, remaining * weights[i] // pool), surplus)
            counts[i] = counts[i] + more
            surplus = surplus - more
    return np.array(counts)


def bell_draw(rng, extent, spread, limit, split=(), kind=jnp.bfloat16):
    values = jax.random.normal(rng, extent, jnp.float32) * spread
    if len(split) > 0:
        values = block_scale(rng, extent, split, -0.22, 0.18) * values
    return jnp.clip(values, min=-limit, max=limit).astype(kind)


def setup_inputs(seed: int = 0) -> dict:
    splits = jax.random.split(jax.random.key(seed), 8)
    table = bell_draw(splits[0], (ROWS, D), 1.0, 6.0, ((0, 64), (1, 4)))
    owner_keys = jax.random.split(jax.random.fold_in(splits[1], 1), TOKENS // TOK_DEV)
    owner_turns = jax.random.permutation(jax.random.fold_in(splits[1], 3), TOKENS // TOK_DEV)
    owner = jax.vmap(lambda own, number: routed_block(jax.random.fold_in(splits[1], 2), own, number, TOK_DEV, N_OWN, 1, CAP, 2))(owner_keys, owner_turns).reshape((TOKENS, 1))
    local_row = touch_ends(jax.random.randint(splits[2], (TOKENS,), 0, ROWS_DEV), jax.random.fold_in(splits[2], 1), 0, ROWS_DEV - 1).astype(jnp.int32)
    segment_ids = jax.vmap(lambda own: jnp.searchsorted(jnp.cumsum(ragged(own, SEQ_DEV, TOK_DEV, SEQ_MOST, 2)), jnp.arange(TOK_DEV), side="right"))(jax.random.split(splits[3], N_OWN)).reshape((N_OWN, TOK_DEV)).astype(jnp.int32)
    proj_in = bell_draw(splits[4], (4, D, HH), D ** -0.5, 0.25, ((2, 4),))
    proj_out = bell_draw(splits[5], (HH, D), HH ** -0.5, 0.25, ((0, 4),))
    grad_out = bell_draw(splits[6], (TOKENS, D), 1.0, 6.0, ((0, 64), (1, 4)))
    return {"table": table, "owner": owner, "local_row": local_row, "segment_ids": segment_ids, "proj_in": proj_in, "proj_out": proj_out, "grad_out": grad_out}


def branch(xf, w_in, w_out, seg):
    tok = xf.shape[0]
    mean = lax.optimization_barrier(jnp.mean(xf, axis=1, keepdims=True))
    var = lax.optimization_barrier(jnp.mean((xf - mean) ** 2, axis=1, keepdims=True))
    normed = ((xf - mean) * lax.rsqrt(var + 1e-05)).astype(jnp.bfloat16)
    parts = [jax.nn.silu(jnp.dot(normed, w_in[c], preferred_element_type=jnp.float32)).astype(jnp.bfloat16) for c in range(4)]
    gate_part, values, queries, keys = parts
    heads = values.shape[1] // HD
    block = min(512, tok)
    position = jnp.arange(tok)
    head_outs = []
    for head in range(heads):
        lo = head * HD
        key_head = keys[:, lo:lo + HD]
        value_head = values[:, lo:lo + HD]
        pieces = []
        for start in range(0, tok, block):
            query_block = queries[start:start + block, lo:lo + HD]
            scores = jnp.dot(query_block, key_head.T, preferred_element_type=jnp.float32) * HD ** (-0.5)
            qpos = position[start:start + block]
            allowed = (seg[start:start + block][:, None] == seg[None, :]) & (position[None, :] <= qpos[:, None])
            weights = (jnp.where(allowed, jax.nn.silu(scores), 0.0) / SEQ_MOST).astype(jnp.bfloat16)
            pieces.append(jnp.dot(weights, value_head, preferred_element_type=jnp.float32))
        attended = jnp.concatenate(pieces, axis=0)
        head_mean = lax.optimization_barrier(jnp.mean(attended, axis=1, keepdims=True))
        head_var = lax.optimization_barrier(jnp.mean((attended - head_mean) ** 2, axis=1, keepdims=True))
        head_outs.append((attended - head_mean) * lax.rsqrt(head_var + 1e-05))
    mixed = (jnp.concatenate(head_outs, axis=1) * gate_part.astype(jnp.float32)).astype(jnp.bfloat16)
    return jnp.dot(mixed, w_out, preferred_element_type=jnp.float32)

def reference(table, owner, local_row, segment_ids, proj_in, proj_out, grad_out):
    row_ids = (owner[:, 0] * ROWS_DEV + local_row).astype(jnp.int32)
    embedded = table[row_ids]
    group = HH // N_TENSOR
    blocks_x = embedded.reshape(N_OWN, TOK_DEV, D)
    blocks_g = grad_out.reshape(N_OWN, TOK_DEV, D)

    def device_step(carry, inputs):
        rows, seg, cot = inputs
        xf = rows.astype(jnp.float32)
        cot_f = cot.astype(jnp.float32)
        total = jnp.zeros((TOK_DEV, D), jnp.float32)
        dx_total = cot_f
        in_parts = []
        out_parts = []
        for group_idx in range(N_TENSOR):
            w_in = proj_in[:, :, group_idx * group:(group_idx + 1) * group]
            w_out = proj_out[group_idx * group:(group_idx + 1) * group]
            result, pull = jax.vjp(lambda a, b, c: branch(a, b, c, seg), xf, w_in, w_out)
            d_x, d_in, d_out = pull(cot_f)
            total = total + result
            dx_total = dx_total + d_x
            in_parts.append(d_in.astype(jnp.float32))
            out_parts.append(d_out.astype(jnp.float32))
        out_rows = (xf + total).astype(jnp.bfloat16)
        new_carry = (carry[0] + jnp.concatenate(in_parts, axis=2), carry[1] + jnp.concatenate(out_parts, axis=0))
        return (new_carry, (out_rows, dx_total))
    init = (jnp.zeros((4, D, HH), jnp.float32), jnp.zeros((HH, D), jnp.float32))
    (grad_in, grad_outw), (outs, dxs) = lax.scan(device_step, init, (blocks_x, segment_ids, blocks_g))
    layer_out = outs.reshape(TOKENS, D)
    table_grad = jnp.zeros((ROWS, D), jnp.float32).at[row_ids].add(dxs.reshape(TOKENS, D))
    return (layer_out, table_grad, grad_in, grad_outw)
```

```python
import functools

import jax
import jax.numpy as jnp
from jax import lax
from jax.experimental import pallas as pl
from jax.experimental.pallas import tpu as pltpu
from jax.sharding import PartitionSpec as P

HD = 128
SEQ_MOST = 512
TOK = 1024
D = 512
NT = 4
NOWN = 64
CAP = 24
SLOTS = NOWN * CAP
ROWS = 2048
QB = 256
BOTH = ("table", "seq")
BF = jnp.bfloat16
F32 = jnp.float32
I32 = jnp.int32
VM = pl.BlockSpec(memory_space=pltpu.VMEM)
SM = pl.BlockSpec(memory_space=pltpu.SMEM)
PARAMS = pltpu.CompilerParams(vmem_limit_bytes=56 * 1024 * 1024)


def iota(shape, dim):
    return lax.broadcasted_iota(I32, shape, dim)


def dot(a, b, ca, cb):
    return lax.dot_general(a, b, (((ca,), (cb,)), ((), ())), preferred_element_type=F32)


def route_kernel(owner_ref, row_ref, req_ref, slot_ref):
    upper = (iota((128, 128), 0) < iota((128, 128), 1)).astype(BF)
    ones = jnp.ones((128, 128), BF)
    scan = jnp.concatenate([upper, ones], axis=1)
    carry = jnp.zeros((NOWN, 128), F32)
    high = jnp.zeros((NOWN, 128), F32)
    low = jnp.zeros((NOWN, 128), F32)
    for b in range(TOK // 128):
        own = owner_ref[b : b + 1, :]
        row = row_ref[b : b + 1, :]
        hot = iota((NOWN, 128), 0) == own
        hot_f = hot.astype(F32)
        hot_b = hot_f.astype(BF)
        sums = dot(hot_b, scan, 1, 0)
        rank = jnp.sum(hot_f * (sums[:, :128] + carry), axis=0, keepdims=True)
        carry = carry + sums[:, 128:]
        rank_i = rank.astype(I32)
        slot_ref[b : b + 1, :] = own * CAP + rank_i
        place = iota((128, 128), 0) == rank_i
        row_hi = jnp.where(place, (row >> 6).astype(F32), 0.0).astype(BF)
        row_lo = jnp.where(place, (row & 63).astype(F32), 0.0).astype(BF)
        high = high + dot(hot_b, row_hi, 1, 1)
        low = low + dot(hot_b, row_lo, 1, 1)
    req_ref[...] = high.astype(I32) * 64 + low.astype(I32)


def route(owner, row):
    return pl.pallas_call(
        route_kernel,
        out_shape=(
            jax.ShapeDtypeStruct((NOWN, 128), I32),
            jax.ShapeDtypeStruct((TOK // 128, 128), I32),
        ),
        in_specs=[VM, VM],
        out_specs=(VM, VM),
        compiler_params=PARAMS,
        name="route",
    )(owner, row)


def fetch_kernel(req_ref, table_ref, out_ref, wide, got):
    wide[...] = table_ref[...].astype(F32)

    def step(r, carry):
        for c in range(CAP):
            got[pl.ds(r * CAP + c, 1), :] = wide[pl.ds(req_ref[r, c], 1), :]
        return carry

    lax.fori_loop(0, NOWN, step, 0)
    out_ref[...] = got[...].astype(BF)


def fetch(req, table):
    return pl.pallas_call(
        fetch_kernel,
        out_shape=jax.ShapeDtypeStruct((SLOTS, 128), BF),
        in_specs=[SM, VM],
        out_specs=VM,
        scratch_shapes=[pltpu.VMEM((ROWS, 128), F32), pltpu.VMEM((SLOTS, 128), F32)],
        compiler_params=PARAMS,
        name="fetch",
    )(req, table)


def column(row_vector):
    wide = jnp.broadcast_to(row_vector.astype(F32), (128, 128))
    return jnp.transpose(wide)


def place_kernel(slot_ref, back_ref, x_ref):
    back = back_ref[...]
    for b in range(TOK // 128):
        col = column(slot_ref[b : b + 1, :]).astype(I32)
        hot = jnp.concatenate(
            [(col == iota((128, 128), 1) + 128 * k).astype(F32).astype(BF) for k in range(SLOTS // 128)],
            axis=1,
        )
        x_ref[b * 128 : (b + 1) * 128, :] = dot(hot, back, 1, 0).astype(BF)


def place(slot, back):
    return pl.pallas_call(
        place_kernel,
        out_shape=jax.ShapeDtypeStruct((TOK, 128), BF),
        in_specs=[VM, VM],
        out_specs=VM,
        compiler_params=PARAMS,
        name="place",
    )(slot, back)


def layer_kernel(
    pos_ref, seg_ref, x0, x1, x2, x3, g0, g1, g2, g3, win_ref, wout_ref,
    dx0, dx1, dx2, dx3, u_ref, y_ref, dp_ref,
    w, wo, pre, act, segc, aw, dsil, dout, dkv, du,
):
    xs, gs, dxs = (x0, x1, x2, x3), (g0, g1, g2, g3), (dx0, dx1, dx2, dx3)
    me = pos_ref[0]
    for k in range(NT):
        at = pl.multiple_of(lax.rem(me + k, NT) * 128, 128)
        for c in range(4):
            w[k * 128 : (k + 1) * 128, c * 128 : (c + 1) * 128] = win_ref[c, pl.ds(at, 128), :]
        wo[:, k * 128 : (k + 1) * 128] = wout_ref[:, pl.ds(at, 128)]
    for b in range(TOK // 128):
        segc[b * 128 : (b + 1) * 128, :] = column(
            seg_ref[0:1, b * 128 : (b + 1) * 128]
        )

    def stats(r0, n):
        x = [r[r0 : r0 + n, :].astype(F32) for r in xs]
        mean = jnp.sum(x[0] + x[1] + x[2] + x[3], axis=1, keepdims=True) * (1.0 / D)
        x = [v - mean for v in x]
        var = jnp.sum(x[0] * x[0] + x[1] * x[1] + x[2] * x[2] + x[3] * x[3], axis=1, keepdims=True)
        scale = lax.rsqrt(var * (1.0 / D) + 1e-05)
        return [v * scale for v in x], scale

    step = 64
    for q in range(TOK // QB):
        lo = q * QB
        for r0 in range(lo, lo + QB, step):
            n, _ = stats(r0, step)
            for k in range(NT):
                u_ref[r0 : r0 + step, k * 128 : (k + 1) * 128] = n[k].astype(BF)
        pre[lo : lo + QB, :] = dot(u_ref[lo : lo + QB, :], w[...], 1, 0)
        for r0 in range(lo, lo + QB, step):
            p = pre[r0 : r0 + step, :]
            s = 0.5 + 0.5 * jnp.tanh(0.5 * p)
            ps = p * s
            act[r0 : r0 + step, :] = ps.astype(BF)
            pre[r0 : r0 + step, :] = s + ps * (1.0 - s)

    dkv[...] = jnp.zeros((TOK, 256), F32)
    for q in range(TOK // QB):
        lo = q * QB
        k0 = max(0, lo - SEQ_MOST)
        width = lo + QB - k0
        queries = act[lo : lo + QB, 256:384]
        o = jnp.zeros((QB, HD), F32)
        for kb in range(k0, lo + QB, QB):
            sc = dot(queries, act[kb : kb + QB, 384:512], 1, 1) * (HD ** (-0.5))
            for j in range(0, QB, 128):
                same = segc[lo : lo + QB, :] == seg_ref[0:1, kb + j : kb + j + 128].astype(F32)
                if kb == lo:
                    same = same & (iota((QB, 128), 1) + j <= iota((QB, 128), 0))
                v = sc[:, j : j + 128]
                s = 0.5 + 0.5 * jnp.tanh(0.5 * v)
                vs = v * s
                at = kb - k0 + j
                aw[:, at : at + 128] = jnp.where(same, vs * (1.0 / SEQ_MOST), 0.0).astype(BF)
                dsil[:, at : at + 128] = jnp.where(
                    same, (s + vs * (1.0 - s)) * (HD ** (-0.5) / SEQ_MOST), 0.0
                )
        o = dot(aw[:, 0:width], act[k0 : lo + QB, 128:256], 1, 0)
        gate = act[lo : lo + QB, 0:128].astype(F32)
        mean = jnp.sum(o, axis=1, keepdims=True) * (1.0 / HD)
        o = o - mean
        scale = lax.rsqrt(jnp.sum(o * o, axis=1, keepdims=True) * (1.0 / HD) + 1e-05)
        n = o * scale
        y_ref[lo : lo + QB, :] = (n * gate).astype(BF)
        dy = dot(gs[0][lo : lo + QB, :], wo[:, 0:128], 1, 1)
        for k in range(1, NT):
            dy = dy + dot(gs[k][lo : lo + QB, :], wo[:, k * 128 : (k + 1) * 128], 1, 1)
        dy = dy.astype(BF).astype(F32)
        dgate = (dy * n).astype(BF).astype(F32)
        dn = dy * gate
        m1 = jnp.sum(dn, axis=1, keepdims=True) * (1.0 / HD)
        m2 = jnp.sum(dn * n, axis=1, keepdims=True) * (1.0 / HD)
        do = ((dn - m1 - n * m2) * scale).astype(BF)
        dp_ref[lo : lo + QB, 0:128] = (dgate * pre[lo : lo + QB, 0:128]).astype(BF)
        dq = jnp.zeros((QB, HD), F32)
        for kb in range(k0, lo + QB, QB):
            at = kb - k0
            da = dot(do, act[kb : kb + QB, 128:256], 1, 1).astype(BF).astype(F32)
            ds = (da * dsil[:, at : at + QB]).astype(BF)
            dq = dq + dot(ds, act[kb : kb + QB, 384:512], 1, 0)
            dkv[kb : kb + QB, 0:128] += dot(aw[:, at : at + QB], do, 0, 0)
            dkv[kb : kb + QB, 128:256] += dot(ds, queries, 0, 0)
        dq = dq.astype(BF).astype(F32)
        dp_ref[lo : lo + QB, 256:384] = (dq * pre[lo : lo + QB, 256:384]).astype(BF)

    for q in range(TOK // QB):
        lo = q * QB
        dvb = dkv[lo : lo + QB, 0:128].astype(BF).astype(F32)
        dkb = dkv[lo : lo + QB, 128:256].astype(BF).astype(F32)
        dp_ref[lo : lo + QB, 128:256] = (dvb * pre[lo : lo + QB, 128:256]).astype(BF)
        dp_ref[lo : lo + QB, 384:512] = (dkb * pre[lo : lo + QB, 384:512]).astype(BF)
        du[...] = dot(dp_ref[lo : lo + QB, :], w[...], 1, 1).astype(BF).astype(F32)
        for r in range(0, QB, step):
            n, scale = stats(lo + r, step)
            d = [du[r : r + step, k * 128 : (k + 1) * 128] for k in range(NT)]
            m1 = jnp.sum(d[0] + d[1] + d[2] + d[3], axis=1, keepdims=True) * (1.0 / D)
            m2 = jnp.sum(
                d[0] * n[0] + d[1] * n[1] + d[2] * n[2] + d[3] * n[3], axis=1, keepdims=True
            ) * (1.0 / D)
            for k in range(NT):
                dxs[k][lo + r : lo + r + step, :] = ((d[k] - m1 - n[k] * m2) * scale).astype(BF)


def layer(pos, seg, xs, gs, w_in, w_out):
    piece = jax.ShapeDtypeStruct((TOK, 128), BF)
    wide = jax.ShapeDtypeStruct((TOK, D), BF)
    return pl.pallas_call(
        layer_kernel,
        out_shape=(piece,) * 4 + (wide, piece, wide),
        in_specs=[SM] + [VM] * 11,
        out_specs=(VM,) * 7,
        scratch_shapes=[
            pltpu.VMEM((D, 512), BF),
            pltpu.VMEM((HD, D), BF),
            pltpu.VMEM((TOK, 512), F32),
            pltpu.VMEM((TOK, 512), BF),
            pltpu.VMEM((TOK, 128), F32),
            pltpu.VMEM((QB, 768), BF),
            pltpu.VMEM((QB, 768), F32),
            pltpu.VMEM((QB, 128), BF),
            pltpu.VMEM((TOK, 256), F32),
            pltpu.VMEM((QB, 512), F32),
        ],
        compiler_params=PARAMS,
        name="layer",
    )(pos, seg, *xs, *gs, w_in, w_out)


def proj_kernel(pos_ref, y_ref, u_ref, dp_ref, g0, g1, g2, g3, wout_ref, z0, z1, z2, z3, dw_ref):
    me = pos_ref[0]
    gs, zs = (g0, g1, g2, g3), (z0, z1, z2, z3)
    for k in range(NT):
        feat = lax.rem(me + k, NT)
        at = pl.multiple_of(feat * 128, 128)
        zs[k][...] = dot(y_ref[...], wout_ref[:, pl.ds(at, 128)], 1, 0).astype(BF)
        dw = dot(u_ref[:, k * 128 : (k + 1) * 128], dp_ref[...], 0, 0)
        for c in range(4):
            dw_ref[pl.ds(pl.multiple_of(c * 512 + at, 128), 128), :] = dw[:, c * 128 : (c + 1) * 128]
        dw_ref[pl.ds(pl.multiple_of(2048 + at, 128), 128), :] = dot(y_ref[...], gs[k][...], 0, 0)


def project(pos, y, u, dp, gs, w_out):
    piece = jax.ShapeDtypeStruct((TOK, 128), BF)
    return pl.pallas_call(
        proj_kernel,
        out_shape=(piece,) * 4 + (jax.ShapeDtypeStruct((2560, 128), F32),),
        in_specs=[SM] + [VM] * 8,
        out_specs=(VM,) * 5,
        compiler_params=PARAMS,
        name="project",
    )(pos, y, u, dp, *gs, w_out)


def slots_kernel(slot_ref, grad_ref, d0, d1, d2, d3, out_ref):
    dx = grad_ref[...].astype(F32) + (
        d0[...].astype(F32) + d1[...].astype(F32) + d2[...].astype(F32) + d3[...].astype(F32)
    )
    dx = dx.astype(BF)
    for s in range(SLOTS // 128):
        hot = jnp.concatenate(
            [
                (slot_ref[b : b + 1, :] == iota((128, 128), 0) + 128 * s).astype(F32).astype(BF)
                for b in range(TOK // 128)
            ],
            axis=1,
        )
        out_ref[s * 128 : (s + 1) * 128, :] = dot(hot, dx, 1, 0).astype(BF)


def to_slots(slot, grad, parts):
    return pl.pallas_call(
        slots_kernel,
        out_shape=jax.ShapeDtypeStruct((SLOTS, 128), BF),
        in_specs=[VM] * 6,
        out_specs=VM,
        compiler_params=PARAMS,
        name="to_slots",
    )(slot, grad, *parts)


def add_rows_kernel(req_ref, arrived_ref, out_ref):
    arrived = arrived_ref[...]
    for s in range(ROWS // 128):
        hot = jnp.concatenate(
            [
                (req_ref[b : b + 1, :] == iota((128, 128), 0) + 128 * s).astype(F32).astype(BF)
                for b in range(SLOTS // 128)
            ],
            axis=1,
        )
        out_ref[s * 128 : (s + 1) * 128, :] = dot(hot, arrived, 1, 0)


def add_rows(req, arrived):
    return pl.pallas_call(
        add_rows_kernel,
        out_shape=jax.ShapeDtypeStruct((ROWS, 128), F32),
        in_specs=[VM, VM],
        out_specs=VM,
        compiler_params=PARAMS,
        name="add_rows",
    )(req, arrived)


def shift(x, axis, fn, n):
    return lax.ppermute(x, axis, [(i, fn(i)) for i in range(n)])


def gather_pieces(x):
    return [x] + [shift(x, "tensor", lambda i, k=k: (i - k) % NT, NT) for k in (1, 3, 2)]


def order(pieces):
    own, one, three, two = pieces
    return [own, one, two, three]


def scatter_pieces(parts):
    return [parts[0]] + [shift(parts[k], "tensor", lambda i, k=k: (i + k) % NT, NT) for k in (1, 3, 2)]


def pick(x, i):
    return lax.dynamic_index_in_dim(x, i, 0, keepdims=False)


def reduce_weights(part):
    at = lax.axis_index("table")
    core, y = at % 2, at // 2
    halves = part.reshape(2, 1280, 128)
    other = shift(pick(halves, 1 - core).astype(BF), "table", lambda i: i ^ 1, 8)
    mine = (pick(halves, core) + other.astype(F32)).reshape(4, 320, 128)
    total = pick(mine, y)
    got = [
        shift(pick(mine, (y + k) % 4).astype(BF), "table", lambda i, k=k: (i + 2 * k) % 8, 8)
        for k in range(1, 4)
    ]
    for v in got:
        total = total + v.astype(F32)
    for bit in (1, 2, 4):
        total = total.astype(BF)
        total = total.astype(F32) + shift(total, "seq", lambda i, b=bit: i ^ b, 8).astype(F32)
    total = total.astype(BF)
    parts = [total] + [
        shift(total, "table", lambda i, k=k: (i - 2 * k) % 8, 8) for k in range(1, 4)
    ]
    stacked = jnp.roll(jnp.stack(parts), y, axis=0).reshape(1280, 128)
    other = shift(stacked, "table", lambda i: i ^ 1, 8)
    whole = jnp.where(
        core == 0, jnp.concatenate([stacked, other]), jnp.concatenate([other, stacked])
    )
    return whole.astype(F32)


def body(table, owner, local_row, segment_ids, proj_in, proj_out, grad_out):
    pos = lax.axis_index("tensor").astype(I32).reshape(1)
    requests, slot = route(owner.reshape(8, 128), local_row.reshape(8, 128))
    gs = order(gather_pieces(grad_out))
    received = lax.all_to_all(requests, BOTH, split_axis=0, concat_axis=0, tiled=True)
    rows = fetch(received, table)
    back = lax.all_to_all(rows.reshape(NOWN, CAP, 128), BOTH, split_axis=0, concat_axis=0, tiled=True)
    x = place(slot, back.reshape(SLOTS, 128))
    xs = order(gather_pieces(x))
    d0, d1, d2, d3, u, y, dp = layer(pos, segment_ids, xs, gs, proj_in, proj_out)
    dparts = scatter_pieces([d0, d1, d2, d3])
    z0, z1, z2, z3, dw = project(pos, y, u, dp, gs, proj_out)
    grads = to_slots(slot, grad_out, dparts)
    arrived = lax.all_to_all(grads.reshape(NOWN, CAP, 128), BOTH, split_axis=0, concat_axis=0, tiled=True)
    zparts = scatter_pieces([z0, z1, z2, z3])
    layer_out = (
        x.astype(F32)
        + (zparts[0].astype(F32) + zparts[1].astype(F32) + zparts[2].astype(F32) + zparts[3].astype(F32))
    ).astype(BF)
    flat = received[:, :CAP].reshape(SLOTS // 128, 128)
    table_grad = add_rows(flat, arrived.reshape(SLOTS, 128))
    whole = reduce_weights(dw)
    grad_in = whole[:2048].reshape(4, 512, 128)
    grad_outw = whole[2048:].reshape(4, 128, 128).transpose(1, 0, 2).reshape(128, 512)
    return layer_out, table_grad, grad_in, grad_outw


def solution(mesh):
    in_specs = (
        P(BOTH, "tensor"),
        P(BOTH, None),
        P(BOTH),
        P(BOTH, None),
        P(None, None, "tensor"),
        P("tensor", None),
        P(BOTH, "tensor"),
    )
    out_specs = (
        P(BOTH, "tensor"),
        P(BOTH, "tensor"),
        P(None, None, "tensor"),
        P("tensor", None),
    )
    return jax.shard_map(body, mesh=mesh, in_specs=in_specs, out_specs=out_specs, check_vma=False)
```

```python
import functools

import jax
import jax.numpy as jnp
from jax import lax
from jax.experimental import pallas as pl
from jax.experimental.pallas import tpu as pltpu
from jax.sharding import PartitionSpec as P

HD = 128
SEQ_MOST = 512
TOK = 1024
D = 512
NT = 4
NOWN = 64
CAP = 24
SLOTS = NOWN * CAP
ROWS = 2048
QB = 256
BOTH = ("table", "seq")
BF = jnp.bfloat16
F32 = jnp.float32
I32 = jnp.int32
VM = pl.BlockSpec(memory_space=pltpu.VMEM)
SM = pl.BlockSpec(memory_space=pltpu.SMEM)
PARAMS = pltpu.CompilerParams(vmem_limit_bytes=56 * 1024 * 1024)


def iota(shape, dim):
    return lax.broadcasted_iota(I32, shape, dim)


def dot(a, b, ca, cb):
    return lax.dot_general(a, b, (((ca,), (cb,)), ((), ())), preferred_element_type=F32)


def route_kernel(owner_ref, row_ref, req_ref, slot_ref):
    upper = (iota((128, 128), 0) < iota((128, 128), 1)).astype(BF)
    ones = jnp.ones((128, 128), BF)
    scan = jnp.concatenate([upper, ones], axis=1)
    carry = jnp.zeros((NOWN, 128), F32)
    high = jnp.zeros((NOWN, 128), F32)
    low = jnp.zeros((NOWN, 128), F32)
    for b in range(TOK // 128):
        own = owner_ref[b : b + 1, :]
        row = row_ref[b : b + 1, :]
        hot = iota((NOWN, 128), 0) == own
        hot_f = hot.astype(F32)
        hot_b = hot_f.astype(BF)
        sums = dot(hot_b, scan, 1, 0)
        rank = jnp.sum(hot_f * (sums[:, :128] + carry), axis=0, keepdims=True)
        carry = carry + sums[:, 128:]
        rank_i = rank.astype(I32)
        slot_ref[b : b + 1, :] = own * CAP + rank_i
        place = iota((128, 128), 0) == rank_i
        row_hi = jnp.where(place, (row >> 6).astype(F32), 0.0).astype(BF)
        row_lo = jnp.where(place, (row & 63).astype(F32), 0.0).astype(BF)
        high = high + dot(hot_b, row_hi, 1, 1)
        low = low + dot(hot_b, row_lo, 1, 1)
    req_ref[...] = high.astype(I32) * 64 + low.astype(I32)


def route(owner, row):
    return pl.pallas_call(
        route_kernel,
        out_shape=(
            jax.ShapeDtypeStruct((NOWN, 128), I32),
            jax.ShapeDtypeStruct((TOK // 128, 128), I32),
        ),
        in_specs=[VM, VM],
        out_specs=(VM, VM),
        compiler_params=PARAMS,
        name="route",
    )(owner, row)


def fetch_kernel(req_ref, table_ref, out_ref, wide, got):
    wide[...] = table_ref[...].astype(F32)

    def step(r, carry):
        for c in range(CAP):
            got[pl.ds(r * CAP + c, 1), :] = wide[pl.ds(req_ref[r, c], 1), :]
        return carry

    lax.fori_loop(0, NOWN, step, 0)
    out_ref[...] = got[...].astype(BF)


def fetch(req, table):
    return pl.pallas_call(
        fetch_kernel,
        out_shape=jax.ShapeDtypeStruct((SLOTS, 128), BF),
        in_specs=[SM, VM],
        out_specs=VM,
        scratch_shapes=[pltpu.VMEM((ROWS, 128), F32), pltpu.VMEM((SLOTS, 128), F32)],
        compiler_params=PARAMS,
        name="fetch",
    )(req, table)


def column(row_vector):
    wide = jnp.broadcast_to(row_vector.astype(F32), (128, 128))
    return jnp.transpose(wide)


def place_kernel(slot_ref, back_ref, x_ref):
    back = back_ref[...]
    for b in range(TOK // 128):
        col = column(slot_ref[b : b + 1, :]).astype(I32)
        hot = jnp.concatenate(
            [(col == iota((128, 128), 1) + 128 * k).astype(F32).astype(BF) for k in range(SLOTS // 128)],
            axis=1,
        )
        x_ref[b * 128 : (b + 1) * 128, :] = dot(hot, back, 1, 0).astype(BF)


def place(slot, back):
    return pl.pallas_call(
        place_kernel,
        out_shape=jax.ShapeDtypeStruct((TOK, 128), BF),
        in_specs=[VM, VM],
        out_specs=VM,
        compiler_params=PARAMS,
        name="place",
    )(slot, back)


def normed(xs, r0, n):
    x = [r[r0 : r0 + n, :].astype(F32) for r in xs]
    mean = jnp.sum(x[0] + x[1] + x[2] + x[3], axis=1, keepdims=True) * (1.0 / D)
    x = [v - mean for v in x]
    var = jnp.sum(x[0] * x[0] + x[1] * x[1] + x[2] * x[2] + x[3] * x[3], axis=1, keepdims=True)
    scale = lax.rsqrt(var * (1.0 / D) + 1e-05)
    return [v * scale for v in x], scale


def layer_kernel(
    pos_ref, seg_ref, x0, x1, x2, x3, g0, g1, g2, g3, win_ref, wout_ref,
    u_ref, y_ref, dp_ref, w,
    wo, pre, act, segc, aw, dsil, dkv,
):
    xs, gs = (x0, x1, x2, x3), (g0, g1, g2, g3)
    me = pos_ref[0]
    for k in range(NT):
        at = pl.multiple_of(lax.rem(me + k, NT) * 128, 128)
        for c in range(4):
            w[k * 128 : (k + 1) * 128, c * 128 : (c + 1) * 128] = win_ref[c, pl.ds(at, 128), :]
        wo[:, k * 128 : (k + 1) * 128] = wout_ref[:, pl.ds(at, 128)]
    for b in range(TOK // 128):
        segc[b * 128 : (b + 1) * 128, :] = column(
            seg_ref[0:1, b * 128 : (b + 1) * 128]
        )

    step = 64
    for q in range(TOK // QB):
        lo = q * QB
        for r0 in range(lo, lo + QB, step):
            n, _ = normed(xs, r0, step)
            for k in range(NT):
                u_ref[r0 : r0 + step, k * 128 : (k + 1) * 128] = n[k].astype(BF)
        pre[lo : lo + QB, :] = dot(u_ref[lo : lo + QB, :], w[...], 1, 0)
        for r0 in range(lo, lo + QB, step):
            p = pre[r0 : r0 + step, :]
            s = 0.5 + 0.5 * jnp.tanh(0.5 * p)
            ps = p * s
            act[r0 : r0 + step, :] = ps.astype(BF)
            pre[r0 : r0 + step, :] = s + ps * (1.0 - s)

    dkv[...] = jnp.zeros((TOK, 256), F32)
    for q in range(TOK // QB):
        lo = q * QB
        k0 = max(0, lo - SEQ_MOST)
        width = lo + QB - k0
        queries = act[lo : lo + QB, 256:384]
        o = jnp.zeros((QB, HD), F32)
        for kb in range(k0, lo + QB, QB):
            sc = dot(queries, act[kb : kb + QB, 384:512], 1, 1) * (HD ** (-0.5))
            for j in range(0, QB, 128):
                same = segc[lo : lo + QB, :] == seg_ref[0:1, kb + j : kb + j + 128].astype(F32)
                if kb == lo:
                    same = same & (iota((QB, 128), 1) + j <= iota((QB, 128), 0))
                v = sc[:, j : j + 128]
                s = 0.5 + 0.5 * jnp.tanh(0.5 * v)
                vs = v * s
                at = kb - k0 + j
                aw[:, at : at + 128] = jnp.where(same, vs * (1.0 / SEQ_MOST), 0.0).astype(BF)
                dsil[:, at : at + 128] = jnp.where(
                    same, (s + vs * (1.0 - s)) * (HD ** (-0.5) / SEQ_MOST), 0.0
                )
        o = dot(aw[:, 0:width], act[k0 : lo + QB, 128:256], 1, 0)
        gate = act[lo : lo + QB, 0:128].astype(F32)
        mean = jnp.sum(o, axis=1, keepdims=True) * (1.0 / HD)
        o = o - mean
        scale = lax.rsqrt(jnp.sum(o * o, axis=1, keepdims=True) * (1.0 / HD) + 1e-05)
        n = o * scale
        y_ref[lo : lo + QB, :] = (n * gate).astype(BF)
        dy = dot(gs[0][lo : lo + QB, :], wo[:, 0:128], 1, 1)
        for k in range(1, NT):
            dy = dy + dot(gs[k][lo : lo + QB, :], wo[:, k * 128 : (k + 1) * 128], 1, 1)
        dy = dy.astype(BF).astype(F32)
        dgate = (dy * n).astype(BF).astype(F32)
        dn = dy * gate
        m1 = jnp.sum(dn, axis=1, keepdims=True) * (1.0 / HD)
        m2 = jnp.sum(dn * n, axis=1, keepdims=True) * (1.0 / HD)
        do = ((dn - m1 - n * m2) * scale).astype(BF)
        dp_ref[lo : lo + QB, 0:128] = (dgate * pre[lo : lo + QB, 0:128]).astype(BF)
        dq = jnp.zeros((QB, HD), F32)
        for kb in range(k0, lo + QB, QB):
            at = kb - k0
            da = dot(do, act[kb : kb + QB, 128:256], 1, 1).astype(BF).astype(F32)
            ds = (da * dsil[:, at : at + QB]).astype(BF)
            dq = dq + dot(ds, act[kb : kb + QB, 384:512], 1, 0)
            dkv[kb : kb + QB, 0:128] += dot(aw[:, at : at + QB], do, 0, 0)
            dkv[kb : kb + QB, 128:256] += dot(ds, queries, 0, 0)
        dq = dq.astype(BF).astype(F32)
        dp_ref[lo : lo + QB, 256:384] = (dq * pre[lo : lo + QB, 256:384]).astype(BF)

    for q in range(TOK // QB):
        lo = q * QB
        dvb = dkv[lo : lo + QB, 0:128].astype(BF).astype(F32)
        dkb = dkv[lo : lo + QB, 128:256].astype(BF).astype(F32)
        dp_ref[lo : lo + QB, 128:256] = (dvb * pre[lo : lo + QB, 128:256]).astype(BF)
        dp_ref[lo : lo + QB, 384:512] = (dkb * pre[lo : lo + QB, 384:512]).astype(BF)


def layer(pos, seg, xs, gs, w_in, w_out):
    wide = jax.ShapeDtypeStruct((TOK, D), BF)
    return pl.pallas_call(
        layer_kernel,
        out_shape=(
            wide,
            jax.ShapeDtypeStruct((TOK, 128), BF),
            wide,
            jax.ShapeDtypeStruct((D, 512), BF),
        ),
        in_specs=[SM] + [VM] * 11,
        out_specs=(VM,) * 4,
        scratch_shapes=[
            pltpu.VMEM((HD, D), BF),
            pltpu.VMEM((TOK, 512), F32),
            pltpu.VMEM((TOK, 512), BF),
            pltpu.VMEM((TOK, 128), F32),
            pltpu.VMEM((QB, 768), BF),
            pltpu.VMEM((QB, 768), F32),
            pltpu.VMEM((TOK, 256), F32),
        ],
        compiler_params=PARAMS,
        name="layer",
    )(pos, seg, *xs, *gs, w_in, w_out)


def weights_kernel(pos_ref, y_ref, u_ref, dp_ref, g0, g1, g2, g3, mine_ref, other_ref, dw_ref):
    me, core = pos_ref[0], pos_ref[1]
    gs = (g0, g1, g2, g3)
    for k in range(NT):
        at = pl.multiple_of(lax.rem(me + k, NT) * 128, 128)
        dw = dot(u_ref[:, k * 128 : (k + 1) * 128], dp_ref[...], 0, 0)
        for c in range(4):
            dw_ref[pl.ds(pl.multiple_of(c * 512 + at, 128), 128), :] = dw[:, c * 128 : (c + 1) * 128]
        dw_ref[pl.ds(pl.multiple_of(2048 + at, 128), 128), :] = dot(y_ref[...], gs[k][...], 0, 0)
    mine_ref[...] = dw_ref[pl.ds(pl.multiple_of(core * 1280, 1280), 1280), :]
    other_ref[...] = dw_ref[pl.ds(pl.multiple_of(1280 - core * 1280, 1280), 1280), :].astype(BF)


def weights(pos, y, u, dp, gs):
    return pl.pallas_call(
        weights_kernel,
        out_shape=(jax.ShapeDtypeStruct((1280, 128), F32), jax.ShapeDtypeStruct((1280, 128), BF)),
        in_specs=[SM] + [VM] * 7,
        out_specs=(VM,) * 2,
        scratch_shapes=[pltpu.VMEM((2560, 128), F32)],
        compiler_params=PARAMS,
        name="weights",
    )(pos, y, u, dp, *gs)


def input_kernel(dp_ref, w, x0, x1, x2, x3, y_ref, wout_ref, dx0, dx1, dx2, dx3, z_ref, du):
    xs, dxs = (x0, x1, x2, x3), (dx0, dx1, dx2, dx3)
    step = 64
    for k in range(NT):
        z_ref[k * TOK : (k + 1) * TOK, :] = dot(
            y_ref[...], wout_ref[:, k * 128 : (k + 1) * 128], 1, 0
        ).astype(BF)
    for q in range(TOK // QB):
        lo = q * QB
        du[...] = dot(dp_ref[lo : lo + QB, :], w[...], 1, 1).astype(BF).astype(F32)
        for r in range(0, QB, step):
            n, scale = normed(xs, lo + r, step)
            d = [du[r : r + step, k * 128 : (k + 1) * 128] for k in range(NT)]
            m1 = jnp.sum(d[0] + d[1] + d[2] + d[3], axis=1, keepdims=True) * (1.0 / D)
            m2 = jnp.sum(
                d[0] * n[0] + d[1] * n[1] + d[2] * n[2] + d[3] * n[3], axis=1, keepdims=True
            ) * (1.0 / D)
            for k in range(NT):
                dxs[k][lo + r : lo + r + step, :] = ((d[k] - m1 - n[k] * m2) * scale).astype(BF)


def input_grad(dp, w, xs, y, w_out):
    piece = jax.ShapeDtypeStruct((TOK, 128), BF)
    return pl.pallas_call(
        input_kernel,
        out_shape=(piece,) * 4 + (jax.ShapeDtypeStruct((NT * TOK, 128), BF),),
        in_specs=[VM] * 8,
        out_specs=(VM,) * 5,
        scratch_shapes=[pltpu.VMEM((QB, 512), F32)],
        compiler_params=PARAMS,
        name="input_grad",
    )(dp, w, *xs, y, w_out)


def slots_kernel(slot_ref, grad_ref, d0, d1, d2, d3, out_ref):
    dx = grad_ref[...].astype(F32) + (
        d0[...].astype(F32) + d1[...].astype(F32) + d2[...].astype(F32) + d3[...].astype(F32)
    )
    dx = dx.astype(BF)
    for s in range(SLOTS // 128):
        hot = jnp.concatenate(
            [
                (slot_ref[b : b + 1, :] == iota((128, 128), 0) + 128 * s).astype(F32).astype(BF)
                for b in range(TOK // 128)
            ],
            axis=1,
        )
        out_ref[s * 128 : (s + 1) * 128, :] = dot(hot, dx, 1, 0).astype(BF)


def to_slots(slot, grad, parts):
    return pl.pallas_call(
        slots_kernel,
        out_shape=jax.ShapeDtypeStruct((SLOTS, 128), BF),
        in_specs=[VM] * 6,
        out_specs=VM,
        compiler_params=PARAMS,
        name="to_slots",
    )(slot, grad, *parts)


def add_rows_kernel(req_ref, arrived_ref, out_ref):
    arrived = arrived_ref[...]
    for s in range(ROWS // 128):
        hot = jnp.concatenate(
            [
                (req_ref[b : b + 1, :] == iota((128, 128), 0) + 128 * s).astype(F32).astype(BF)
                for b in range(SLOTS // 128)
            ],
            axis=1,
        )
        out_ref[s * 128 : (s + 1) * 128, :] = dot(hot, arrived, 1, 0)


def add_rows(req, arrived):
    return pl.pallas_call(
        add_rows_kernel,
        out_shape=jax.ShapeDtypeStruct((ROWS, 128), F32),
        in_specs=[VM, VM],
        out_specs=VM,
        compiler_params=PARAMS,
        name="add_rows",
    )(req, arrived)


def join_kernel(y_ref, p0, p1, p2, p3, out_ref):
    for k, p in enumerate((p0, p1, p2, p3)):
        at = pl.multiple_of(lax.rem(y_ref[0] + k, 4) * 320, 320)
        out_ref[pl.ds(at, 320), :] = p[...]


def join(y, parts):
    return pl.pallas_call(
        join_kernel,
        out_shape=jax.ShapeDtypeStruct((1280, 128), BF),
        in_specs=[SM] + [VM] * 4,
        out_specs=VM,
        compiler_params=PARAMS,
        name="join",
    )(y, *parts)


def unpack_kernel(whole_ref, in_ref, out_ref):
    for c in range(4):
        in_ref[c, :, :] = whole_ref[c * 512 : (c + 1) * 512, :].astype(F32)
    for k in range(NT):
        out_ref[:, k * 128 : (k + 1) * 128] = whole_ref[2048 + k * 128 : 2176 + k * 128, :].astype(F32)


def unpack(whole):
    return pl.pallas_call(
        unpack_kernel,
        out_shape=(jax.ShapeDtypeStruct((4, D, 128), F32), jax.ShapeDtypeStruct((HD, D), F32)),
        in_specs=[VM],
        out_specs=(VM, VM),
        compiler_params=PARAMS,
        name="unpack",
    )(whole)


def shift(x, axis, fn, n):
    return lax.ppermute(x, axis, [(i, fn(i)) for i in range(n)])


def gather_pieces(x):
    return [x] + [shift(x, "tensor", lambda i, k=k: (i - k) % NT, NT) for k in (1, 3, 2)]


def order(pieces):
    own, one, three, two = pieces
    return [own, one, two, three]


def scatter_pieces(parts):
    return [parts[0]] + [shift(parts[k], "tensor", lambda i, k=k: (i + k) % NT, NT) for k in (1, 3, 2)]


def pick(x, i):
    return lax.dynamic_index_in_dim(x, i, 0, keepdims=False)


def reduce_weights(mine, other, arrived):
    at = lax.axis_index("table")
    core, y = at % 2, at // 2
    other = shift(other, "table", lambda i: i ^ 1, 8)
    mine = (mine + other.astype(F32)).reshape(4, 320, 128)
    total = pick(mine, y)
    got = [
        shift(pick(mine, (y + k) % 4).astype(BF), "table", lambda i, k=k: (i + 2 * k) % 8, 8)
        for k in range(1, 4)
    ]
    for v in got:
        total = total + v.astype(F32)
    for bit in (1, 2, 4):
        total = total.astype(BF)
        total = total.astype(F32) + shift(total, "seq", lambda i, b=bit: i ^ b, 8).astype(F32)
    total, arrived = lax.optimization_barrier((total.astype(BF), arrived))
    parts = [total] + [
        shift(total, "table", lambda i, k=k: (i - 2 * k) % 8, 8) for k in range(1, 4)
    ]
    whole = lax.all_gather(
        join(y.astype(I32).reshape(1), parts),
        "table",
        axis=0,
        tiled=True,
        axis_index_groups=[[2 * i, 2 * i + 1] for i in range(4)],
    )
    return unpack(whole), arrived


def body(table, owner, local_row, segment_ids, proj_in, proj_out, grad_out):
    pos = jnp.stack([lax.axis_index("tensor"), lax.axis_index("table") % 2]).astype(I32)
    requests, slot = route(owner.reshape(8, 128), local_row.reshape(8, 128))
    gs = order(gather_pieces(grad_out))
    received = lax.all_to_all(requests, BOTH, split_axis=0, concat_axis=0, tiled=True)
    rows = fetch(received, table)
    back = lax.all_to_all(rows.reshape(NOWN, CAP, 128), BOTH, split_axis=0, concat_axis=0, tiled=True)
    x = place(slot, back.reshape(SLOTS, 128))
    xs = order(gather_pieces(x))
    u, y, dp, w = layer(pos, segment_ids, xs, gs, proj_in, proj_out)
    mine, other = weights(pos, y, u, dp, gs)
    dp, mine, other = lax.optimization_barrier((dp, mine, other))
    d0, d1, d2, d3, z = input_grad(dp, w, xs, y, proj_out)
    dparts = scatter_pieces([d0, d1, d2, d3])
    grads = to_slots(slot, grad_out, dparts)
    grads, z = lax.optimization_barrier((grads, z))
    arrived = lax.all_to_all(grads.reshape(NOWN, CAP, 128), BOTH, split_axis=0, concat_axis=0, tiled=True)
    zsum = lax.psum_scatter(z, "tensor", scatter_dimension=0, tiled=True)
    layer_out = (x.astype(F32) + zsum.astype(F32)).astype(BF)
    flat = received[:, :CAP].reshape(SLOTS // 128, 128)
    (grad_in, grad_outw), arrived = reduce_weights(mine, other, arrived)
    table_grad = add_rows(flat, arrived.reshape(SLOTS, 128))
    return layer_out, table_grad, grad_in, grad_outw


def solution(mesh):
    in_specs = (
        P(BOTH, "tensor"),
        P(BOTH, None),
        P(BOTH),
        P(BOTH, None),
        P(None, None, "tensor"),
        P("tensor", None),
        P(BOTH, "tensor"),
    )
    out_specs = (
        P(BOTH, "tensor"),
        P(BOTH, "tensor"),
        P(None, None, "tensor"),
        P("tensor", None),
    )
    return jax.shard_map(body, mesh=mesh, in_specs=in_specs, out_specs=out_specs, check_vma=False)
```

```python
import functools

import jax
import jax.numpy as jnp
from jax import lax
from jax.experimental import pallas as pl
from jax.experimental.pallas import tpu as pltpu
from jax.sharding import PartitionSpec as P

HD = 128
SEQ_MOST = 512
TOK = 1024
D = 512
NT = 4
NOWN = 64
CAP = 24
SLOTS = NOWN * CAP
ROWS = 2048
QB = 256
BOTH = ("table", "seq")
BF = jnp.bfloat16
F32 = jnp.float32
I32 = jnp.int32
VM = pl.BlockSpec(memory_space=pltpu.VMEM)
SM = pl.BlockSpec(memory_space=pltpu.SMEM)
PARAMS = pltpu.CompilerParams(vmem_limit_bytes=56 * 1024 * 1024)


def iota(shape, dim):
    return lax.broadcasted_iota(I32, shape, dim)


def dot(a, b, ca, cb):
    return lax.dot_general(a, b, (((ca,), (cb,)), ((), ())), preferred_element_type=F32)


def route_kernel(owner_ref, row_ref, req_ref, slot_ref):
    upper = (iota((128, 128), 0) < iota((128, 128), 1)).astype(BF)
    ones = jnp.ones((128, 128), BF)
    scan = jnp.concatenate([upper, ones], axis=1)
    carry = jnp.zeros((NOWN, 128), F32)
    high = jnp.zeros((NOWN, 128), F32)
    low = jnp.zeros((NOWN, 128), F32)
    for b in range(TOK // 128):
        own = owner_ref[b : b + 1, :]
        row = row_ref[b : b + 1, :]
        hot = iota((NOWN, 128), 0) == own
        hot_f = hot.astype(F32)
        hot_b = hot_f.astype(BF)
        sums = dot(hot_b, scan, 1, 0)
        rank = jnp.sum(hot_f * (sums[:, :128] + carry), axis=0, keepdims=True)
        carry = carry + sums[:, 128:]
        rank_i = rank.astype(I32)
        slot_ref[b : b + 1, :] = own * CAP + rank_i
        place = iota((128, 128), 0) == rank_i
        row_hi = jnp.where(place, (row >> 6).astype(F32), 0.0).astype(BF)
        row_lo = jnp.where(place, (row & 63).astype(F32), 0.0).astype(BF)
        high = high + dot(hot_b, row_hi, 1, 1)
        low = low + dot(hot_b, row_lo, 1, 1)
    req_ref[...] = high.astype(I32) * 64 + low.astype(I32)


def route(owner, row):
    return pl.pallas_call(
        route_kernel,
        out_shape=(
            jax.ShapeDtypeStruct((NOWN, 128), I32),
            jax.ShapeDtypeStruct((TOK // 128, 128), I32),
        ),
        in_specs=[VM, VM],
        out_specs=(VM, VM),
        compiler_params=PARAMS,
        name="route",
    )(owner, row)


def hot_where(high, value, low_hot):
    return jnp.where(high == value, low_hot, jnp.zeros_like(low_hot))


def fetch_kernel(req_ref, table_ref, out_ref, got):
    half = ROWS // 2
    both = jnp.concatenate([table_ref[:half, :], table_ref[half:, :]], axis=1)
    for c0 in range(0, CAP, 4):
        hots, uppers = [], []
        for c in range(c0, c0 + 4):
            row = jnp.broadcast_to(req_ref[:, c : c + 1], (NOWN, 128))
            low = ((row & 127) == iota((NOWN, 128), 1)).astype(F32).astype(BF)
            high = ((row >> 7) & 7).astype(F32).astype(BF)
            hots.append(jnp.concatenate([hot_where(high, j, low) for j in range(8)], axis=1))
            uppers.append(row >= half)
        pair = dot(jnp.concatenate(hots, axis=0), both, 1, 0)
        rows = jnp.where(jnp.concatenate(uppers, axis=0), pair[:, 128:], pair[:, :128])
        for i in range(4):
            got[pl.ds(c0 + i, NOWN, stride=CAP), :] = rows[i * NOWN : (i + 1) * NOWN, :]
    out_ref[...] = got[...].astype(BF)


def fetch(req, table):
    return pl.pallas_call(
        fetch_kernel,
        out_shape=jax.ShapeDtypeStruct((SLOTS, 128), BF),
        in_specs=[VM, VM],
        out_specs=VM,
        scratch_shapes=[pltpu.VMEM((SLOTS, 128), F32)],
        compiler_params=PARAMS,
        name="fetch",
    )(req, table)


def column(row_vector):
    wide = jnp.broadcast_to(row_vector.astype(F32), (128, 128))
    return jnp.transpose(wide)


def place_kernel(slot_ref, back_ref, x_ref):
    half = SLOTS // 2
    both = jnp.concatenate([back_ref[:half, :], back_ref[half:, :]], axis=1)
    for b0 in range(0, TOK // 128, 2):
        hots, uppers = [], []
        for b in (b0, b0 + 1):
            slot = column(slot_ref[b : b + 1, :]).astype(I32)
            upper = slot >= half
            slot = jnp.where(upper, slot - half, slot)
            low = ((slot & 127) == iota((128, 128), 1)).astype(F32).astype(BF)
            high = (slot >> 7).astype(F32).astype(BF)
            hots.append(jnp.concatenate([hot_where(high, j, low) for j in range(half // 128)], axis=1))
            uppers.append(upper)
        pair = dot(jnp.concatenate(hots, axis=0), both, 1, 0)
        rows = jnp.where(jnp.concatenate(uppers, axis=0), pair[:, 128:], pair[:, :128])
        x_ref[b0 * 128 : b0 * 128 + 256, :] = rows.astype(BF)


def place(slot, back):
    return pl.pallas_call(
        place_kernel,
        out_shape=jax.ShapeDtypeStruct((TOK, 128), BF),
        in_specs=[VM, VM],
        out_specs=VM,
        compiler_params=PARAMS,
        name="place",
    )(slot, back)


def layer_kernel(
    pos_ref, seg_ref, x0, x1, x2, x3, g0, g1, g2, g3, win_ref, wout_ref,
    dx0, dx1, dx2, dx3, u_ref, y_ref, dp_ref,
    w, wo, pre, act, segc, aw, dsil, dout, dkv, du,
):
    xs, gs, dxs = (x0, x1, x2, x3), (g0, g1, g2, g3), (dx0, dx1, dx2, dx3)
    me = pos_ref[0]
    for k in range(NT):
        at = pl.multiple_of(lax.rem(me + k, NT) * 128, 128)
        for c in range(4):
            w[k * 128 : (k + 1) * 128, c * 128 : (c + 1) * 128] = win_ref[c, pl.ds(at, 128), :]
        wo[:, k * 128 : (k + 1) * 128] = wout_ref[:, pl.ds(at, 128)]
    for b in range(TOK // 128):
        segc[b * 128 : (b + 1) * 128, :] = column(
            seg_ref[0:1, b * 128 : (b + 1) * 128]
        )

    def stats(r0, n):
        x = [r[r0 : r0 + n, :].astype(F32) for r in xs]
        mean = jnp.sum(x[0] + x[1] + x[2] + x[3], axis=1, keepdims=True) * (1.0 / D)
        x = [v - mean for v in x]
        var = jnp.sum(x[0] * x[0] + x[1] * x[1] + x[2] * x[2] + x[3] * x[3], axis=1, keepdims=True)
        scale = lax.rsqrt(var * (1.0 / D) + 1e-05)
        return [v * scale for v in x], scale

    step = 64
    for q in range(TOK // QB):
        lo = q * QB
        for r0 in range(lo, lo + QB, step):
            n, _ = stats(r0, step)
            for k in range(NT):
                u_ref[r0 : r0 + step, k * 128 : (k + 1) * 128] = n[k].astype(BF)
        pre[lo : lo + QB, :] = dot(u_ref[lo : lo + QB, :], w[...], 1, 0)
        for r0 in range(lo, lo + QB, step):
            p = pre[r0 : r0 + step, :]
            s = 0.5 + 0.5 * jnp.tanh(0.5 * p)
            ps = p * s
            act[r0 : r0 + step, :] = ps.astype(BF)
            pre[r0 : r0 + step, :] = s + ps * (1.0 - s)

    dkv[...] = jnp.zeros((TOK, 256), F32)
    for q in range(TOK // QB):
        lo = q * QB
        k0 = max(0, lo - SEQ_MOST)
        width = lo + QB - k0
        queries = act[lo : lo + QB, 256:384]
        o = jnp.zeros((QB, HD), F32)
        for kb in range(k0, lo + QB, QB):
            sc = dot(queries, act[kb : kb + QB, 384:512], 1, 1) * (HD ** (-0.5))
            for j in range(0, QB, 128):
                same = segc[lo : lo + QB, :] == seg_ref[0:1, kb + j : kb + j + 128].astype(F32)
                if kb == lo:
                    same = same & (iota((QB, 128), 1) + j <= iota((QB, 128), 0))
                v = sc[:, j : j + 128]
                s = 0.5 + 0.5 * jnp.tanh(0.5 * v)
                vs = v * s
                at = kb - k0 + j
                aw[:, at : at + 128] = jnp.where(same, vs * (1.0 / SEQ_MOST), 0.0).astype(BF)
                dsil[:, at : at + 128] = jnp.where(
                    same, (s + vs * (1.0 - s)) * (HD ** (-0.5) / SEQ_MOST), 0.0
                )
        o = dot(aw[:, 0:width], act[k0 : lo + QB, 128:256], 1, 0)
        gate = act[lo : lo + QB, 0:128].astype(F32)
        mean = jnp.sum(o, axis=1, keepdims=True) * (1.0 / HD)
        o = o - mean
        scale = lax.rsqrt(jnp.sum(o * o, axis=1, keepdims=True) * (1.0 / HD) + 1e-05)
        n = o * scale
        y_ref[lo : lo + QB, :] = (n * gate).astype(BF)
        dy = dot(gs[0][lo : lo + QB, :], wo[:, 0:128], 1, 1)
        for k in range(1, NT):
            dy = dy + dot(gs[k][lo : lo + QB, :], wo[:, k * 128 : (k + 1) * 128], 1, 1)
        dy = dy.astype(BF).astype(F32)
        dgate = (dy * n).astype(BF).astype(F32)
        dn = dy * gate
        m1 = jnp.sum(dn, axis=1, keepdims=True) * (1.0 / HD)
        m2 = jnp.sum(dn * n, axis=1, keepdims=True) * (1.0 / HD)
        do = ((dn - m1 - n * m2) * scale).astype(BF)
        dp_ref[lo : lo + QB, 0:128] = (dgate * pre[lo : lo + QB, 0:128]).astype(BF)
        dq = jnp.zeros((QB, HD), F32)
        for kb in range(k0, lo + QB, QB):
            at = kb - k0
            da = dot(do, act[kb : kb + QB, 128:256], 1, 1).astype(BF).astype(F32)
            ds = (da * dsil[:, at : at + QB]).astype(BF)
            dq = dq + dot(ds, act[kb : kb + QB, 384:512], 1, 0)
            dkv[kb : kb + QB, 0:128] += dot(aw[:, at : at + QB], do, 0, 0)
            dkv[kb : kb + QB, 128:256] += dot(ds, queries, 0, 0)
        dq = dq.astype(BF).astype(F32)
        dp_ref[lo : lo + QB, 256:384] = (dq * pre[lo : lo + QB, 256:384]).astype(BF)

    for q in range(TOK // QB):
        lo = q * QB
        dvb = dkv[lo : lo + QB, 0:128].astype(BF).astype(F32)
        dkb = dkv[lo : lo + QB, 128:256].astype(BF).astype(F32)
        dp_ref[lo : lo + QB, 128:256] = (dvb * pre[lo : lo + QB, 128:256]).astype(BF)
        dp_ref[lo : lo + QB, 384:512] = (dkb * pre[lo : lo + QB, 384:512]).astype(BF)
        du[...] = dot(dp_ref[lo : lo + QB, :], w[...], 1, 1).astype(BF).astype(F32)
        for r in range(0, QB, step):
            n, scale = stats(lo + r, step)
            d = [du[r : r + step, k * 128 : (k + 1) * 128] for k in range(NT)]
            m1 = jnp.sum(d[0] + d[1] + d[2] + d[3], axis=1, keepdims=True) * (1.0 / D)
            m2 = jnp.sum(
                d[0] * n[0] + d[1] * n[1] + d[2] * n[2] + d[3] * n[3], axis=1, keepdims=True
            ) * (1.0 / D)
            for k in range(NT):
                dxs[k][lo + r : lo + r + step, :] = ((d[k] - m1 - n[k] * m2) * scale).astype(BF)


def layer(pos, seg, xs, gs, w_in, w_out):
    piece = jax.ShapeDtypeStruct((TOK, 128), BF)
    wide = jax.ShapeDtypeStruct((TOK, D), BF)
    return pl.pallas_call(
        layer_kernel,
        out_shape=(piece,) * 4 + (wide, piece, wide),
        in_specs=[SM] + [VM] * 11,
        out_specs=(VM,) * 7,
        scratch_shapes=[
            pltpu.VMEM((D, 512), BF),
            pltpu.VMEM((HD, D), BF),
            pltpu.VMEM((TOK, 512), F32),
            pltpu.VMEM((TOK, 512), BF),
            pltpu.VMEM((TOK, 128), F32),
            pltpu.VMEM((QB, 768), BF),
            pltpu.VMEM((QB, 768), F32),
            pltpu.VMEM((QB, 128), BF),
            pltpu.VMEM((TOK, 256), F32),
            pltpu.VMEM((QB, 512), F32),
        ],
        compiler_params=PARAMS,
        name="layer",
    )(pos, seg, *xs, *gs, w_in, w_out)


def proj_kernel(
    pos_ref, y_ref, u_ref, dp_ref, g0, g1, g2, g3, wout_ref, mine_ref, other_ref, z0, z1, z2, z3, dw_ref
):
    me, core = pos_ref[0], pos_ref[1]
    gs, zs = (g0, g1, g2, g3), (z0, z1, z2, z3)
    for k in range(NT):
        at = pl.multiple_of(lax.rem(me + k, NT) * 128, 128)
        dw = dot(u_ref[:, k * 128 : (k + 1) * 128], dp_ref[...], 0, 0)
        for c in range(4):
            dw_ref[pl.ds(pl.multiple_of(c * 512 + at, 128), 128), :] = dw[:, c * 128 : (c + 1) * 128]
        dw_ref[pl.ds(pl.multiple_of(2048 + at, 128), 128), :] = dot(y_ref[...], gs[k][...], 0, 0)
        zs[k][...] = dot(y_ref[...], wout_ref[:, pl.ds(at, 128)], 1, 0).astype(BF)
    mine_ref[...] = dw_ref[pl.ds(pl.multiple_of(core * 1280, 1280), 1280), :]
    other_ref[...] = dw_ref[pl.ds(pl.multiple_of(1280 - core * 1280, 1280), 1280), :].astype(BF)


def project(pos, y, u, dp, gs, w_out):
    piece = jax.ShapeDtypeStruct((TOK, 128), BF)
    return pl.pallas_call(
        proj_kernel,
        out_shape=(jax.ShapeDtypeStruct((1280, 128), F32), jax.ShapeDtypeStruct((1280, 128), BF))
        + (piece,) * 4,
        in_specs=[SM] + [VM] * 8,
        out_specs=(VM,) * 6,
        scratch_shapes=[pltpu.VMEM((2560, 128), F32)],
        compiler_params=PARAMS,
        name="project",
    )(pos, y, u, dp, *gs, w_out)


def spread(at_ref, blocks, size, values):
    lows, highs, pairs = [], [], []
    for b in range(blocks):
        at = at_ref[b : b + 1, :]
        upper = column((at >= size).astype(F32)) > 0.5
        value = values[b * 128 : (b + 1) * 128, :]
        pairs.append(
            jnp.concatenate([jnp.where(upper, 0.0, value), jnp.where(upper, value, 0.0)], axis=1).astype(BF)
        )
        at = jnp.broadcast_to(jnp.where(at >= size, at - size, at), (128, 128))
        lows.append(((at & 127) == iota((128, 128), 0)).astype(F32).astype(BF))
        highs.append((at >> 7).astype(F32).astype(BF))
    low = jnp.concatenate(lows, axis=1)
    high = jnp.concatenate(highs, axis=1)
    pair = jnp.concatenate(pairs, axis=0)
    return [dot(hot_where(high, s, low), pair, 1, 0) for s in range(size // 128)]


def slots_kernel(slot_ref, grad_ref, d0, d1, d2, d3, out_ref):
    dx = grad_ref[...].astype(F32) + (
        d0[...].astype(F32) + d1[...].astype(F32) + d2[...].astype(F32) + d3[...].astype(F32)
    )
    half = SLOTS // 2
    for s, both in enumerate(spread(slot_ref, TOK // 128, half, dx)):
        out_ref[s * 128 : (s + 1) * 128, :] = both[:, :128].astype(BF)
        out_ref[half + s * 128 : half + (s + 1) * 128, :] = both[:, 128:].astype(BF)


def to_slots(slot, grad, parts):
    return pl.pallas_call(
        slots_kernel,
        out_shape=jax.ShapeDtypeStruct((SLOTS, 128), BF),
        in_specs=[VM] * 6,
        out_specs=VM,
        compiler_params=PARAMS,
        name="to_slots",
    )(slot, grad, *parts)


def add_rows_kernel(req_ref, arrived_ref, out_ref):
    half = ROWS // 2
    for s, both in enumerate(spread(req_ref, SLOTS // 128, half, arrived_ref[...].astype(F32))):
        out_ref[s * 128 : (s + 1) * 128, :] = both[:, :128]
        out_ref[half + s * 128 : half + (s + 1) * 128, :] = both[:, 128:]


def add_rows(req, arrived):
    return pl.pallas_call(
        add_rows_kernel,
        out_shape=jax.ShapeDtypeStruct((ROWS, 128), F32),
        in_specs=[VM, VM],
        out_specs=VM,
        compiler_params=PARAMS,
        name="add_rows",
    )(req, arrived)


def join_kernel(y_ref, p0, p1, p2, p3, out_ref):
    for k, p in enumerate((p0, p1, p2, p3)):
        at = pl.multiple_of(lax.rem(y_ref[0] + k, 4) * 320, 320)
        out_ref[pl.ds(at, 320), :] = p[...]


def join(y, parts):
    return pl.pallas_call(
        join_kernel,
        out_shape=jax.ShapeDtypeStruct((1280, 128), BF),
        in_specs=[SM] + [VM] * 4,
        out_specs=VM,
        compiler_params=PARAMS,
        name="join",
    )(y, *parts)


def unpack_kernel(whole_ref, in_ref, out_ref):
    for c in range(4):
        in_ref[c, :, :] = whole_ref[c * 512 : (c + 1) * 512, :].astype(F32)
    for k in range(NT):
        out_ref[:, k * 128 : (k + 1) * 128] = whole_ref[2048 + k * 128 : 2176 + k * 128, :].astype(F32)


def unpack(whole):
    return pl.pallas_call(
        unpack_kernel,
        out_shape=(jax.ShapeDtypeStruct((4, D, 128), F32), jax.ShapeDtypeStruct((HD, D), F32)),
        in_specs=[VM],
        out_specs=(VM, VM),
        compiler_params=PARAMS,
        name="unpack",
    )(whole)


def shift(x, axis, fn, n):
    return lax.ppermute(x, axis, [(i, fn(i)) for i in range(n)])


def gather_pieces(x):
    return [x] + [shift(x, "tensor", lambda i, k=k: (i - k) % NT, NT) for k in (1, 3, 2)]


def order(pieces):
    own, one, three, two = pieces
    return [own, one, two, three]


def scatter_pieces(parts):
    return [parts[0]] + [shift(parts[k], "tensor", lambda i, k=k: (i + k) % NT, NT) for k in (1, 3, 2)]


def pick(x, i):
    return lax.dynamic_index_in_dim(x, i, 0, keepdims=False)


def reduce_weights(mine, other, grads):
    at = lax.axis_index("table")
    core, y = at % 2, at // 2
    other = shift(other, "table", lambda i: i ^ 1, 8)
    mine = (mine + other.astype(F32)).reshape(4, 320, 128)
    total = pick(mine, y)
    got = [
        shift(pick(mine, (y + k) % 4).astype(BF), "table", lambda i, k=k: (i + 2 * k) % 8, 8)
        for k in range(1, 4)
    ]
    for v in got:
        total = total + v.astype(F32)
    total, grads = lax.optimization_barrier((total.astype(BF), grads))
    for bit in (1, 2, 4):
        total = total.astype(F32) + shift(total, "seq", lambda i, b=bit: i ^ b, 8).astype(F32)
        total = total.astype(BF)
    return total, grads


def gather_weights(total):
    y = lax.axis_index("table") // 2
    parts = [total] + [
        shift(total, "table", lambda i, k=k: (i - 2 * k) % 8, 8) for k in range(1, 4)
    ]
    whole = lax.all_gather(
        join(y.astype(I32).reshape(1), parts),
        "table",
        axis=0,
        tiled=True,
        axis_index_groups=[[2 * i, 2 * i + 1] for i in range(4)],
    )
    return unpack(whole)


def body(table, owner, local_row, segment_ids, proj_in, proj_out, grad_out):
    pos = jnp.stack([lax.axis_index("tensor"), lax.axis_index("table") % 2]).astype(I32)
    requests, slot = route(owner.reshape(8, 128), local_row.reshape(8, 128))
    requests, pos = lax.optimization_barrier((requests, pos))
    gs = order(gather_pieces(grad_out))
    received = lax.all_to_all(requests, BOTH, split_axis=0, concat_axis=0, tiled=True)
    rows = fetch(received, table)
    back = lax.all_to_all(rows.reshape(NOWN, CAP, 128), BOTH, split_axis=0, concat_axis=0, tiled=True)
    x = place(slot, back.reshape(SLOTS, 128))
    xs = order(gather_pieces(x))
    d0, d1, d2, d3, u, y, dp = layer(pos, segment_ids, xs, gs, proj_in, proj_out)
    dparts = scatter_pieces([d0, d1, d2, d3])
    mine, other, z0, z1, z2, z3 = project(pos, y, u, dp, gs, proj_out)
    grads = to_slots(slot, grad_out, dparts)
    total, grads = reduce_weights(mine, other, grads)
    arrived = lax.all_to_all(grads.reshape(NOWN, CAP, 128), BOTH, split_axis=0, concat_axis=0, tiled=True)
    zparts = scatter_pieces([z0, z1, z2, z3])
    layer_out = (
        x.astype(F32)
        + (zparts[0].astype(F32) + zparts[1].astype(F32) + zparts[2].astype(F32) + zparts[3].astype(F32))
    ).astype(BF)
    flat = received[:, :CAP].reshape(SLOTS // 128, 128)
    total, arrived, layer_out = lax.optimization_barrier((total, arrived, layer_out))
    table_grad = add_rows(flat, arrived.reshape(SLOTS, 128))
    grad_in, grad_outw = gather_weights(total)
    return layer_out, table_grad, grad_in, grad_outw


def solution(mesh):
    in_specs = (
        P(BOTH, "tensor"),
        P(BOTH, None),
        P(BOTH),
        P(BOTH, None),
        P(None, None, "tensor"),
        P("tensor", None),
        P(BOTH, "tensor"),
    )
    out_specs = (
        P(BOTH, "tensor"),
        P(BOTH, "tensor"),
        P(None, None, "tensor"),
        P("tensor", None),
    )
    return jax.shard_map(body, mesh=mesh, in_specs=in_specs, out_specs=out_specs, check_vma=False)
```

```python
import functools

import jax
import jax.numpy as jnp
from jax import lax
from jax.experimental import pallas as pl
from jax.experimental.pallas import tpu as pltpu
from jax.sharding import PartitionSpec as P

HD = 128
SEQ_MOST = 512
TOK = 1024
D = 512
NT = 4
NOWN = 64
CAP = 24
SLOTS = NOWN * CAP
ROWS = 2048
QB = 256
BOTH = ("table", "seq")
BF = jnp.bfloat16
F32 = jnp.float32
I32 = jnp.int32
VM = pl.BlockSpec(memory_space=pltpu.VMEM)
SM = pl.BlockSpec(memory_space=pltpu.SMEM)
PARAMS = pltpu.CompilerParams(vmem_limit_bytes=56 * 1024 * 1024)


def iota(shape, dim):
    return lax.broadcasted_iota(I32, shape, dim)


def dot(a, b, ca, cb):
    return lax.dot_general(a, b, (((ca,), (cb,)), ((), ())), preferred_element_type=F32)


def route_kernel(owner_ref, row_ref, req_ref, slot_ref):
    blocks = TOK // 128
    upper = (iota((128, 128), 0) < iota((128, 128), 1)).astype(BF)
    scan = jnp.concatenate([upper, jnp.ones((128, 128), BF)], axis=1)
    hots = [(iota((NOWN, 128), 0) == owner_ref[b : b + 1, :]).astype(F32) for b in range(blocks)]
    sums = dot(jnp.concatenate(hots, axis=0).astype(BF), scan, 1, 0)
    carry = jnp.zeros((NOWN, 128), F32)
    highs, lows = [], []
    for b in range(blocks):
        part = sums[b * NOWN : (b + 1) * NOWN, :]
        rank = jnp.sum(hots[b] * (part[:, :128] + carry), axis=0, keepdims=True).astype(I32)
        carry = carry + part[:, 128:]
        row = row_ref[b : b + 1, :]
        slot_ref[b : b + 1, :] = owner_ref[b : b + 1, :] * CAP + rank
        here = iota((32, 128), 0) == rank
        highs.append(jnp.where(here, (row >> 6).astype(F32), 0.0))
        lows.append(jnp.where(here, (row & 63).astype(F32), 0.0))
    hot = jnp.concatenate(hots, axis=1).astype(BF)
    high = dot(hot, jnp.concatenate(highs, axis=1).astype(BF), 1, 1)
    low = dot(hot, jnp.concatenate(lows, axis=1).astype(BF), 1, 1)
    req_ref[...] = jnp.zeros((NOWN, 128), I32)
    req_ref[:, 0:32] = (high * 64.0 + low).astype(I32)


def route(owner, row):
    return pl.pallas_call(
        route_kernel,
        out_shape=(
            jax.ShapeDtypeStruct((NOWN, 128), I32),
            jax.ShapeDtypeStruct((TOK // 128, 128), I32),
        ),
        in_specs=[VM, VM],
        out_specs=(VM, VM),
        compiler_params=PARAMS,
        name="route",
    )(owner, row)


def hot_where(high, value, low_hot):
    return jnp.where(high == value, low_hot, jnp.zeros_like(low_hot))


def fetch_kernel(req_ref, table_ref, out_ref, got):
    half = ROWS // 2
    both = jnp.concatenate([table_ref[:half, :], table_ref[half:, :]], axis=1)
    for c0 in range(0, CAP, 4):
        hots, uppers = [], []
        for c in range(c0, c0 + 4):
            row = jnp.broadcast_to(req_ref[:, c : c + 1], (NOWN, 128))
            low = ((row & 127) == iota((NOWN, 128), 1)).astype(F32).astype(BF)
            high = ((row >> 7) & 7).astype(F32).astype(BF)
            hots.append(jnp.concatenate([hot_where(high, j, low) for j in range(8)], axis=1))
            uppers.append(row >= half)
        pair = dot(jnp.concatenate(hots, axis=0), both, 1, 0)
        rows = jnp.where(jnp.concatenate(uppers, axis=0), pair[:, 128:], pair[:, :128])
        for i in range(4):
            got[pl.ds(c0 + i, NOWN, stride=CAP), :] = rows[i * NOWN : (i + 1) * NOWN, :]
    out_ref[...] = got[...].astype(BF)


def fetch(req, table):
    return pl.pallas_call(
        fetch_kernel,
        out_shape=jax.ShapeDtypeStruct((SLOTS, 128), BF),
        in_specs=[VM, VM],
        out_specs=VM,
        scratch_shapes=[pltpu.VMEM((SLOTS, 128), F32)],
        compiler_params=PARAMS,
        name="fetch",
    )(req, table)


def column(row_vector):
    wide = jnp.broadcast_to(row_vector.astype(F32), (128, 128))
    return jnp.transpose(wide)


def place_kernel(slot_ref, back_ref, x_ref):
    half = SLOTS // 2
    both = jnp.concatenate([back_ref[:half, :], back_ref[half:, :]], axis=1)
    for b0 in range(0, TOK // 128, 2):
        hots, uppers = [], []
        for b in (b0, b0 + 1):
            slot = column(slot_ref[b : b + 1, :]).astype(I32)
            upper = slot >= half
            slot = jnp.where(upper, slot - half, slot)
            low = ((slot & 127) == iota((128, 128), 1)).astype(F32).astype(BF)
            high = (slot >> 7).astype(F32).astype(BF)
            hots.append(jnp.concatenate([hot_where(high, j, low) for j in range(half // 128)], axis=1))
            uppers.append(upper)
        pair = dot(jnp.concatenate(hots, axis=0), both, 1, 0)
        rows = jnp.where(jnp.concatenate(uppers, axis=0), pair[:, 128:], pair[:, :128])
        x_ref[b0 * 128 : b0 * 128 + 256, :] = rows.astype(BF)


def place(slot, back):
    return pl.pallas_call(
        place_kernel,
        out_shape=jax.ShapeDtypeStruct((TOK, 128), BF),
        in_specs=[VM, VM],
        out_specs=VM,
        compiler_params=PARAMS,
        name="place",
    )(slot, back)


def layer_kernel(
    pos_ref, core_ref, seg_ref, x0, x1, x2, x3, g0, g1, g2, g3, win_ref, wout_ref,
    mine_ref, other_ref, dx0, dx1, dx2, dx3, z0, z1, z2, z3,
    w, wo, pre, act, segc, aw, dsil, dkv, du, u_ref, y_ref, dp_ref, dw_ref,
):
    xs, gs = (x0, x1, x2, x3), (g0, g1, g2, g3)
    dxs, zs = (dx0, dx1, dx2, dx3), (z0, z1, z2, z3)
    me, core = pos_ref[0], core_ref[0]
    for k in range(NT):
        at = pl.multiple_of(lax.rem(me + k, NT) * 128, 128)
        for c in range(4):
            w[k * 128 : (k + 1) * 128, c * 128 : (c + 1) * 128] = win_ref[c, pl.ds(at, 128), :]
        wo[:, k * 128 : (k + 1) * 128] = wout_ref[:, pl.ds(at, 128)]
    for b in range(TOK // 128):
        segc[b * 128 : (b + 1) * 128, :] = column(
            seg_ref[0:1, b * 128 : (b + 1) * 128]
        )

    def stats(r0, n):
        x = [r[r0 : r0 + n, :].astype(F32) for r in xs]
        mean = jnp.sum(x[0] + x[1] + x[2] + x[3], axis=1, keepdims=True) * (1.0 / D)
        x = [v - mean for v in x]
        var = jnp.sum(x[0] * x[0] + x[1] * x[1] + x[2] * x[2] + x[3] * x[3], axis=1, keepdims=True)
        scale = lax.rsqrt(var * (1.0 / D) + 1e-05)
        return [v * scale for v in x], scale

    step = 64
    for q in range(TOK // QB):
        lo = q * QB
        for r0 in range(lo, lo + QB, step):
            n, _ = stats(r0, step)
            for k in range(NT):
                u_ref[r0 : r0 + step, k * 128 : (k + 1) * 128] = n[k].astype(BF)
        pre[lo : lo + QB, :] = dot(u_ref[lo : lo + QB, :], w[...], 1, 0)
        for r0 in range(lo, lo + QB, step):
            p = pre[r0 : r0 + step, :]
            s = 0.5 + 0.5 * jnp.tanh(0.5 * p)
            ps = p * s
            act[r0 : r0 + step, :] = ps.astype(BF)
            pre[r0 : r0 + step, :] = s + ps * (1.0 - s)

    dkv[...] = jnp.zeros((TOK, 256), F32)
    for q in range(TOK // QB):
        lo = q * QB
        k0 = max(0, lo - SEQ_MOST)
        width = lo + QB - k0
        queries = act[lo : lo + QB, 256:384]
        o = jnp.zeros((QB, HD), F32)
        for kb in range(k0, lo + QB, QB):
            sc = dot(queries, act[kb : kb + QB, 384:512], 1, 1) * (HD ** (-0.5))
            for j in range(0, QB, 128):
                same = segc[lo : lo + QB, :] == seg_ref[0:1, kb + j : kb + j + 128].astype(F32)
                if kb == lo:
                    same = same & (iota((QB, 128), 1) + j <= iota((QB, 128), 0))
                v = sc[:, j : j + 128]
                s = 0.5 + 0.5 * jnp.tanh(0.5 * v)
                vs = v * s
                at = kb - k0 + j
                aw[:, at : at + 128] = jnp.where(same, vs * (1.0 / SEQ_MOST), 0.0).astype(BF)
                dsil[:, at : at + 128] = jnp.where(
                    same, (s + vs * (1.0 - s)) * (HD ** (-0.5) / SEQ_MOST), 0.0
                )
        o = dot(aw[:, 0:width], act[k0 : lo + QB, 128:256], 1, 0)
        gate = act[lo : lo + QB, 0:128].astype(F32)
        mean = jnp.sum(o, axis=1, keepdims=True) * (1.0 / HD)
        o = o - mean
        scale = lax.rsqrt(jnp.sum(o * o, axis=1, keepdims=True) * (1.0 / HD) + 1e-05)
        n = o * scale
        y_ref[lo : lo + QB, :] = (n * gate).astype(BF)
        dy = dot(gs[0][lo : lo + QB, :], wo[:, 0:128], 1, 1)
        for k in range(1, NT):
            dy = dy + dot(gs[k][lo : lo + QB, :], wo[:, k * 128 : (k + 1) * 128], 1, 1)
        dy = dy.astype(BF).astype(F32)
        dgate = (dy * n).astype(BF).astype(F32)
        dn = dy * gate
        m1 = jnp.sum(dn, axis=1, keepdims=True) * (1.0 / HD)
        m2 = jnp.sum(dn * n, axis=1, keepdims=True) * (1.0 / HD)
        do = ((dn - m1 - n * m2) * scale).astype(BF)
        dp_ref[lo : lo + QB, 0:128] = (dgate * pre[lo : lo + QB, 0:128]).astype(BF)
        dq = jnp.zeros((QB, HD), F32)
        for kb in range(k0, lo + QB, QB):
            at = kb - k0
            da = dot(do, act[kb : kb + QB, 128:256], 1, 1).astype(BF).astype(F32)
            ds = (da * dsil[:, at : at + QB]).astype(BF)
            dq = dq + dot(ds, act[kb : kb + QB, 384:512], 1, 0)
            dkv[kb : kb + QB, 0:128] += dot(aw[:, at : at + QB], do, 0, 0)
            dkv[kb : kb + QB, 128:256] += dot(ds, queries, 0, 0)
        dq = dq.astype(BF).astype(F32)
        dp_ref[lo : lo + QB, 256:384] = (dq * pre[lo : lo + QB, 256:384]).astype(BF)

    for q in range(TOK // QB):
        lo = q * QB
        dvb = dkv[lo : lo + QB, 0:128].astype(BF).astype(F32)
        dkb = dkv[lo : lo + QB, 128:256].astype(BF).astype(F32)
        dp_ref[lo : lo + QB, 128:256] = (dvb * pre[lo : lo + QB, 128:256]).astype(BF)
        dp_ref[lo : lo + QB, 384:512] = (dkb * pre[lo : lo + QB, 384:512]).astype(BF)
        du[...] = dot(dp_ref[lo : lo + QB, :], w[...], 1, 1).astype(BF).astype(F32)
        for r in range(0, QB, step):
            n, scale = stats(lo + r, step)
            d = [du[r : r + step, k * 128 : (k + 1) * 128] for k in range(NT)]
            m1 = jnp.sum(d[0] + d[1] + d[2] + d[3], axis=1, keepdims=True) * (1.0 / D)
            m2 = jnp.sum(
                d[0] * n[0] + d[1] * n[1] + d[2] * n[2] + d[3] * n[3], axis=1, keepdims=True
            ) * (1.0 / D)
            for k in range(NT):
                dxs[k][lo + r : lo + r + step, :] = ((d[k] - m1 - n[k] * m2) * scale).astype(BF)

    for k in range(NT):
        at = pl.multiple_of(lax.rem(me + k, NT) * 128, 128)
        dw = dot(u_ref[:, k * 128 : (k + 1) * 128], dp_ref[...], 0, 0)
        for c in range(4):
            dw_ref[pl.ds(pl.multiple_of(c * 512 + at, 128), 128), :] = dw[:, c * 128 : (c + 1) * 128]
        dw_ref[pl.ds(pl.multiple_of(2048 + at, 128), 128), :] = dot(y_ref[...], gs[k][...], 0, 0)
        zs[k][...] = dot(y_ref[...], wo[:, k * 128 : (k + 1) * 128], 1, 0).astype(BF)
    mine_ref[...] = dw_ref[pl.ds(pl.multiple_of(core * 1280, 1280), 1280), :]
    other_ref[...] = dw_ref[pl.ds(pl.multiple_of(1280 - core * 1280, 1280), 1280), :].astype(BF)


def layer(pos, core, seg, xs, gs, w_in, w_out):
    piece = jax.ShapeDtypeStruct((TOK, 128), BF)
    return pl.pallas_call(
        layer_kernel,
        out_shape=(jax.ShapeDtypeStruct((1280, 128), F32), jax.ShapeDtypeStruct((1280, 128), BF))
        + (piece,) * 8,
        in_specs=[SM, SM] + [VM] * 11,
        out_specs=(VM,) * 10,
        scratch_shapes=[
            pltpu.VMEM((D, 512), BF),
            pltpu.VMEM((HD, D), BF),
            pltpu.VMEM((TOK, 512), F32),
            pltpu.VMEM((TOK, 512), BF),
            pltpu.VMEM((TOK, 128), F32),
            pltpu.VMEM((QB, 768), BF),
            pltpu.VMEM((QB, 768), F32),
            pltpu.VMEM((TOK, 256), F32),
            pltpu.VMEM((QB, 512), F32),
            pltpu.VMEM((TOK, D), BF),
            pltpu.VMEM((TOK, HD), BF),
            pltpu.VMEM((TOK, 512), BF),
            pltpu.VMEM((2560, 128), F32),
        ],
        compiler_params=PARAMS,
        name="layer",
    )(pos, core, seg, *xs, *gs, w_in, w_out)


def spread(at_ref, blocks, size, values):
    lows, highs, pairs = [], [], []
    for b in range(blocks):
        at = at_ref[b : b + 1, :]
        upper = column((at >= size).astype(F32)) > 0.5
        value = values[b * 128 : (b + 1) * 128, :]
        pairs.append(
            jnp.concatenate([jnp.where(upper, 0.0, value), jnp.where(upper, value, 0.0)], axis=1).astype(BF)
        )
        at = jnp.broadcast_to(jnp.where(at >= size, at - size, at), (128, 128))
        lows.append(((at & 127) == iota((128, 128), 0)).astype(F32).astype(BF))
        highs.append((at >> 7).astype(F32).astype(BF))
    low = jnp.concatenate(lows, axis=1)
    high = jnp.concatenate(highs, axis=1)
    pair = jnp.concatenate(pairs, axis=0)
    return [dot(hot_where(high, s, low), pair, 1, 0) for s in range(size // 128)]


def slots_kernel(slot_ref, grad_ref, d0, d1, d2, d3, out_ref):
    dx = grad_ref[...].astype(F32) + (
        d0[...].astype(F32) + d1[...].astype(F32) + d2[...].astype(F32) + d3[...].astype(F32)
    )
    half = SLOTS // 2
    for s, both in enumerate(spread(slot_ref, TOK // 128, half, dx)):
        out_ref[s * 128 : (s + 1) * 128, :] = both[:, :128].astype(BF)
        out_ref[half + s * 128 : half + (s + 1) * 128, :] = both[:, 128:].astype(BF)


def to_slots(slot, grad, parts):
    return pl.pallas_call(
        slots_kernel,
        out_shape=jax.ShapeDtypeStruct((SLOTS, 128), BF),
        in_specs=[VM] * 6,
        out_specs=VM,
        compiler_params=PARAMS,
        name="to_slots",
    )(slot, grad, *parts)


def add_rows_kernel(req_ref, arrived_ref, out_ref):
    half = ROWS // 2
    for s, both in enumerate(spread(req_ref, SLOTS // 128, half, arrived_ref[...].astype(F32))):
        out_ref[s * 128 : (s + 1) * 128, :] = both[:, :128]
        out_ref[half + s * 128 : half + (s + 1) * 128, :] = both[:, 128:]


def add_rows(req, arrived):
    return pl.pallas_call(
        add_rows_kernel,
        out_shape=jax.ShapeDtypeStruct((ROWS, 128), F32),
        in_specs=[VM, VM],
        out_specs=VM,
        compiler_params=PARAMS,
        name="add_rows",
    )(req, arrived)


def unpack_kernel(y_ref, p0, p1, p2, p3, in_ref, out_ref, whole):
    for k, p in enumerate((p0, p1, p2, p3)):
        half, quarter = y_place(lax.rem(y_ref[0] + k, 4))
        for core in range(2):
            at = pl.multiple_of(half * 640 + quarter * 320 + core * 1280, 320)
            whole[pl.ds(at, 320), :] = p[core * 320 : (core + 1) * 320, :].astype(F32)
    in_ref[...] = whole[0:2048, :]
    for k in range(NT):
        out_ref[:, k * 128 : (k + 1) * 128] = whole[2048 + k * 128 : 2176 + k * 128, :]


def unpack(y, parts):
    return pl.pallas_call(
        unpack_kernel,
        out_shape=(jax.ShapeDtypeStruct((2048, 128), F32), jax.ShapeDtypeStruct((HD, D), F32)),
        in_specs=[SM] + [VM] * 4,
        out_specs=(VM, VM),
        scratch_shapes=[pltpu.VMEM((2560, 128), F32)],
        compiler_params=PARAMS,
        name="unpack",
    )(y, *parts)


def shift(x, axis, fn, n):
    return lax.ppermute(x, axis, [(i, fn(i)) for i in range(n)])


def gather_pieces(x):
    return [x] + [shift(x, "tensor", lambda i, k=k: (i - k) % NT, NT) for k in (1, 3, 2)]


def order(pieces):
    own, one, three, two = pieces
    return [own, one, two, three]


def scatter_pieces(parts):
    return [parts[0]] + [shift(parts[k], "tensor", lambda i, k=k: (i + k) % NT, NT) for k in (1, 3, 2)]


def pick(x, i):
    return lax.dynamic_index_in_dim(x, i, 0, keepdims=False)


def y_place(y):
    return ((y == 1) | (y == 2)).astype(I32), (y >= 2).astype(I32)


def reduce_over_chips(mine, other):
    half, quarter = y_place(lax.axis_index("table") // 2)
    other = shift(other, "table", lambda i: i ^ 1, 8)
    mine = (mine + other.astype(F32)).reshape(2, 640, 128)
    got = shift(pick(mine, 1 - half).astype(BF), "table", lambda i: i ^ 2, 8)
    mine = (pick(mine, half) + got.astype(F32)).reshape(2, 320, 128)
    got = shift(pick(mine, 1 - quarter).astype(BF), "table", lambda i: 6 - (i & 6) + (i & 1), 8)
    return pick(mine, quarter), got


def add_step(total, mask):
    return (total.astype(F32) + shift(total, "seq", lambda i: i ^ mask, 8).astype(F32)).astype(BF)


def gather_weights(total):
    y = (lax.axis_index("table") // 2).astype(I32).reshape(1)
    pairs = [[2 * i, 2 * i + 1] for i in range(4)]
    both = lax.all_gather(total, "table", axis=0, tiled=True, axis_index_groups=pairs)
    parts = [both] + [shift(both, "table", lambda i, k=k: (i - 2 * k) % 8, 8) for k in range(1, 4)]
    return unpack(y, parts)


def body(table, owner, local_row, segment_ids, proj_in, proj_out, grad_out):
    pos = lax.axis_index("tensor").astype(I32).reshape(1)
    core = (lax.axis_index("table") % 2).astype(I32).reshape(1)
    requests, slot = route(owner.reshape(8, 128), local_row.reshape(8, 128))
    gs = order(gather_pieces(grad_out))
    received = lax.all_to_all(requests, BOTH, split_axis=0, concat_axis=0, tiled=True)
    rows = fetch(received, table)
    back = lax.all_to_all(rows.reshape(NOWN, CAP, 128), BOTH, split_axis=0, concat_axis=0, tiled=True)
    x = place(slot, back.reshape(SLOTS, 128))
    xs = order(gather_pieces(x))
    mine, other, d0, d1, d2, d3, z0, z1, z2, z3 = layer(
        pos, core, segment_ids, xs, gs, proj_in, proj_out
    )
    dparts = scatter_pieces([d0, d1, d2, d3])
    own, got = reduce_over_chips(mine, other)
    dparts, got = lax.optimization_barrier((dparts, got))
    grads = to_slots(slot, grad_out, dparts)
    total = add_step(add_step((own + got.astype(F32)).astype(BF), 1), 2)
    arrived = lax.all_to_all(grads.reshape(NOWN, CAP, 128), BOTH, split_axis=0, concat_axis=0, tiled=True)
    total, zs = lax.optimization_barrier((total, [z0, z1, z2, z3]))
    total = add_step(total, 7)
    zparts = scatter_pieces(zs)
    flat = received[:, :CAP].reshape(SLOTS // 128, 128)
    total, arrived, zparts, flat = lax.optimization_barrier((total, arrived, zparts, flat))
    table_grad = add_rows(flat, arrived.reshape(SLOTS, 128))
    grad_in, grad_outw = gather_weights(total)
    layer_out = (
        x.astype(F32)
        + (zparts[0].astype(F32) + zparts[1].astype(F32) + zparts[2].astype(F32) + zparts[3].astype(F32))
    ).astype(BF)
    return layer_out, table_grad, grad_in.reshape(4, D, 128), grad_outw


def solution(mesh):
    in_specs = (
        P(BOTH, "tensor"),
        P(BOTH, None),
        P(BOTH),
        P(BOTH, None),
        P(None, None, "tensor"),
        P("tensor", None),
        P(BOTH, "tensor"),
    )
    out_specs = (
        P(BOTH, "tensor"),
        P(BOTH, "tensor"),
        P(None, None, "tensor"),
        P("tensor", None),
    )
    return jax.shard_map(body, mesh=mesh, in_specs=in_specs, out_specs=out_specs, check_vma=False)
```

```python
import functools

import jax
import jax.numpy as jnp
from jax import lax
from jax.experimental import pallas as pl
from jax.experimental.pallas import tpu as pltpu
from jax.sharding import PartitionSpec as P

HD = 128
SEQ_MOST = 512
TOK = 1024
D = 512
NT = 4
NOWN = 64
CAP = 24
SLOTS = NOWN * CAP
ROWS = 2048
QB = 256
BOTH = ("table", "seq")
BF = jnp.bfloat16
F32 = jnp.float32
I32 = jnp.int32
VM = pl.BlockSpec(memory_space=pltpu.VMEM)
SM = pl.BlockSpec(memory_space=pltpu.SMEM)
PARAMS = pltpu.CompilerParams(vmem_limit_bytes=56 * 1024 * 1024)


def iota(shape, dim):
    return lax.broadcasted_iota(I32, shape, dim)


def dot(a, b, ca, cb):
    return lax.dot_general(a, b, (((ca,), (cb,)), ((), ())), preferred_element_type=F32)


def route_kernel(owner_ref, row_ref, req_ref, slot_ref):
    blocks = TOK // 128
    upper = (iota((128, 128), 0) < iota((128, 128), 1)).astype(BF)
    scan = jnp.concatenate([upper, jnp.ones((128, 128), BF)], axis=1)
    hots = [(iota((NOWN, 128), 0) == owner_ref[b : b + 1, :]).astype(F32) for b in range(blocks)]
    sums = dot(jnp.concatenate(hots, axis=0).astype(BF), scan, 1, 0)
    carry = jnp.zeros((NOWN, 128), F32)
    highs, lows = [], []
    for b in range(blocks):
        part = sums[b * NOWN : (b + 1) * NOWN, :]
        rank = jnp.sum(hots[b] * (part[:, :128] + carry), axis=0, keepdims=True).astype(I32)
        carry = carry + part[:, 128:]
        row = row_ref[b : b + 1, :]
        slot_ref[b : b + 1, :] = owner_ref[b : b + 1, :] * CAP + rank
        here = iota((32, 128), 0) == rank
        highs.append(jnp.where(here, (row >> 6).astype(F32), 0.0))
        lows.append(jnp.where(here, (row & 63).astype(F32), 0.0))
    hot = jnp.concatenate(hots, axis=1).astype(BF)
    high = dot(hot, jnp.concatenate(highs, axis=1).astype(BF), 1, 1)
    low = dot(hot, jnp.concatenate(lows, axis=1).astype(BF), 1, 1)
    req_ref[...] = jnp.zeros((NOWN, 128), I32)
    req_ref[:, 0:32] = (high * 64.0 + low).astype(I32)


def route(owner, row):
    return pl.pallas_call(
        route_kernel,
        out_shape=(
            jax.ShapeDtypeStruct((NOWN, 128), I32),
            jax.ShapeDtypeStruct((TOK // 128, 128), I32),
        ),
        in_specs=[VM, VM],
        out_specs=(VM, VM),
        compiler_params=PARAMS,
        name="route",
    )(owner, row)


def hot_where(high, value, low_hot):
    return jnp.where(high == value, low_hot, jnp.zeros_like(low_hot))


def fetch_kernel(req_ref, table_ref, out_ref, got):
    half = ROWS // 2
    both = jnp.concatenate([table_ref[:half, :], table_ref[half:, :]], axis=1)
    for c0 in range(0, CAP, 4):
        hots, uppers = [], []
        for c in range(c0, c0 + 4):
            row = jnp.broadcast_to(req_ref[:, c : c + 1], (NOWN, 128))
            low = ((row & 127) == iota((NOWN, 128), 1)).astype(F32).astype(BF)
            high = ((row >> 7) & 7).astype(F32).astype(BF)
            hots.append(jnp.concatenate([hot_where(high, j, low) for j in range(8)], axis=1))
            uppers.append(row >= half)
        pair = dot(jnp.concatenate(hots, axis=0), both, 1, 0)
        rows = jnp.where(jnp.concatenate(uppers, axis=0), pair[:, 128:], pair[:, :128])
        for i in range(4):
            got[pl.ds(c0 + i, NOWN, stride=CAP), :] = rows[i * NOWN : (i + 1) * NOWN, :]
    out_ref[...] = got[...].astype(BF)


def fetch(req, table):
    return pl.pallas_call(
        fetch_kernel,
        out_shape=jax.ShapeDtypeStruct((SLOTS, 128), BF),
        in_specs=[VM, VM],
        out_specs=VM,
        scratch_shapes=[pltpu.VMEM((SLOTS, 128), F32)],
        compiler_params=PARAMS,
        name="fetch",
    )(req, table)


def column(row_vector):
    wide = jnp.broadcast_to(row_vector.astype(F32), (128, 128))
    return jnp.transpose(wide)


def place_kernel(slot_ref, back_ref, x_ref):
    half = SLOTS // 2
    both = jnp.concatenate([back_ref[:half, :], back_ref[half:, :]], axis=1)
    for b0 in range(0, TOK // 128, 2):
        hots, uppers = [], []
        for b in (b0, b0 + 1):
            slot = column(slot_ref[b : b + 1, :]).astype(I32)
            upper = slot >= half
            slot = jnp.where(upper, slot - half, slot)
            low = ((slot & 127) == iota((128, 128), 1)).astype(F32).astype(BF)
            high = (slot >> 7).astype(F32).astype(BF)
            hots.append(jnp.concatenate([hot_where(high, j, low) for j in range(half // 128)], axis=1))
            uppers.append(upper)
        pair = dot(jnp.concatenate(hots, axis=0), both, 1, 0)
        rows = jnp.where(jnp.concatenate(uppers, axis=0), pair[:, 128:], pair[:, :128])
        x_ref[b0 * 128 : b0 * 128 + 256, :] = rows.astype(BF)


def place(slot, back):
    return pl.pallas_call(
        place_kernel,
        out_shape=jax.ShapeDtypeStruct((TOK, 128), BF),
        in_specs=[VM, VM],
        out_specs=VM,
        compiler_params=PARAMS,
        name="place",
    )(slot, back)


def layer_kernel(
    pos_ref, core_ref, seg_ref, x0, x1, x2, x3, g0, g1, g2, g3, win_ref, wout_ref,
    mine_ref, other_ref, dx0, dx1, dx2, dx3, z0, z1, z2, z3,
    w, wo, pre, act, segc, aw, dsil, dkv, du, u_ref, y_ref, dp_ref, dw_ref,
):
    xs, gs = (x0, x1, x2, x3), (g0, g1, g2, g3)
    dxs, zs = (dx0, dx1, dx2, dx3), (z0, z1, z2, z3)
    me, core = pos_ref[0], core_ref[0]
    for k in range(NT):
        at = pl.multiple_of(lax.rem(me + k, NT) * 128, 128)
        for c in range(4):
            w[k * 128 : (k + 1) * 128, c * 128 : (c + 1) * 128] = win_ref[c, pl.ds(at, 128), :]
        wo[:, k * 128 : (k + 1) * 128] = wout_ref[:, pl.ds(at, 128)]
    for b in range(TOK // 128):
        segc[b * 128 : (b + 1) * 128, :] = column(
            seg_ref[0:1, b * 128 : (b + 1) * 128]
        )

    def stats(r0, n):
        x = [r[r0 : r0 + n, :].astype(F32) for r in xs]
        mean = jnp.sum(x[0] + x[1] + x[2] + x[3], axis=1, keepdims=True) * (1.0 / D)
        x = [v - mean for v in x]
        var = jnp.sum(x[0] * x[0] + x[1] * x[1] + x[2] * x[2] + x[3] * x[3], axis=1, keepdims=True)
        scale = lax.rsqrt(var * (1.0 / D) + 1e-05)
        return [v * scale for v in x], scale

    step = 64
    for q in range(TOK // QB):
        lo = q * QB
        for r0 in range(lo, lo + QB, step):
            n, _ = stats(r0, step)
            for k in range(NT):
                u_ref[r0 : r0 + step, k * 128 : (k + 1) * 128] = n[k].astype(BF)
        pre[lo : lo + QB, :] = dot(u_ref[lo : lo + QB, :], w[...], 1, 0)
        for r0 in range(lo, lo + QB, step):
            p = pre[r0 : r0 + step, :]
            s = 0.5 + 0.5 * jnp.tanh(0.5 * p)
            ps = p * s
            act[r0 : r0 + step, :] = ps.astype(BF)
            pre[r0 : r0 + step, :] = s + ps * (1.0 - s)

    dkv[...] = jnp.zeros((TOK, 256), F32)
    for q in range(TOK // QB):
        lo = q * QB
        k0 = max(0, lo - SEQ_MOST)
        width = lo + QB - k0
        queries = act[lo : lo + QB, 256:384]
        o = jnp.zeros((QB, HD), F32)
        for kb in range(k0, lo + QB, QB):
            sc = dot(queries, act[kb : kb + QB, 384:512], 1, 1) * (HD ** (-0.5))
            for j in range(0, QB, 128):
                same = segc[lo : lo + QB, :] == seg_ref[0:1, kb + j : kb + j + 128].astype(F32)
                if kb == lo:
                    same = same & (iota((QB, 128), 1) + j <= iota((QB, 128), 0))
                v = sc[:, j : j + 128]
                s = 0.5 + 0.5 * jnp.tanh(0.5 * v)
                vs = v * s
                at = kb - k0 + j
                aw[:, at : at + 128] = jnp.where(same, vs * (1.0 / SEQ_MOST), 0.0).astype(BF)
                dsil[:, at : at + 128] = jnp.where(
                    same, (s + vs * (1.0 - s)) * (HD ** (-0.5) / SEQ_MOST), 0.0
                )
        o = dot(aw[:, 0:width], act[k0 : lo + QB, 128:256], 1, 0)
        gate = act[lo : lo + QB, 0:128].astype(F32)
        mean = jnp.sum(o, axis=1, keepdims=True) * (1.0 / HD)
        o = o - mean
        scale = lax.rsqrt(jnp.sum(o * o, axis=1, keepdims=True) * (1.0 / HD) + 1e-05)
        n = o * scale
        y_ref[lo : lo + QB, :] = (n * gate).astype(BF)
        dy = dot(gs[0][lo : lo + QB, :], wo[:, 0:128], 1, 1)
        for k in range(1, NT):
            dy = dy + dot(gs[k][lo : lo + QB, :], wo[:, k * 128 : (k + 1) * 128], 1, 1)
        dy = dy.astype(BF).astype(F32)
        dgate = (dy * n).astype(BF).astype(F32)
        dn = dy * gate
        m1 = jnp.sum(dn, axis=1, keepdims=True) * (1.0 / HD)
        m2 = jnp.sum(dn * n, axis=1, keepdims=True) * (1.0 / HD)
        do = ((dn - m1 - n * m2) * scale).astype(BF)
        dp_ref[lo : lo + QB, 0:128] = (dgate * pre[lo : lo + QB, 0:128]).astype(BF)
        dq = jnp.zeros((QB, HD), F32)
        for kb in range(k0, lo + QB, QB):
            at = kb - k0
            da = dot(do, act[kb : kb + QB, 128:256], 1, 1).astype(BF).astype(F32)
            ds = (da * dsil[:, at : at + QB]).astype(BF)
            dq = dq + dot(ds, act[kb : kb + QB, 384:512], 1, 0)
            dkv[kb : kb + QB, 0:128] += dot(aw[:, at : at + QB], do, 0, 0)
            dkv[kb : kb + QB, 128:256] += dot(ds, queries, 0, 0)
        dq = dq.astype(BF).astype(F32)
        dp_ref[lo : lo + QB, 256:384] = (dq * pre[lo : lo + QB, 256:384]).astype(BF)

    for q in range(TOK // QB):
        lo = q * QB
        dvb = dkv[lo : lo + QB, 0:128].astype(BF).astype(F32)
        dkb = dkv[lo : lo + QB, 128:256].astype(BF).astype(F32)
        dp_ref[lo : lo + QB, 128:256] = (dvb * pre[lo : lo + QB, 128:256]).astype(BF)
        dp_ref[lo : lo + QB, 384:512] = (dkb * pre[lo : lo + QB, 384:512]).astype(BF)
        du[...] = dot(dp_ref[lo : lo + QB, :], w[...], 1, 1).astype(BF).astype(F32)
        for r in range(0, QB, step):
            n, scale = stats(lo + r, step)
            d = [du[r : r + step, k * 128 : (k + 1) * 128] for k in range(NT)]
            m1 = jnp.sum(d[0] + d[1] + d[2] + d[3], axis=1, keepdims=True) * (1.0 / D)
            m2 = jnp.sum(
                d[0] * n[0] + d[1] * n[1] + d[2] * n[2] + d[3] * n[3], axis=1, keepdims=True
            ) * (1.0 / D)
            for k in range(NT):
                dxs[k][lo + r : lo + r + step, :] = ((d[k] - m1 - n[k] * m2) * scale).astype(BF)

    for k in range(NT):
        at = pl.multiple_of(lax.rem(me + k, NT) * 128, 128)
        dw = dot(u_ref[:, k * 128 : (k + 1) * 128], dp_ref[...], 0, 0)
        for c in range(4):
            dw_ref[pl.ds(pl.multiple_of(c * 512 + at, 128), 128), :] = dw[:, c * 128 : (c + 1) * 128]
        dw_ref[pl.ds(pl.multiple_of(2048 + at, 128), 128), :] = dot(y_ref[...], gs[k][...], 0, 0)
        zs[k][...] = dot(y_ref[...], wo[:, k * 128 : (k + 1) * 128], 1, 0).astype(BF)
    mine_ref[...] = dw_ref[pl.ds(pl.multiple_of(core * 1280, 1280), 1280), :]
    other_ref[...] = dw_ref[pl.ds(pl.multiple_of(1280 - core * 1280, 1280), 1280), :].astype(BF)


def layer(pos, core, seg, xs, gs, w_in, w_out):
    piece = jax.ShapeDtypeStruct((TOK, 128), BF)
    return pl.pallas_call(
        layer_kernel,
        out_shape=(jax.ShapeDtypeStruct((1280, 128), F32), jax.ShapeDtypeStruct((1280, 128), BF))
        + (piece,) * 8,
        in_specs=[SM, SM] + [VM] * 11,
        out_specs=(VM,) * 10,
        scratch_shapes=[
            pltpu.VMEM((D, 512), BF),
            pltpu.VMEM((HD, D), BF),
            pltpu.VMEM((TOK, 512), F32),
            pltpu.VMEM((TOK, 512), BF),
            pltpu.VMEM((TOK, 128), F32),
            pltpu.VMEM((QB, 768), BF),
            pltpu.VMEM((QB, 768), F32),
            pltpu.VMEM((TOK, 256), F32),
            pltpu.VMEM((QB, 512), F32),
            pltpu.VMEM((TOK, D), BF),
            pltpu.VMEM((TOK, HD), BF),
            pltpu.VMEM((TOK, 512), BF),
            pltpu.VMEM((2560, 128), F32),
        ],
        compiler_params=PARAMS,
        name="layer",
    )(pos, core, seg, *xs, *gs, w_in, w_out)


def spread(at_ref, blocks, size, values):
    lows, highs, pairs = [], [], []
    for b in range(blocks):
        at = at_ref[b : b + 1, :]
        upper = column((at >= size).astype(F32)) > 0.5
        value = values[b * 128 : (b + 1) * 128, :]
        pairs.append(
            jnp.concatenate([jnp.where(upper, 0.0, value), jnp.where(upper, value, 0.0)], axis=1).astype(BF)
        )
        at = jnp.broadcast_to(jnp.where(at >= size, at - size, at), (128, 128))
        lows.append(((at & 127) == iota((128, 128), 0)).astype(F32).astype(BF))
        highs.append((at >> 7).astype(F32).astype(BF))
    low = jnp.concatenate(lows, axis=1)
    high = jnp.concatenate(highs, axis=1)
    pair = jnp.concatenate(pairs, axis=0)
    return [dot(hot_where(high, s, low), pair, 1, 0) for s in range(size // 128)]


def slots_kernel(slot_ref, grad_ref, d0, d1, d2, d3, out_ref):
    dx = grad_ref[...].astype(F32) + (
        d0[...].astype(F32) + d1[...].astype(F32) + d2[...].astype(F32) + d3[...].astype(F32)
    )
    half = SLOTS // 2
    for s, both in enumerate(spread(slot_ref, TOK // 128, half, dx)):
        out_ref[s * 128 : (s + 1) * 128, :] = both[:, :128].astype(BF)
        out_ref[half + s * 128 : half + (s + 1) * 128, :] = both[:, 128:].astype(BF)


def to_slots(slot, grad, parts):
    return pl.pallas_call(
        slots_kernel,
        out_shape=jax.ShapeDtypeStruct((SLOTS, 128), BF),
        in_specs=[VM] * 6,
        out_specs=VM,
        compiler_params=PARAMS,
        name="to_slots",
    )(slot, grad, *parts)


def add_rows_kernel(req_ref, arrived_ref, out_ref):
    half = ROWS // 2
    for s, both in enumerate(spread(req_ref, SLOTS // 128, half, arrived_ref[...].astype(F32))):
        out_ref[s * 128 : (s + 1) * 128, :] = both[:, :128]
        out_ref[half + s * 128 : half + (s + 1) * 128, :] = both[:, 128:]


def add_rows(req, arrived):
    return pl.pallas_call(
        add_rows_kernel,
        out_shape=jax.ShapeDtypeStruct((ROWS, 128), F32),
        in_specs=[VM, VM],
        out_specs=VM,
        compiler_params=PARAMS,
        name="add_rows",
    )(req, arrived)


def unpack_kernel(y_ref, p0, p1, p2, p3, in_ref, out_ref, whole):
    for k, p in enumerate((p0, p1, p2, p3)):
        half, quarter = y_place(lax.rem(y_ref[0] + k, 4))
        for core in range(2):
            at = pl.multiple_of(half * 640 + quarter * 320 + core * 1280, 320)
            whole[pl.ds(at, 320), :] = p[core * 320 : (core + 1) * 320, :].astype(F32)
    in_ref[...] = whole[0:2048, :]
    for k in range(NT):
        out_ref[:, k * 128 : (k + 1) * 128] = whole[2048 + k * 128 : 2176 + k * 128, :]


def unpack(y, parts):
    return pl.pallas_call(
        unpack_kernel,
        out_shape=(jax.ShapeDtypeStruct((2048, 128), F32), jax.ShapeDtypeStruct((HD, D), F32)),
        in_specs=[SM] + [VM] * 4,
        out_specs=(VM, VM),
        scratch_shapes=[pltpu.VMEM((2560, 128), F32)],
        compiler_params=PARAMS,
        name="unpack",
    )(y, *parts)


def shift(x, axis, fn, n):
    return lax.ppermute(x, axis, [(i, fn(i)) for i in range(n)])


def gather_pieces(x):
    return [x] + [shift(x, "tensor", lambda i, k=k: (i - k) % NT, NT) for k in (1, 3, 2)]


def order(pieces):
    own, one, three, two = pieces
    return [own, one, two, three]


def scatter_pieces(parts):
    return [parts[0]] + [shift(parts[k], "tensor", lambda i, k=k: (i + k) % NT, NT) for k in (1, 3, 2)]


def pick(x, i):
    return lax.dynamic_index_in_dim(x, i, 0, keepdims=False)


def y_place(y):
    return ((y == 1) | (y == 2)).astype(I32), (y >= 2).astype(I32)


def reduce_over_chips(mine, other):
    half, quarter = y_place(lax.axis_index("table") // 2)
    other = shift(other, "table", lambda i: i ^ 1, 8)
    mine = (mine + other.astype(F32)).reshape(2, 640, 128)
    got = shift(pick(mine, 1 - half).astype(BF), "table", lambda i: i ^ 2, 8)
    mine = (pick(mine, half) + got.astype(F32)).reshape(2, 320, 128)
    got = shift(pick(mine, 1 - quarter).astype(BF), "table", lambda i: 6 - (i & 6) + (i & 1), 8)
    return pick(mine, quarter), got


def add_step(total, mask):
    return (total.astype(F32) + shift(total, "seq", lambda i: i ^ mask, 8).astype(F32)).astype(BF)


def gather_weights(total):
    y = (lax.axis_index("table") // 2).astype(I32).reshape(1)
    pairs = [[2 * i, 2 * i + 1] for i in range(4)]
    both = lax.all_gather(total, "table", axis=0, tiled=True, axis_index_groups=pairs)
    parts = [both] + [shift(both, "table", lambda i, k=k: (i - 2 * k) % 8, 8) for k in range(1, 4)]
    return unpack(y, parts)


def body(table, owner, local_row, segment_ids, proj_in, proj_out, grad_out):
    pos = lax.axis_index("tensor").astype(I32).reshape(1)
    core = (lax.axis_index("table") % 2).astype(I32).reshape(1)
    requests, slot = route(owner.reshape(8, 128), local_row.reshape(8, 128))
    gs = order(gather_pieces(grad_out))
    received = lax.all_to_all(requests, BOTH, split_axis=0, concat_axis=0, tiled=True)
    rows = fetch(received, table)
    back = lax.all_to_all(rows.reshape(NOWN, CAP, 128), BOTH, split_axis=0, concat_axis=0, tiled=True)
    x = place(slot, back.reshape(SLOTS, 128))
    xs = order(gather_pieces(x))
    mine, other, d0, d1, d2, d3, z0, z1, z2, z3 = layer(
        pos, core, segment_ids, xs, gs, proj_in, proj_out
    )
    dparts = scatter_pieces([d0, d1, d2, d3])
    own, got = reduce_over_chips(mine, other)
    flat = received[:, :CAP].reshape(SLOTS // 128, 128)
    total = add_step((own + got.astype(F32)).astype(BF), 1)
    dparts, total, flat = lax.optimization_barrier((dparts, total, flat))
    grads = to_slots(slot, grad_out, dparts)
    total = add_step(add_step(total, 2), 7)
    grads, total, zs = lax.optimization_barrier((grads, total, [z0, z1, z2, z3]))
    arrived = lax.all_to_all(grads.reshape(NOWN, CAP, 128), BOTH, split_axis=0, concat_axis=0, tiled=True)
    grad_in, grad_outw = gather_weights(total)
    zparts = scatter_pieces(zs)
    table_grad = add_rows(flat, arrived.reshape(SLOTS, 128))
    layer_out = (
        x.astype(F32)
        + (zparts[0].astype(F32) + zparts[1].astype(F32) + zparts[2].astype(F32) + zparts[3].astype(F32))
    ).astype(BF)
    return layer_out, table_grad, grad_in.reshape(4, D, 128), grad_outw


def solution(mesh):
    in_specs = (
        P(BOTH, "tensor"),
        P(BOTH, None),
        P(BOTH),
        P(BOTH, None),
        P(None, None, "tensor"),
        P("tensor", None),
        P(BOTH, "tensor"),
    )
    out_specs = (
        P(BOTH, "tensor"),
        P(BOTH, "tensor"),
        P(None, None, "tensor"),
        P("tensor", None),
    )
    return jax.shard_map(body, mesh=mesh, in_specs=in_specs, out_specs=out_specs, check_vma=False)
```

```python
import functools

import jax
import jax.numpy as jnp
from jax import lax
from jax.experimental import pallas as pl
from jax.experimental.pallas import tpu as pltpu
from jax.sharding import PartitionSpec as P

HD = 128
SEQ_MOST = 512
TOK = 1024
D = 512
NT = 4
NOWN = 64
CAP = 24
SLOTS = NOWN * CAP
ROWS = 2048
QB = 256
BOTH = ("table", "seq")
BF = jnp.bfloat16
F32 = jnp.float32
I32 = jnp.int32
VM = pl.BlockSpec(memory_space=pltpu.VMEM)
SM = pl.BlockSpec(memory_space=pltpu.SMEM)
PARAMS = pltpu.CompilerParams(vmem_limit_bytes=56 * 1024 * 1024)


def iota(shape, dim):
    return lax.broadcasted_iota(I32, shape, dim)


def dot(a, b, ca, cb):
    return lax.dot_general(a, b, (((ca,), (cb,)), ((), ())), preferred_element_type=F32)


def route_kernel(owner_ref, row_ref, req_ref, slot_ref):
    blocks = TOK // 128
    upper = (iota((128, 128), 0) < iota((128, 128), 1)).astype(BF)
    scan = jnp.concatenate([upper, jnp.ones((128, 128), BF)], axis=1)
    hots = [(iota((NOWN, 128), 0) == owner_ref[b : b + 1, :]).astype(F32) for b in range(blocks)]
    sums = dot(jnp.concatenate(hots, axis=0).astype(BF), scan, 1, 0)
    carry = jnp.zeros((NOWN, 128), F32)
    highs, lows = [], []
    for b in range(blocks):
        part = sums[b * NOWN : (b + 1) * NOWN, :]
        rank = jnp.sum(hots[b] * (part[:, :128] + carry), axis=0, keepdims=True).astype(I32)
        carry = carry + part[:, 128:]
        row = row_ref[b : b + 1, :]
        slot_ref[b : b + 1, :] = owner_ref[b : b + 1, :] * CAP + rank
        here = iota((32, 128), 0) == rank
        highs.append(jnp.where(here, (row >> 6).astype(F32), 0.0))
        lows.append(jnp.where(here, (row & 63).astype(F32), 0.0))
    hot = jnp.concatenate(hots, axis=1).astype(BF)
    high = dot(hot, jnp.concatenate(highs, axis=1).astype(BF), 1, 1)
    low = dot(hot, jnp.concatenate(lows, axis=1).astype(BF), 1, 1)
    req_ref[...] = jnp.zeros((NOWN, 128), I32)
    req_ref[:, 0:32] = (high * 64.0 + low).astype(I32)


def route(owner, row):
    return pl.pallas_call(
        route_kernel,
        out_shape=(
            jax.ShapeDtypeStruct((NOWN, 128), I32),
            jax.ShapeDtypeStruct((TOK // 128, 128), I32),
        ),
        in_specs=[VM, VM],
        out_specs=(VM, VM),
        compiler_params=PARAMS,
        name="route",
    )(owner, row)


def hot_where(high, value, low_hot):
    return jnp.where(high == value, low_hot, jnp.zeros_like(low_hot))


def fetch_kernel(req_ref, table_ref, out_ref, got):
    half = ROWS // 2
    both = jnp.concatenate([table_ref[:half, :], table_ref[half:, :]], axis=1)
    for c0 in range(0, CAP, 4):
        hots, uppers = [], []
        for c in range(c0, c0 + 4):
            row = jnp.broadcast_to(req_ref[:, c : c + 1], (NOWN, 128))
            low = ((row & 127) == iota((NOWN, 128), 1)).astype(F32).astype(BF)
            high = ((row >> 7) & 7).astype(F32).astype(BF)
            hots.append(jnp.concatenate([hot_where(high, j, low) for j in range(8)], axis=1))
            uppers.append(row >= half)
        pair = dot(jnp.concatenate(hots, axis=0), both, 1, 0)
        rows = jnp.where(jnp.concatenate(uppers, axis=0), pair[:, 128:], pair[:, :128])
        for i in range(4):
            got[pl.ds(c0 + i, NOWN, stride=CAP), :] = rows[i * NOWN : (i + 1) * NOWN, :]
    out_ref[...] = got[...].astype(BF)


def fetch(req, table):
    return pl.pallas_call(
        fetch_kernel,
        out_shape=jax.ShapeDtypeStruct((SLOTS, 128), BF),
        in_specs=[VM, VM],
        out_specs=VM,
        scratch_shapes=[pltpu.VMEM((SLOTS, 128), F32)],
        compiler_params=PARAMS,
        name="fetch",
    )(req, table)


def column(row_vector):
    wide = jnp.broadcast_to(row_vector.astype(F32), (128, 128))
    return jnp.transpose(wide)


def place_kernel(slot_ref, back_ref, x_ref):
    half = SLOTS // 2
    both = jnp.concatenate([back_ref[:half, :], back_ref[half:, :]], axis=1)
    for b0 in range(0, TOK // 128, 2):
        hots, uppers = [], []
        for b in (b0, b0 + 1):
            slot = column(slot_ref[b : b + 1, :]).astype(I32)
            upper = slot >= half
            slot = jnp.where(upper, slot - half, slot)
            low = ((slot & 127) == iota((128, 128), 1)).astype(F32).astype(BF)
            high = (slot >> 7).astype(F32).astype(BF)
            hots.append(jnp.concatenate([hot_where(high, j, low) for j in range(half // 128)], axis=1))
            uppers.append(upper)
        pair = dot(jnp.concatenate(hots, axis=0), both, 1, 0)
        rows = jnp.where(jnp.concatenate(uppers, axis=0), pair[:, 128:], pair[:, :128])
        x_ref[b0 * 128 : b0 * 128 + 256, :] = rows.astype(BF)


def place(slot, back):
    return pl.pallas_call(
        place_kernel,
        out_shape=jax.ShapeDtypeStruct((TOK, 128), BF),
        in_specs=[VM, VM],
        out_specs=VM,
        compiler_params=PARAMS,
        name="place",
    )(slot, back)


def layer_kernel(
    pos_ref, core_ref, seg_ref, x0, x1, x2, x3, g0, g1, g2, g3, win_ref, wout_ref,
    mine_ref, other_ref, dx0, dx1, dx2, dx3, z0, z1, z2, z3,
    w, wo, pre, act, segc, aw, dsil, dkv, du, u_ref, y_ref, dp_ref, dw_ref,
):
    xs, gs = (x0, x1, x2, x3), (g0, g1, g2, g3)
    dxs, zs = (dx0, dx1, dx2, dx3), (z0, z1, z2, z3)
    me, core = pos_ref[0], core_ref[0]
    for k in range(NT):
        at = pl.multiple_of(lax.rem(me + k, NT) * 128, 128)
        for c in range(4):
            w[k * 128 : (k + 1) * 128, c * 128 : (c + 1) * 128] = win_ref[c, pl.ds(at, 128), :]
        wo[:, k * 128 : (k + 1) * 128] = wout_ref[:, pl.ds(at, 128)]
    for b in range(TOK // 128):
        segc[b * 128 : (b + 1) * 128, :] = column(
            seg_ref[0:1, b * 128 : (b + 1) * 128]
        )

    def stats(r0, n):
        x = [r[r0 : r0 + n, :].astype(F32) for r in xs]
        mean = jnp.sum(x[0] + x[1] + x[2] + x[3], axis=1, keepdims=True) * (1.0 / D)
        x = [v - mean for v in x]
        var = jnp.sum(x[0] * x[0] + x[1] * x[1] + x[2] * x[2] + x[3] * x[3], axis=1, keepdims=True)
        scale = lax.rsqrt(var * (1.0 / D) + 1e-05)
        return [v * scale for v in x], scale

    step = 64
    for q in range(TOK // QB):
        lo = q * QB
        for r0 in range(lo, lo + QB, step):
            n, _ = stats(r0, step)
            for k in range(NT):
                u_ref[r0 : r0 + step, k * 128 : (k + 1) * 128] = n[k].astype(BF)
        pre[lo : lo + QB, :] = dot(u_ref[lo : lo + QB, :], w[...], 1, 0)
        for r0 in range(lo, lo + QB, step):
            p = pre[r0 : r0 + step, :]
            s = 0.5 + 0.5 * jnp.tanh(0.5 * p)
            ps = p * s
            act[r0 : r0 + step, :] = ps.astype(BF)
            pre[r0 : r0 + step, :] = s + ps * (1.0 - s)

    dkv[...] = jnp.zeros((TOK, 256), F32)
    for q in range(TOK // QB):
        lo = q * QB
        k0 = max(0, lo - SEQ_MOST)
        width = lo + QB - k0
        queries = act[lo : lo + QB, 256:384]
        o = jnp.zeros((QB, HD), F32)
        for kb in range(k0, lo + QB, QB):
            sc = dot(queries, act[kb : kb + QB, 384:512], 1, 1) * (HD ** (-0.5))
            for j in range(0, QB, 128):
                same = segc[lo : lo + QB, :] == seg_ref[0:1, kb + j : kb + j + 128].astype(F32)
                if kb == lo:
                    same = same & (iota((QB, 128), 1) + j <= iota((QB, 128), 0))
                v = sc[:, j : j + 128]
                s = 0.5 + 0.5 * jnp.tanh(0.5 * v)
                vs = v * s
                at = kb - k0 + j
                aw[:, at : at + 128] = jnp.where(same, vs * (1.0 / SEQ_MOST), 0.0).astype(BF)
                dsil[:, at : at + 128] = jnp.where(
                    same, (s + vs * (1.0 - s)) * (HD ** (-0.5) / SEQ_MOST), 0.0
                )
        o = dot(aw[:, 0:width], act[k0 : lo + QB, 128:256], 1, 0)
        gate = act[lo : lo + QB, 0:128].astype(F32)
        mean = jnp.sum(o, axis=1, keepdims=True) * (1.0 / HD)
        o = o - mean
        scale = lax.rsqrt(jnp.sum(o * o, axis=1, keepdims=True) * (1.0 / HD) + 1e-05)
        n = o * scale
        y_ref[lo : lo + QB, :] = (n * gate).astype(BF)
        dy = dot(gs[0][lo : lo + QB, :], wo[:, 0:128], 1, 1)
        for k in range(1, NT):
            dy = dy + dot(gs[k][lo : lo + QB, :], wo[:, k * 128 : (k + 1) * 128], 1, 1)
        dy = dy.astype(BF).astype(F32)
        dgate = (dy * n).astype(BF).astype(F32)
        dn = dy * gate
        m1 = jnp.sum(dn, axis=1, keepdims=True) * (1.0 / HD)
        m2 = jnp.sum(dn * n, axis=1, keepdims=True) * (1.0 / HD)
        do = ((dn - m1 - n * m2) * scale).astype(BF)
        dp_ref[lo : lo + QB, 0:128] = (dgate * pre[lo : lo + QB, 0:128]).astype(BF)
        dq = jnp.zeros((QB, HD), F32)
        for kb in range(k0, lo + QB, QB):
            at = kb - k0
            da = dot(do, act[kb : kb + QB, 128:256], 1, 1).astype(BF).astype(F32)
            ds = (da * dsil[:, at : at + QB]).astype(BF)
            dq = dq + dot(ds, act[kb : kb + QB, 384:512], 1, 0)
            dkv[kb : kb + QB, 0:128] += dot(aw[:, at : at + QB], do, 0, 0)
            dkv[kb : kb + QB, 128:256] += dot(ds, queries, 0, 0)
        dq = dq.astype(BF).astype(F32)
        dp_ref[lo : lo + QB, 256:384] = (dq * pre[lo : lo + QB, 256:384]).astype(BF)

    for q in range(TOK // QB):
        lo = q * QB
        dvb = dkv[lo : lo + QB, 0:128].astype(BF).astype(F32)
        dkb = dkv[lo : lo + QB, 128:256].astype(BF).astype(F32)
        dp_ref[lo : lo + QB, 128:256] = (dvb * pre[lo : lo + QB, 128:256]).astype(BF)
        dp_ref[lo : lo + QB, 384:512] = (dkb * pre[lo : lo + QB, 384:512]).astype(BF)
        du[...] = dot(dp_ref[lo : lo + QB, :], w[...], 1, 1).astype(BF).astype(F32)
        for r in range(0, QB, step):
            n, scale = stats(lo + r, step)
            d = [du[r : r + step, k * 128 : (k + 1) * 128] for k in range(NT)]
            m1 = jnp.sum(d[0] + d[1] + d[2] + d[3], axis=1, keepdims=True) * (1.0 / D)
            m2 = jnp.sum(
                d[0] * n[0] + d[1] * n[1] + d[2] * n[2] + d[3] * n[3], axis=1, keepdims=True
            ) * (1.0 / D)
            for k in range(NT):
                dxs[k][lo + r : lo + r + step, :] = ((d[k] - m1 - n[k] * m2) * scale).astype(BF)

    for k in range(NT):
        at = pl.multiple_of(lax.rem(me + k, NT) * 128, 128)
        dw = dot(u_ref[:, k * 128 : (k + 1) * 128], dp_ref[...], 0, 0)
        for c in range(4):
            dw_ref[pl.ds(pl.multiple_of(c * 512 + at, 128), 128), :] = dw[:, c * 128 : (c + 1) * 128]
        dw_ref[pl.ds(pl.multiple_of(2048 + at, 128), 128), :] = dot(y_ref[...], gs[k][...], 0, 0)
        zs[k][...] = dot(y_ref[...], wo[:, k * 128 : (k + 1) * 128], 1, 0).astype(BF)
    mine_ref[...] = dw_ref[pl.ds(pl.multiple_of(core * 1280, 1280), 1280), :]
    other_ref[...] = dw_ref[pl.ds(pl.multiple_of(1280 - core * 1280, 1280), 1280), :].astype(BF)


def layer(pos, core, seg, xs, gs, w_in, w_out):
    piece = jax.ShapeDtypeStruct((TOK, 128), BF)
    return pl.pallas_call(
        layer_kernel,
        out_shape=(jax.ShapeDtypeStruct((1280, 128), F32), jax.ShapeDtypeStruct((1280, 128), BF))
        + (piece,) * 8,
        in_specs=[SM, SM] + [VM] * 11,
        out_specs=(VM,) * 10,
        scratch_shapes=[
            pltpu.VMEM((D, 512), BF),
            pltpu.VMEM((HD, D), BF),
            pltpu.VMEM((TOK, 512), F32),
            pltpu.VMEM((TOK, 512), BF),
            pltpu.VMEM((TOK, 128), F32),
            pltpu.VMEM((QB, 768), BF),
            pltpu.VMEM((QB, 768), F32),
            pltpu.VMEM((TOK, 256), F32),
            pltpu.VMEM((QB, 512), F32),
            pltpu.VMEM((TOK, D), BF),
            pltpu.VMEM((TOK, HD), BF),
            pltpu.VMEM((TOK, 512), BF),
            pltpu.VMEM((2560, 128), F32),
        ],
        compiler_params=PARAMS,
        name="layer",
    )(pos, core, seg, *xs, *gs, w_in, w_out)


def spread(at_ref, blocks, size, values):
    lows, highs, pairs = [], [], []
    for b in range(blocks):
        at = at_ref[b : b + 1, :]
        upper = column((at >= size).astype(F32)) > 0.5
        value = values[b * 128 : (b + 1) * 128, :]
        pairs.append(
            jnp.concatenate([jnp.where(upper, 0.0, value), jnp.where(upper, value, 0.0)], axis=1).astype(BF)
        )
        at = jnp.broadcast_to(jnp.where(at >= size, at - size, at), (128, 128))
        lows.append(((at & 127) == iota((128, 128), 0)).astype(F32).astype(BF))
        highs.append((at >> 7).astype(F32).astype(BF))
    low = jnp.concatenate(lows, axis=1)
    high = jnp.concatenate(highs, axis=1)
    pair = jnp.concatenate(pairs, axis=0)
    return [dot(hot_where(high, s, low), pair, 1, 0) for s in range(size // 128)]


def slots_kernel(slot_ref, grad_ref, d0, d1, d2, d3, out_ref):
    dx = grad_ref[...].astype(F32) + (
        d0[...].astype(F32) + d1[...].astype(F32) + d2[...].astype(F32) + d3[...].astype(F32)
    )
    half = SLOTS // 2
    for s, both in enumerate(spread(slot_ref, TOK // 128, half, dx)):
        out_ref[s * 128 : (s + 1) * 128, :] = both[:, :128].astype(BF)
        out_ref[half + s * 128 : half + (s + 1) * 128, :] = both[:, 128:].astype(BF)


def to_slots(slot, grad, parts):
    return pl.pallas_call(
        slots_kernel,
        out_shape=jax.ShapeDtypeStruct((SLOTS, 128), BF),
        in_specs=[VM] * 6,
        out_specs=VM,
        compiler_params=PARAMS,
        name="to_slots",
    )(slot, grad, *parts)


def add_rows_kernel(req_ref, arrived_ref, out_ref):
    half = ROWS // 2
    for s, both in enumerate(spread(req_ref, SLOTS // 128, half, arrived_ref[...].astype(F32))):
        out_ref[s * 128 : (s + 1) * 128, :] = both[:, :128]
        out_ref[half + s * 128 : half + (s + 1) * 128, :] = both[:, 128:]


def add_rows(req, arrived):
    return pl.pallas_call(
        add_rows_kernel,
        out_shape=jax.ShapeDtypeStruct((ROWS, 128), F32),
        in_specs=[VM, VM],
        out_specs=VM,
        compiler_params=PARAMS,
        name="add_rows",
    )(req, arrived)


def unpack_kernel(y_ref, p0, p1, p2, p3, in_ref, out_ref, whole):
    for k, p in enumerate((p0, p1, p2, p3)):
        half, quarter = y_place(lax.rem(y_ref[0] + k, 4))
        for core in range(2):
            at = pl.multiple_of(half * 640 + quarter * 320 + core * 1280, 320)
            whole[pl.ds(at, 320), :] = p[core * 320 : (core + 1) * 320, :].astype(F32)
    in_ref[...] = whole[0:2048, :]
    for k in range(NT):
        out_ref[:, k * 128 : (k + 1) * 128] = whole[2048 + k * 128 : 2176 + k * 128, :]


def unpack(y, parts):
    return pl.pallas_call(
        unpack_kernel,
        out_shape=(jax.ShapeDtypeStruct((2048, 128), F32), jax.ShapeDtypeStruct((HD, D), F32)),
        in_specs=[SM] + [VM] * 4,
        out_specs=(VM, VM),
        scratch_shapes=[pltpu.VMEM((2560, 128), F32)],
        compiler_params=PARAMS,
        name="unpack",
    )(y, *parts)


def shift(x, axis, fn, n):
    return lax.ppermute(x, axis, [(i, fn(i)) for i in range(n)])


def gather_pieces(x):
    return [x] + [shift(x, "tensor", lambda i, k=k: (i - k) % NT, NT) for k in (1, 3, 2)]


def order(pieces):
    own, one, three, two = pieces
    return [own, one, two, three]


def scatter_pieces(parts):
    return [parts[0]] + [shift(parts[k], "tensor", lambda i, k=k: (i + k) % NT, NT) for k in (1, 3, 2)]


def pick(x, i):
    return lax.dynamic_index_in_dim(x, i, 0, keepdims=False)


def y_place(y):
    return ((y == 1) | (y == 2)).astype(I32), (y >= 2).astype(I32)


def reduce_over_chips(mine, other):
    half, quarter = y_place(lax.axis_index("table") // 2)
    other = shift(other, "table", lambda i: i ^ 1, 8)
    mine = (mine + other.astype(F32)).reshape(2, 640, 128)
    got = shift(pick(mine, 1 - half).astype(BF), "table", lambda i: i ^ 2, 8)
    mine = (pick(mine, half) + got.astype(F32)).reshape(2, 320, 128)
    got = shift(pick(mine, 1 - quarter).astype(BF), "table", lambda i: 6 - (i & 6) + (i & 1), 8)
    return pick(mine, quarter), got


def add_step(total, mask):
    return (total.astype(F32) + shift(total, "seq", lambda i: i ^ mask, 8).astype(F32)).astype(BF)


def gather_weights(total):
    y = (lax.axis_index("table") // 2).astype(I32).reshape(1)
    pairs = [[2 * i, 2 * i + 1] for i in range(4)]
    both = lax.all_gather(total, "table", axis=0, tiled=True, axis_index_groups=pairs)
    parts = [both] + [shift(both, "table", lambda i, k=k: (i - 2 * k) % 8, 8) for k in range(1, 4)]
    return unpack(y, parts)


def body(table, owner, local_row, segment_ids, proj_in, proj_out, grad_out):
    pos = lax.axis_index("tensor").astype(I32).reshape(1)
    core = (lax.axis_index("table") % 2).astype(I32).reshape(1)
    requests, slot = route(owner.reshape(8, 128), local_row.reshape(8, 128))
    gs = order(gather_pieces(grad_out))
    received = lax.all_to_all(requests, BOTH, split_axis=0, concat_axis=0, tiled=True)
    rows = fetch(received, table)
    back = lax.all_to_all(rows.reshape(NOWN, CAP, 128), BOTH, split_axis=0, concat_axis=0, tiled=True)
    x = place(slot, back.reshape(SLOTS, 128))
    xs = order(gather_pieces(x))
    mine, other, d0, d1, d2, d3, z0, z1, z2, z3 = layer(
        pos, core, segment_ids, xs, gs, proj_in, proj_out
    )
    dparts = scatter_pieces([d0, d1, d2, d3])
    own, got = reduce_over_chips(mine, other)
    flat = received[:, :CAP].reshape(SLOTS // 128, 128)
    dparts, got, flat = lax.optimization_barrier((dparts, got, flat))
    grads = to_slots(slot, grad_out, dparts)
    total = add_step((own + got.astype(F32)).astype(BF), 1)
    total = add_step(add_step(total, 2), 7)
    grads, total, zs = lax.optimization_barrier((grads, total, [z0, z1, z2, z3]))
    arrived = lax.all_to_all(grads.reshape(NOWN, CAP, 128), BOTH, split_axis=0, concat_axis=0, tiled=True)
    grad_in, grad_outw = gather_weights(total)
    zparts = scatter_pieces(zs)
    arrived, zparts = lax.optimization_barrier((arrived, zparts))
    table_grad = add_rows(flat, arrived.reshape(SLOTS, 128))
    layer_out = (
        x.astype(F32)
        + (zparts[0].astype(F32) + zparts[1].astype(F32) + zparts[2].astype(F32) + zparts[3].astype(F32))
    ).astype(BF)
    return layer_out, table_grad, grad_in.reshape(4, D, 128), grad_outw


def solution(mesh):
    in_specs = (
        P(BOTH, "tensor"),
        P(BOTH, None),
        P(BOTH),
        P(BOTH, None),
        P(None, None, "tensor"),
        P("tensor", None),
        P(BOTH, "tensor"),
    )
    out_specs = (
        P(BOTH, "tensor"),
        P(BOTH, "tensor"),
        P(None, None, "tensor"),
        P("tensor", None),
    )
    return jax.shard_map(body, mesh=mesh, in_specs=in_specs, out_specs=out_specs, check_vma=False)
```

```python
import functools

import jax
import jax.numpy as jnp
from jax import lax
from jax.experimental import pallas as pl
from jax.experimental.pallas import tpu as pltpu
from jax.sharding import PartitionSpec as P

HD = 128
SEQ_MOST = 512
TOK = 1024
D = 512
NT = 4
NOWN = 64
CAP = 24
SLOTS = NOWN * CAP
ROWS = 2048
QB = 256
BOTH = ("table", "seq")
BF = jnp.bfloat16
F32 = jnp.float32
I32 = jnp.int32
VM = pl.BlockSpec(memory_space=pltpu.VMEM)
SM = pl.BlockSpec(memory_space=pltpu.SMEM)
PARAMS = pltpu.CompilerParams(vmem_limit_bytes=56 * 1024 * 1024)


def iota(shape, dim):
    return lax.broadcasted_iota(I32, shape, dim)


def dot(a, b, ca, cb):
    return lax.dot_general(a, b, (((ca,), (cb,)), ((), ())), preferred_element_type=F32)


def route_kernel(owner_ref, row_ref, req_ref, slot_ref):
    blocks = TOK // 128
    upper = (iota((128, 128), 0) < iota((128, 128), 1)).astype(BF)
    scan = jnp.concatenate([upper, jnp.ones((128, 128), BF)], axis=1)
    hots = [(iota((NOWN, 128), 0) == owner_ref[b : b + 1, :]).astype(F32) for b in range(blocks)]
    sums = dot(jnp.concatenate(hots, axis=0).astype(BF), scan, 1, 0)
    carry = jnp.zeros((NOWN, 128), F32)
    highs, lows = [], []
    for b in range(blocks):
        part = sums[b * NOWN : (b + 1) * NOWN, :]
        rank = jnp.sum(hots[b] * (part[:, :128] + carry), axis=0, keepdims=True).astype(I32)
        carry = carry + part[:, 128:]
        row = row_ref[b : b + 1, :]
        slot_ref[b : b + 1, :] = owner_ref[b : b + 1, :] * CAP + rank
        here = iota((32, 128), 0) == rank
        highs.append(jnp.where(here, (row >> 6).astype(F32), 0.0))
        lows.append(jnp.where(here, (row & 63).astype(F32), 0.0))
    hot = jnp.concatenate(hots, axis=1).astype(BF)
    high = dot(hot, jnp.concatenate(highs, axis=1).astype(BF), 1, 1)
    low = dot(hot, jnp.concatenate(lows, axis=1).astype(BF), 1, 1)
    req_ref[...] = jnp.zeros((NOWN, 128), I32)
    req_ref[:, 0:32] = (high * 64.0 + low).astype(I32)


def route(owner, row):
    return pl.pallas_call(
        route_kernel,
        out_shape=(
            jax.ShapeDtypeStruct((NOWN, 128), I32),
            jax.ShapeDtypeStruct((TOK // 128, 128), I32),
        ),
        in_specs=[VM, VM],
        out_specs=(VM, VM),
        compiler_params=PARAMS,
        name="route",
    )(owner, row)


def hot_where(high, value, low_hot):
    return jnp.where(high == value, low_hot, jnp.zeros_like(low_hot))


def fetch_kernel(req_ref, table_ref, out_ref, got):
    half = ROWS // 2
    both = jnp.concatenate([table_ref[:half, :], table_ref[half:, :]], axis=1)
    for c0 in range(0, CAP, 4):
        hots, uppers = [], []
        for c in range(c0, c0 + 4):
            row = jnp.broadcast_to(req_ref[:, c : c + 1], (NOWN, 128))
            low = ((row & 127) == iota((NOWN, 128), 1)).astype(F32).astype(BF)
            high = ((row >> 7) & 7).astype(F32).astype(BF)
            hots.append(jnp.concatenate([hot_where(high, j, low) for j in range(8)], axis=1))
            uppers.append(row >= half)
        pair = dot(jnp.concatenate(hots, axis=0), both, 1, 0)
        rows = jnp.where(jnp.concatenate(uppers, axis=0), pair[:, 128:], pair[:, :128])
        for i in range(4):
            got[pl.ds(c0 + i, NOWN, stride=CAP), :] = rows[i * NOWN : (i + 1) * NOWN, :]
    out_ref[...] = got[...].astype(BF)


def fetch(req, table):
    return pl.pallas_call(
        fetch_kernel,
        out_shape=jax.ShapeDtypeStruct((SLOTS, 128), BF),
        in_specs=[VM, VM],
        out_specs=VM,
        scratch_shapes=[pltpu.VMEM((SLOTS, 128), F32)],
        compiler_params=PARAMS,
        name="fetch",
    )(req, table)


def column(row_vector):
    wide = jnp.broadcast_to(row_vector.astype(F32), (128, 128))
    return jnp.transpose(wide)


def place_kernel(slot_ref, back_ref, x_ref):
    half = SLOTS // 2
    both = jnp.concatenate([back_ref[:half, :], back_ref[half:, :]], axis=1)
    for b0 in range(0, TOK // 128, 2):
        hots, uppers = [], []
        for b in (b0, b0 + 1):
            slot = column(slot_ref[b : b + 1, :]).astype(I32)
            upper = slot >= half
            slot = jnp.where(upper, slot - half, slot)
            low = ((slot & 127) == iota((128, 128), 1)).astype(F32).astype(BF)
            high = (slot >> 7).astype(F32).astype(BF)
            hots.append(jnp.concatenate([hot_where(high, j, low) for j in range(half // 128)], axis=1))
            uppers.append(upper)
        pair = dot(jnp.concatenate(hots, axis=0), both, 1, 0)
        rows = jnp.where(jnp.concatenate(uppers, axis=0), pair[:, 128:], pair[:, :128])
        x_ref[b0 * 128 : b0 * 128 + 256, :] = rows.astype(BF)


def place(slot, back):
    return pl.pallas_call(
        place_kernel,
        out_shape=jax.ShapeDtypeStruct((TOK, 128), BF),
        in_specs=[VM, VM],
        out_specs=VM,
        compiler_params=PARAMS,
        name="place",
    )(slot, back)


def layer_kernel(
    pos_ref, core_ref, seg_ref, x0, x1, x2, x3, g0, g1, g2, g3, win_ref, wout_ref,
    mine_ref, other_ref, own_ref, right_ref, left_ref, near_right, near_left,
    w, wo, pre, act, segc, aw, dsil, dkv, du, u_ref, y_ref, dp_ref, dw_ref,
):
    xs, gs = (x0, x1, x2, x3), (g0, g1, g2, g3)
    me, core = pos_ref[0], core_ref[0]

    def keep(k, kind, row, value):
        late = row >= TOK // 2
        at = kind * (TOK // 2) + row % (TOK // 2)
        if k == 0:
            ref, at = own_ref, at + (TOK if late else 0)
        elif k == 1:
            ref, at = (right_ref, at + TOK) if late else (near_right, at)
        elif k == 2:
            ref = left_ref if late else right_ref
        else:
            ref, at = (near_left, at) if late else (left_ref, at + TOK)
        ref[at : at + value.shape[0], :] = value.astype(BF)

    for k in range(NT):
        at = pl.multiple_of(lax.rem(me + k, NT) * 128, 128)
        for c in range(4):
            w[k * 128 : (k + 1) * 128, c * 128 : (c + 1) * 128] = win_ref[c, pl.ds(at, 128), :]
        wo[:, k * 128 : (k + 1) * 128] = wout_ref[:, pl.ds(at, 128)]
    for b in range(TOK // 128):
        segc[b * 128 : (b + 1) * 128, :] = column(
            seg_ref[0:1, b * 128 : (b + 1) * 128]
        )

    def stats(r0, n):
        x = [r[r0 : r0 + n, :].astype(F32) for r in xs]
        mean = jnp.sum(x[0] + x[1] + x[2] + x[3], axis=1, keepdims=True) * (1.0 / D)
        x = [v - mean for v in x]
        var = jnp.sum(x[0] * x[0] + x[1] * x[1] + x[2] * x[2] + x[3] * x[3], axis=1, keepdims=True)
        scale = lax.rsqrt(var * (1.0 / D) + 1e-05)
        return [v * scale for v in x], scale

    step = 64
    for q in range(TOK // QB):
        lo = q * QB
        for r0 in range(lo, lo + QB, step):
            n, _ = stats(r0, step)
            for k in range(NT):
                u_ref[r0 : r0 + step, k * 128 : (k + 1) * 128] = n[k].astype(BF)
        pre[lo : lo + QB, :] = dot(u_ref[lo : lo + QB, :], w[...], 1, 0)
        for r0 in range(lo, lo + QB, step):
            p = pre[r0 : r0 + step, :]
            s = 0.5 + 0.5 * jnp.tanh(0.5 * p)
            ps = p * s
            act[r0 : r0 + step, :] = ps.astype(BF)
            pre[r0 : r0 + step, :] = s + ps * (1.0 - s)

    dkv[...] = jnp.zeros((TOK, 256), F32)
    for q in range(TOK // QB):
        lo = q * QB
        k0 = max(0, lo - SEQ_MOST)
        width = lo + QB - k0
        queries = act[lo : lo + QB, 256:384]
        o = jnp.zeros((QB, HD), F32)
        for kb in range(k0, lo + QB, QB):
            sc = dot(queries, act[kb : kb + QB, 384:512], 1, 1) * (HD ** (-0.5))
            for j in range(0, QB, 128):
                same = segc[lo : lo + QB, :] == seg_ref[0:1, kb + j : kb + j + 128].astype(F32)
                if kb == lo:
                    same = same & (iota((QB, 128), 1) + j <= iota((QB, 128), 0))
                v = sc[:, j : j + 128]
                s = 0.5 + 0.5 * jnp.tanh(0.5 * v)
                vs = v * s
                at = kb - k0 + j
                aw[:, at : at + 128] = jnp.where(same, vs * (1.0 / SEQ_MOST), 0.0).astype(BF)
                dsil[:, at : at + 128] = jnp.where(
                    same, (s + vs * (1.0 - s)) * (HD ** (-0.5) / SEQ_MOST), 0.0
                )
        o = dot(aw[:, 0:width], act[k0 : lo + QB, 128:256], 1, 0)
        gate = act[lo : lo + QB, 0:128].astype(F32)
        mean = jnp.sum(o, axis=1, keepdims=True) * (1.0 / HD)
        o = o - mean
        scale = lax.rsqrt(jnp.sum(o * o, axis=1, keepdims=True) * (1.0 / HD) + 1e-05)
        n = o * scale
        y_ref[lo : lo + QB, :] = (n * gate).astype(BF)
        dy = dot(gs[0][lo : lo + QB, :], wo[:, 0:128], 1, 1)
        for k in range(1, NT):
            dy = dy + dot(gs[k][lo : lo + QB, :], wo[:, k * 128 : (k + 1) * 128], 1, 1)
        dy = dy.astype(BF).astype(F32)
        dgate = (dy * n).astype(BF).astype(F32)
        dn = dy * gate
        m1 = jnp.sum(dn, axis=1, keepdims=True) * (1.0 / HD)
        m2 = jnp.sum(dn * n, axis=1, keepdims=True) * (1.0 / HD)
        do = ((dn - m1 - n * m2) * scale).astype(BF)
        dp_ref[lo : lo + QB, 0:128] = (dgate * pre[lo : lo + QB, 0:128]).astype(BF)
        dq = jnp.zeros((QB, HD), F32)
        for kb in range(k0, lo + QB, QB):
            at = kb - k0
            da = dot(do, act[kb : kb + QB, 128:256], 1, 1).astype(BF).astype(F32)
            ds = (da * dsil[:, at : at + QB]).astype(BF)
            dq = dq + dot(ds, act[kb : kb + QB, 384:512], 1, 0)
            dkv[kb : kb + QB, 0:128] += dot(aw[:, at : at + QB], do, 0, 0)
            dkv[kb : kb + QB, 128:256] += dot(ds, queries, 0, 0)
        dq = dq.astype(BF).astype(F32)
        dp_ref[lo : lo + QB, 256:384] = (dq * pre[lo : lo + QB, 256:384]).astype(BF)

    for q in range(TOK // QB):
        lo = q * QB
        dvb = dkv[lo : lo + QB, 0:128].astype(BF).astype(F32)
        dkb = dkv[lo : lo + QB, 128:256].astype(BF).astype(F32)
        dp_ref[lo : lo + QB, 128:256] = (dvb * pre[lo : lo + QB, 128:256]).astype(BF)
        dp_ref[lo : lo + QB, 384:512] = (dkb * pre[lo : lo + QB, 384:512]).astype(BF)
        du[...] = dot(dp_ref[lo : lo + QB, :], w[...], 1, 1).astype(BF).astype(F32)
        for r in range(0, QB, step):
            n, scale = stats(lo + r, step)
            d = [du[r : r + step, k * 128 : (k + 1) * 128] for k in range(NT)]
            m1 = jnp.sum(d[0] + d[1] + d[2] + d[3], axis=1, keepdims=True) * (1.0 / D)
            m2 = jnp.sum(
                d[0] * n[0] + d[1] * n[1] + d[2] * n[2] + d[3] * n[3], axis=1, keepdims=True
            ) * (1.0 / D)
            for k in range(NT):
                keep(k, 0, lo + r, (d[k] - m1 - n[k] * m2) * scale)

    for k in range(NT):
        at = pl.multiple_of(lax.rem(me + k, NT) * 128, 128)
        dw = dot(u_ref[:, k * 128 : (k + 1) * 128], dp_ref[...], 0, 0)
        for c in range(4):
            dw_ref[pl.ds(pl.multiple_of(c * 512 + at, 128), 128), :] = dw[:, c * 128 : (c + 1) * 128]
        dw_ref[pl.ds(pl.multiple_of(2048 + at, 128), 128), :] = dot(y_ref[...], gs[k][...], 0, 0)
        for row in (0, TOK // 2):
            keep(k, 1, row, dot(y_ref[row : row + TOK // 2, :], wo[:, k * 128 : (k + 1) * 128], 1, 0))
    mine_ref[...] = dw_ref[pl.ds(pl.multiple_of(core * 1280, 1280), 1280), :]
    other_ref[...] = dw_ref[pl.ds(pl.multiple_of(1280 - core * 1280, 1280), 1280), :].astype(BF)


def layer(pos, core, seg, xs, gs, w_in, w_out):
    piece = jax.ShapeDtypeStruct((TOK, 128), BF)
    pair = jax.ShapeDtypeStruct((2 * TOK, 128), BF)
    return pl.pallas_call(
        layer_kernel,
        out_shape=(jax.ShapeDtypeStruct((1280, 128), F32), jax.ShapeDtypeStruct((1280, 128), BF))
        + (pair,) * 3
        + (piece,) * 2,
        in_specs=[SM, SM] + [VM] * 11,
        out_specs=(VM,) * 7,
        scratch_shapes=[
            pltpu.VMEM((D, 512), BF),
            pltpu.VMEM((HD, D), BF),
            pltpu.VMEM((TOK, 512), F32),
            pltpu.VMEM((TOK, 512), BF),
            pltpu.VMEM((TOK, 128), F32),
            pltpu.VMEM((QB, 768), BF),
            pltpu.VMEM((QB, 768), F32),
            pltpu.VMEM((TOK, 256), F32),
            pltpu.VMEM((QB, 512), F32),
            pltpu.VMEM((TOK, D), BF),
            pltpu.VMEM((TOK, HD), BF),
            pltpu.VMEM((TOK, 512), BF),
            pltpu.VMEM((2560, 128), F32),
        ],
        compiler_params=PARAMS,
        name="layer",
    )(pos, core, seg, *xs, *gs, w_in, w_out)


def spread(at_ref, blocks, size, values):
    lows, highs, pairs = [], [], []
    for b in range(blocks):
        at = at_ref[b : b + 1, :]
        upper = column((at >= size).astype(F32)) > 0.5
        value = values[b * 128 : (b + 1) * 128, :]
        pairs.append(
            jnp.concatenate([jnp.where(upper, 0.0, value), jnp.where(upper, value, 0.0)], axis=1).astype(BF)
        )
        at = jnp.broadcast_to(jnp.where(at >= size, at - size, at), (128, 128))
        lows.append(((at & 127) == iota((128, 128), 0)).astype(F32).astype(BF))
        highs.append((at >> 7).astype(F32).astype(BF))
    low = jnp.concatenate(lows, axis=1)
    high = jnp.concatenate(highs, axis=1)
    pair = jnp.concatenate(pairs, axis=0)
    return [dot(hot_where(high, s, low), pair, 1, 0) for s in range(size // 128)]


def summed(first, kind, own, from_left, from_right, via_left, via_right):
    half = TOK // 2
    at = kind * half
    early = own[at : at + half, :].astype(F32) + (
        via_left[at : at + half, :].astype(F32) + from_right[TOK + at : TOK + at + half, :].astype(F32)
    )
    late = own[TOK + at : TOK + at + half, :].astype(F32) + (
        via_right[at : at + half, :].astype(F32) + from_left[TOK + at : TOK + at + half, :].astype(F32)
    )
    return first.astype(F32) + jnp.concatenate([early, late], axis=0)


def slots_kernel(slot_ref, grad_ref, own, from_left, from_right, via_left, via_right, out_ref):
    dx = summed(
        grad_ref[...], 0, own[...], from_left[...], from_right[...], via_left[...], via_right[...]
    )
    half = SLOTS // 2
    for s, both in enumerate(spread(slot_ref, TOK // 128, half, dx)):
        out_ref[s * 128 : (s + 1) * 128, :] = both[:, :128].astype(BF)
        out_ref[half + s * 128 : half + (s + 1) * 128, :] = both[:, 128:].astype(BF)


def to_slots(slot, grad, parts):
    return pl.pallas_call(
        slots_kernel,
        out_shape=jax.ShapeDtypeStruct((SLOTS, 128), BF),
        in_specs=[VM] * 7,
        out_specs=VM,
        compiler_params=PARAMS,
        name="to_slots",
    )(slot, grad, *parts)


def add_rows_kernel(req_ref, arrived_ref, out_ref):
    half = ROWS // 2
    for s, both in enumerate(spread(req_ref, SLOTS // 128, half, arrived_ref[...].astype(F32))):
        out_ref[s * 128 : (s + 1) * 128, :] = both[:, :128]
        out_ref[half + s * 128 : half + (s + 1) * 128, :] = both[:, 128:]


def add_rows(req, arrived):
    return pl.pallas_call(
        add_rows_kernel,
        out_shape=jax.ShapeDtypeStruct((ROWS, 128), F32),
        in_specs=[VM, VM],
        out_specs=VM,
        compiler_params=PARAMS,
        name="add_rows",
    )(req, arrived)


def unpack_kernel(y_ref, p0, p1, p2, p3, in_ref, out_ref, whole):
    for k, p in enumerate((p0, p1, p2, p3)):
        half, quarter = y_place(lax.rem(y_ref[0] + k, 4))
        for core in range(2):
            at = pl.multiple_of(half * 640 + quarter * 320 + core * 1280, 320)
            whole[pl.ds(at, 320), :] = p[core * 320 : (core + 1) * 320, :].astype(F32)
    in_ref[...] = whole[0:2048, :]
    for k in range(NT):
        out_ref[:, k * 128 : (k + 1) * 128] = whole[2048 + k * 128 : 2176 + k * 128, :]


def unpack(y, parts):
    return pl.pallas_call(
        unpack_kernel,
        out_shape=(jax.ShapeDtypeStruct((2048, 128), F32), jax.ShapeDtypeStruct((HD, D), F32)),
        in_specs=[SM] + [VM] * 4,
        out_specs=(VM, VM),
        scratch_shapes=[pltpu.VMEM((2560, 128), F32)],
        compiler_params=PARAMS,
        name="unpack",
    )(y, *parts)


def shift(x, axis, fn, n):
    return lax.ppermute(x, axis, [(i, fn(i)) for i in range(n)])


def gather_pieces(x):
    return [x] + [shift(x, "tensor", lambda i, k=k: (i - k) % NT, NT) for k in (1, 3, 2)]


def order(pieces):
    own, one, three, two = pieces
    return [own, one, two, three]


def to_right(x):
    return shift(x, "tensor", lambda i: (i + 1) % NT, NT)


def to_left(x):
    return shift(x, "tensor", lambda i: (i - 1) % NT, NT)


def pick(x, i):
    return lax.dynamic_index_in_dim(x, i, 0, keepdims=False)


def y_place(y):
    return ((y == 1) | (y == 2)).astype(I32), (y >= 2).astype(I32)


def reduce_over_chips(mine, other):
    half, quarter = y_place(lax.axis_index("table") // 2)
    other = shift(other, "table", lambda i: i ^ 1, 8)
    mine = (mine + other.astype(F32)).reshape(2, 640, 128)
    got = shift(pick(mine, 1 - half).astype(BF), "table", lambda i: i ^ 2, 8)
    mine = (pick(mine, half) + got.astype(F32)).reshape(2, 320, 128)
    got = shift(pick(mine, 1 - quarter).astype(BF), "table", lambda i: 6 - (i & 6) + (i & 1), 8)
    return pick(mine, quarter), got


def add_step(total, mask):
    return (total.astype(F32) + shift(total, "seq", lambda i: i ^ mask, 8).astype(F32)).astype(BF)


def gather_weights(total):
    y = (lax.axis_index("table") // 2).astype(I32).reshape(1)
    pairs = [[2 * i, 2 * i + 1] for i in range(4)]
    both = lax.all_gather(total, "table", axis=0, tiled=True, axis_index_groups=pairs)
    parts = [both] + [shift(both, "table", lambda i, k=k: (i - 2 * k) % 8, 8) for k in range(1, 4)]
    return unpack(y, parts)


def body(table, owner, local_row, segment_ids, proj_in, proj_out, grad_out):
    pos = lax.axis_index("tensor").astype(I32).reshape(1)
    core = (lax.axis_index("table") % 2).astype(I32).reshape(1)
    requests, slot = route(owner.reshape(8, 128), local_row.reshape(8, 128))
    gs = order(gather_pieces(grad_out))
    received = lax.all_to_all(requests, BOTH, split_axis=0, concat_axis=0, tiled=True)
    rows = fetch(received, table)
    back = lax.all_to_all(rows.reshape(NOWN, CAP, 128), BOTH, split_axis=0, concat_axis=0, tiled=True)
    x = place(slot, back.reshape(SLOTS, 128))
    xs = order(gather_pieces(x))
    mine, other, own, right, left, near_right, near_left = layer(
        pos, core, segment_ids, xs, gs, proj_in, proj_out
    )
    from_left, from_right = to_right(right), to_left(left)
    kept, got = reduce_over_chips(mine, other)
    flat = received[:, :CAP].reshape(SLOTS // 128, 128)
    from_left, from_right, got, flat = lax.optimization_barrier((from_left, from_right, got, flat))
    via_left = to_right((near_right.astype(F32) + from_left[:TOK].astype(F32)).astype(BF))
    via_right = to_left((near_left.astype(F32) + from_right[:TOK].astype(F32)).astype(BF))
    total = add_step((kept + got.astype(F32)).astype(BF), 1)
    total = add_step(total, 2)
    via_left, via_right, total = lax.optimization_barrier((via_left, via_right, total))
    parts = [own, from_left, from_right, via_left, via_right]
    grads = to_slots(slot, grad_out, parts)
    total = add_step(total, 7)
    grads, total = lax.optimization_barrier((grads, total))
    arrived = lax.all_to_all(grads.reshape(NOWN, CAP, 128), BOTH, split_axis=0, concat_axis=0, tiled=True)
    grad_in, grad_outw = gather_weights(total)
    layer_out = summed(x, 1, *parts).astype(BF)
    table_grad = add_rows(flat, arrived.reshape(SLOTS, 128))
    return layer_out, table_grad, grad_in.reshape(4, D, 128), grad_outw


def solution(mesh):
    in_specs = (
        P(BOTH, "tensor"),
        P(BOTH, None),
        P(BOTH),
        P(BOTH, None),
        P(None, None, "tensor"),
        P("tensor", None),
        P(BOTH, "tensor"),
    )
    out_specs = (
        P(BOTH, "tensor"),
        P(BOTH, "tensor"),
        P(None, None, "tensor"),
        P("tensor", None),
    )
    return jax.shard_map(body, mesh=mesh, in_specs=in_specs, out_specs=out_specs, check_vma=False)
```

```python
import functools

import jax
import jax.numpy as jnp
from jax import lax
from jax.experimental import pallas as pl
from jax.experimental.pallas import tpu as pltpu
from jax.sharding import PartitionSpec as P

HD = 128
SEQ_MOST = 512
TOK = 1024
D = 512
NT = 4
NOWN = 64
CAP = 24
SLOTS = NOWN * CAP
ROWS = 2048
QB = 256
BOTH = ("table", "seq")
BF = jnp.bfloat16
F32 = jnp.float32
I32 = jnp.int32
VM = pl.BlockSpec(memory_space=pltpu.VMEM)
SM = pl.BlockSpec(memory_space=pltpu.SMEM)
PARAMS = pltpu.CompilerParams(vmem_limit_bytes=56 * 1024 * 1024)


def iota(shape, dim):
    return lax.broadcasted_iota(I32, shape, dim)


def dot(a, b, ca, cb):
    return lax.dot_general(a, b, (((ca,), (cb,)), ((), ())), preferred_element_type=F32)


def route_kernel(owner_ref, row_ref, req_ref, slot_ref):
    blocks = TOK // 128
    upper = (iota((128, 128), 0) < iota((128, 128), 1)).astype(BF)
    scan = jnp.concatenate([upper, jnp.ones((128, 128), BF)], axis=1)
    hots = [(iota((NOWN, 128), 0) == owner_ref[b : b + 1, :]).astype(F32) for b in range(blocks)]
    sums = dot(jnp.concatenate(hots, axis=0).astype(BF), scan, 1, 0)
    carry = jnp.zeros((NOWN, 128), F32)
    highs, lows = [], []
    for b in range(blocks):
        part = sums[b * NOWN : (b + 1) * NOWN, :]
        rank = jnp.sum(hots[b] * (part[:, :128] + carry), axis=0, keepdims=True).astype(I32)
        carry = carry + part[:, 128:]
        row = row_ref[b : b + 1, :]
        slot_ref[b : b + 1, :] = owner_ref[b : b + 1, :] * CAP + rank
        here = iota((32, 128), 0) == rank
        highs.append(jnp.where(here, (row >> 6).astype(F32), 0.0))
        lows.append(jnp.where(here, (row & 63).astype(F32), 0.0))
    hot = jnp.concatenate(hots, axis=1).astype(BF)
    high = dot(hot, jnp.concatenate(highs, axis=1).astype(BF), 1, 1)
    low = dot(hot, jnp.concatenate(lows, axis=1).astype(BF), 1, 1)
    req_ref[...] = jnp.zeros((NOWN, 128), I32)
    req_ref[:, 0:32] = (high * 64.0 + low).astype(I32)


def route(owner, row):
    return pl.pallas_call(
        route_kernel,
        out_shape=(
            jax.ShapeDtypeStruct((NOWN, 128), I32),
            jax.ShapeDtypeStruct((TOK // 128, 128), I32),
        ),
        in_specs=[VM, VM],
        out_specs=(VM, VM),
        compiler_params=PARAMS,
        name="route",
    )(owner, row)


def hot_where(high, value, low_hot):
    return jnp.where(high == value, low_hot, jnp.zeros_like(low_hot))


def fetch_kernel(req_ref, table_ref, out_ref, got):
    half = ROWS // 2
    both = jnp.concatenate([table_ref[:half, :], table_ref[half:, :]], axis=1)
    for c0 in range(0, CAP, 4):
        hots, uppers = [], []
        for c in range(c0, c0 + 4):
            row = jnp.broadcast_to(req_ref[:, c : c + 1], (NOWN, 128))
            low = ((row & 127) == iota((NOWN, 128), 1)).astype(F32).astype(BF)
            high = ((row >> 7) & 7).astype(F32).astype(BF)
            hots.append(jnp.concatenate([hot_where(high, j, low) for j in range(8)], axis=1))
            uppers.append(row >= half)
        pair = dot(jnp.concatenate(hots, axis=0), both, 1, 0)
        rows = jnp.where(jnp.concatenate(uppers, axis=0), pair[:, 128:], pair[:, :128])
        for i in range(4):
            got[pl.ds(c0 + i, NOWN, stride=CAP), :] = rows[i * NOWN : (i + 1) * NOWN, :]
    out_ref[...] = got[...].astype(BF)


def fetch(req, table):
    return pl.pallas_call(
        fetch_kernel,
        out_shape=jax.ShapeDtypeStruct((SLOTS, 128), BF),
        in_specs=[VM, VM],
        out_specs=VM,
        scratch_shapes=[pltpu.VMEM((SLOTS, 128), F32)],
        compiler_params=PARAMS,
        name="fetch",
    )(req, table)


def column(row_vector):
    wide = jnp.broadcast_to(row_vector.astype(F32), (128, 128))
    return jnp.transpose(wide)


def place_kernel(slot_ref, back_ref, x_ref):
    half = SLOTS // 2
    both = jnp.concatenate([back_ref[:half, :], back_ref[half:, :]], axis=1)
    for b0 in range(0, TOK // 128, 2):
        hots, uppers = [], []
        for b in (b0, b0 + 1):
            slot = column(slot_ref[b : b + 1, :]).astype(I32)
            upper = slot >= half
            slot = jnp.where(upper, slot - half, slot)
            low = ((slot & 127) == iota((128, 128), 1)).astype(F32).astype(BF)
            high = (slot >> 7).astype(F32).astype(BF)
            hots.append(jnp.concatenate([hot_where(high, j, low) for j in range(half // 128)], axis=1))
            uppers.append(upper)
        pair = dot(jnp.concatenate(hots, axis=0), both, 1, 0)
        rows = jnp.where(jnp.concatenate(uppers, axis=0), pair[:, 128:], pair[:, :128])
        x_ref[b0 * 128 : b0 * 128 + 256, :] = rows.astype(BF)


def place(slot, back):
    return pl.pallas_call(
        place_kernel,
        out_shape=jax.ShapeDtypeStruct((TOK, 128), BF),
        in_specs=[VM, VM],
        out_specs=VM,
        compiler_params=PARAMS,
        name="place",
    )(slot, back)


def layer_kernel(
    pos_ref, core_ref, seg_ref, x0, x1, x2, x3, g0, g1, g2, g3, win_ref, wout_ref,
    mine_ref, other_ref, c0, c1, c2, c3,
    w, wo, pre, act, segc, aw, dsil, dkv, du, u_ref, y_ref, dp_ref, dw_ref,
):
    xs, gs = (x0, x1, x2, x3), (g0, g1, g2, g3)
    both = (c0, c1, c2, c3)
    me, core = pos_ref[0], core_ref[0]
    for k in range(NT):
        at = pl.multiple_of(lax.rem(me + k, NT) * 128, 128)
        for c in range(4):
            w[k * 128 : (k + 1) * 128, c * 128 : (c + 1) * 128] = win_ref[c, pl.ds(at, 128), :]
        wo[:, k * 128 : (k + 1) * 128] = wout_ref[:, pl.ds(at, 128)]
    for b in range(TOK // 128):
        segc[b * 128 : (b + 1) * 128, :] = column(
            seg_ref[0:1, b * 128 : (b + 1) * 128]
        )

    def stats(r0, n):
        x = [r[r0 : r0 + n, :].astype(F32) for r in xs]
        mean = jnp.sum(x[0] + x[1] + x[2] + x[3], axis=1, keepdims=True) * (1.0 / D)
        x = [v - mean for v in x]
        var = jnp.sum(x[0] * x[0] + x[1] * x[1] + x[2] * x[2] + x[3] * x[3], axis=1, keepdims=True)
        scale = lax.rsqrt(var * (1.0 / D) + 1e-05)
        return [v * scale for v in x], scale

    step = 64
    for q in range(TOK // QB):
        lo = q * QB
        for r0 in range(lo, lo + QB, step):
            n, _ = stats(r0, step)
            for k in range(NT):
                u_ref[r0 : r0 + step, k * 128 : (k + 1) * 128] = n[k].astype(BF)
        pre[lo : lo + QB, :] = dot(u_ref[lo : lo + QB, :], w[...], 1, 0)
        for r0 in range(lo, lo + QB, step):
            p = pre[r0 : r0 + step, :]
            s = 0.5 + 0.5 * jnp.tanh(0.5 * p)
            ps = p * s
            act[r0 : r0 + step, :] = ps.astype(BF)
            pre[r0 : r0 + step, :] = s + ps * (1.0 - s)

    dkv[...] = jnp.zeros((TOK, 256), F32)
    for q in range(TOK // QB):
        lo = q * QB
        k0 = max(0, lo - SEQ_MOST)
        width = lo + QB - k0
        queries = act[lo : lo + QB, 256:384]
        o = jnp.zeros((QB, HD), F32)
        for kb in range(k0, lo + QB, QB):
            sc = dot(queries, act[kb : kb + QB, 384:512], 1, 1) * (HD ** (-0.5))
            for j in range(0, QB, 128):
                same = segc[lo : lo + QB, :] == seg_ref[0:1, kb + j : kb + j + 128].astype(F32)
                if kb == lo:
                    same = same & (iota((QB, 128), 1) + j <= iota((QB, 128), 0))
                v = sc[:, j : j + 128]
                s = 0.5 + 0.5 * jnp.tanh(0.5 * v)
                vs = v * s
                at = kb - k0 + j
                aw[:, at : at + 128] = jnp.where(same, vs * (1.0 / SEQ_MOST), 0.0).astype(BF)
                dsil[:, at : at + 128] = jnp.where(
                    same, (s + vs * (1.0 - s)) * (HD ** (-0.5) / SEQ_MOST), 0.0
                )
        o = dot(aw[:, 0:width], act[k0 : lo + QB, 128:256], 1, 0)
        gate = act[lo : lo + QB, 0:128].astype(F32)
        mean = jnp.sum(o, axis=1, keepdims=True) * (1.0 / HD)
        o = o - mean
        scale = lax.rsqrt(jnp.sum(o * o, axis=1, keepdims=True) * (1.0 / HD) + 1e-05)
        n = o * scale
        y_ref[lo : lo + QB, :] = (n * gate).astype(BF)
        dy = dot(gs[0][lo : lo + QB, :], wo[:, 0:128], 1, 1)
        for k in range(1, NT):
            dy = dy + dot(gs[k][lo : lo + QB, :], wo[:, k * 128 : (k + 1) * 128], 1, 1)
        dy = dy.astype(BF).astype(F32)
        dgate = (dy * n).astype(BF).astype(F32)
        dn = dy * gate
        m1 = jnp.sum(dn, axis=1, keepdims=True) * (1.0 / HD)
        m2 = jnp.sum(dn * n, axis=1, keepdims=True) * (1.0 / HD)
        do = ((dn - m1 - n * m2) * scale).astype(BF)
        dp_ref[lo : lo + QB, 0:128] = (dgate * pre[lo : lo + QB, 0:128]).astype(BF)
        dq = jnp.zeros((QB, HD), F32)
        for kb in range(k0, lo + QB, QB):
            at = kb - k0
            da = dot(do, act[kb : kb + QB, 128:256], 1, 1).astype(BF).astype(F32)
            ds = (da * dsil[:, at : at + QB]).astype(BF)
            dq = dq + dot(ds, act[kb : kb + QB, 384:512], 1, 0)
            dkv[kb : kb + QB, 0:128] += dot(aw[:, at : at + QB], do, 0, 0)
            dkv[kb : kb + QB, 128:256] += dot(ds, queries, 0, 0)
        dq = dq.astype(BF).astype(F32)
        dp_ref[lo : lo + QB, 256:384] = (dq * pre[lo : lo + QB, 256:384]).astype(BF)

    for q in range(TOK // QB):
        lo = q * QB
        dvb = dkv[lo : lo + QB, 0:128].astype(BF).astype(F32)
        dkb = dkv[lo : lo + QB, 128:256].astype(BF).astype(F32)
        dp_ref[lo : lo + QB, 128:256] = (dvb * pre[lo : lo + QB, 128:256]).astype(BF)
        dp_ref[lo : lo + QB, 384:512] = (dkb * pre[lo : lo + QB, 384:512]).astype(BF)
        du[...] = dot(dp_ref[lo : lo + QB, :], w[...], 1, 1).astype(BF).astype(F32)
        for r in range(0, QB, step):
            n, scale = stats(lo + r, step)
            d = [du[r : r + step, k * 128 : (k + 1) * 128] for k in range(NT)]
            m1 = jnp.sum(d[0] + d[1] + d[2] + d[3], axis=1, keepdims=True) * (1.0 / D)
            m2 = jnp.sum(
                d[0] * n[0] + d[1] * n[1] + d[2] * n[2] + d[3] * n[3], axis=1, keepdims=True
            ) * (1.0 / D)
            for k in range(NT):
                both[k][lo + r : lo + r + step, :] = ((d[k] - m1 - n[k] * m2) * scale).astype(BF)

    for k in range(NT):
        at = pl.multiple_of(lax.rem(me + k, NT) * 128, 128)
        dw = dot(u_ref[:, k * 128 : (k + 1) * 128], dp_ref[...], 0, 0)
        for c in range(4):
            dw_ref[pl.ds(pl.multiple_of(c * 512 + at, 128), 128), :] = dw[:, c * 128 : (c + 1) * 128]
        dw_ref[pl.ds(pl.multiple_of(2048 + at, 128), 128), :] = dot(y_ref[...], gs[k][...], 0, 0)
        both[k][TOK:, :] = dot(y_ref[...], wo[:, k * 128 : (k + 1) * 128], 1, 0).astype(BF)
    mine_ref[...] = dw_ref[pl.ds(pl.multiple_of(core * 1280, 1280), 1280), :]
    other_ref[...] = dw_ref[pl.ds(pl.multiple_of(1280 - core * 1280, 1280), 1280), :].astype(BF)


def layer(pos, core, seg, xs, gs, w_in, w_out):
    pair = jax.ShapeDtypeStruct((2 * TOK, 128), BF)
    return pl.pallas_call(
        layer_kernel,
        out_shape=(jax.ShapeDtypeStruct((1280, 128), F32), jax.ShapeDtypeStruct((1280, 128), BF))
        + (pair,) * 4,
        in_specs=[SM, SM] + [VM] * 11,
        out_specs=(VM,) * 6,
        scratch_shapes=[
            pltpu.VMEM((D, 512), BF),
            pltpu.VMEM((HD, D), BF),
            pltpu.VMEM((TOK, 512), F32),
            pltpu.VMEM((TOK, 512), BF),
            pltpu.VMEM((TOK, 128), F32),
            pltpu.VMEM((QB, 768), BF),
            pltpu.VMEM((QB, 768), F32),
            pltpu.VMEM((TOK, 256), F32),
            pltpu.VMEM((QB, 512), F32),
            pltpu.VMEM((TOK, D), BF),
            pltpu.VMEM((TOK, HD), BF),
            pltpu.VMEM((TOK, 512), BF),
            pltpu.VMEM((2560, 128), F32),
        ],
        compiler_params=PARAMS,
        name="layer",
    )(pos, core, seg, *xs, *gs, w_in, w_out)


def spread(at_ref, blocks, size, values):
    lows, highs, pairs = [], [], []
    for b in range(blocks):
        at = at_ref[b : b + 1, :]
        upper = column((at >= size).astype(F32)) > 0.5
        value = values[b * 128 : (b + 1) * 128, :]
        pairs.append(
            jnp.concatenate([jnp.where(upper, 0.0, value), jnp.where(upper, value, 0.0)], axis=1).astype(BF)
        )
        at = jnp.broadcast_to(jnp.where(at >= size, at - size, at), (128, 128))
        lows.append(((at & 127) == iota((128, 128), 0)).astype(F32).astype(BF))
        highs.append((at >> 7).astype(F32).astype(BF))
    low = jnp.concatenate(lows, axis=1)
    high = jnp.concatenate(highs, axis=1)
    pair = jnp.concatenate(pairs, axis=0)
    return [dot(hot_where(high, s, low), pair, 1, 0) for s in range(size // 128)]


def slots_kernel(slot_ref, grad_ref, d0, d1, d2, d3, out_ref):
    dx = grad_ref[...].astype(F32) + (
        d0[...].astype(F32) + d1[...].astype(F32) + d2[...].astype(F32) + d3[...].astype(F32)
    )
    half = SLOTS // 2
    for s, both in enumerate(spread(slot_ref, TOK // 128, half, dx)):
        out_ref[s * 128 : (s + 1) * 128, :] = both[:, :128].astype(BF)
        out_ref[half + s * 128 : half + (s + 1) * 128, :] = both[:, 128:].astype(BF)


def to_slots(slot, grad, parts):
    top = pl.BlockSpec((TOK, 128), lambda i: (0, 0))
    return pl.pallas_call(
        slots_kernel,
        out_shape=jax.ShapeDtypeStruct((SLOTS, 128), BF),
        grid=(1,),
        in_specs=[pl.BlockSpec((TOK // 128, 128), lambda i: (0, 0))] + [top] * 5,
        out_specs=pl.BlockSpec((SLOTS, 128), lambda i: (0, 0)),
        compiler_params=PARAMS,
        name="to_slots",
    )(slot, grad, *parts)


def add_rows_kernel(req_ref, arrived_ref, out_ref):
    half = ROWS // 2
    for s, both in enumerate(spread(req_ref, SLOTS // 128, half, arrived_ref[...].astype(F32))):
        out_ref[s * 128 : (s + 1) * 128, :] = both[:, :128]
        out_ref[half + s * 128 : half + (s + 1) * 128, :] = both[:, 128:]


def add_rows(req, arrived):
    return pl.pallas_call(
        add_rows_kernel,
        out_shape=jax.ShapeDtypeStruct((ROWS, 128), F32),
        in_specs=[VM, VM],
        out_specs=VM,
        compiler_params=PARAMS,
        name="add_rows",
    )(req, arrived)


def unpack_kernel(y_ref, p0, p1, p2, p3, in_ref, out_ref, whole):
    for k, p in enumerate((p0, p1, p2, p3)):
        half, quarter = y_place(lax.rem(y_ref[0] + k, 4))
        for core in range(2):
            at = pl.multiple_of(half * 640 + quarter * 320 + core * 1280, 320)
            whole[pl.ds(at, 320), :] = p[core * 320 : (core + 1) * 320, :].astype(F32)
    in_ref[...] = whole[0:2048, :]
    for k in range(NT):
        out_ref[:, k * 128 : (k + 1) * 128] = whole[2048 + k * 128 : 2176 + k * 128, :]


def unpack(y, parts):
    return pl.pallas_call(
        unpack_kernel,
        out_shape=(jax.ShapeDtypeStruct((2048, 128), F32), jax.ShapeDtypeStruct((HD, D), F32)),
        in_specs=[SM] + [VM] * 4,
        out_specs=(VM, VM),
        scratch_shapes=[pltpu.VMEM((2560, 128), F32)],
        compiler_params=PARAMS,
        name="unpack",
    )(y, *parts)


def shift(x, axis, fn, n):
    return lax.ppermute(x, axis, [(i, fn(i)) for i in range(n)])


def gather_pieces(x):
    return [x] + [shift(x, "tensor", lambda i, k=k: (i - k) % NT, NT) for k in (1, 3, 2)]


def order(pieces):
    own, one, three, two = pieces
    return [own, one, two, three]


def scatter_pieces(parts):
    return [parts[0]] + [shift(parts[k], "tensor", lambda i, k=k: (i + k) % NT, NT) for k in (1, 3, 2)]


def pick(x, i):
    return lax.dynamic_index_in_dim(x, i, 0, keepdims=False)


def y_place(y):
    return ((y == 1) | (y == 2)).astype(I32), (y >= 2).astype(I32)


def reduce_over_chips(mine, other):
    half, quarter = y_place(lax.axis_index("table") // 2)
    other = shift(other, "table", lambda i: i ^ 1, 8)
    mine = (mine + other.astype(F32)).reshape(2, 640, 128)
    got = shift(pick(mine, 1 - half).astype(BF), "table", lambda i: i ^ 2, 8)
    mine = (pick(mine, half) + got.astype(F32)).reshape(2, 320, 128)
    got = shift(pick(mine, 1 - quarter).astype(BF), "table", lambda i: 6 - (i & 6) + (i & 1), 8)
    return pick(mine, quarter), got


def add_step(total, mask):
    return (total.astype(F32) + shift(total, "seq", lambda i: i ^ mask, 8).astype(F32)).astype(BF)


def add_group(total):
    got = [shift(total, "seq", lambda i, k=k: i ^ k, 8) for k in (1, 2, 3)]
    for other in got:
        total = total.astype(F32) + other.astype(F32)
    return total.astype(BF)


def gather_weights(total):
    y = (lax.axis_index("table") // 2).astype(I32).reshape(1)
    pairs = [[2 * i, 2 * i + 1] for i in range(4)]
    both = lax.all_gather(total, "table", axis=0, tiled=True, axis_index_groups=pairs)
    parts = [both] + [shift(both, "table", lambda i, k=k: (i - 2 * k) % 8, 8) for k in range(1, 4)]
    return unpack(y, parts)


def body(table, owner, local_row, segment_ids, proj_in, proj_out, grad_out):
    pos = lax.axis_index("tensor").astype(I32).reshape(1)
    core = (lax.axis_index("table") % 2).astype(I32).reshape(1)
    requests, slot = route(owner.reshape(8, 128), local_row.reshape(8, 128))
    gs = order(gather_pieces(grad_out))
    received = lax.all_to_all(requests, BOTH, split_axis=0, concat_axis=0, tiled=True)
    rows = fetch(received, table)
    back = lax.all_to_all(rows.reshape(NOWN, CAP, 128), BOTH, split_axis=0, concat_axis=0, tiled=True)
    x = place(slot, back.reshape(SLOTS, 128))
    xs = order(gather_pieces(x))
    mine, other, c0, c1, c2, c3 = layer(pos, core, segment_ids, xs, gs, proj_in, proj_out)
    cparts = scatter_pieces([c0, c1, c2, c3])
    own, got = reduce_over_chips(mine, other)
    flat = received[:, :CAP].reshape(SLOTS // 128, 128)
    got, cparts[3] = lax.optimization_barrier((got, cparts[3]))
    total = add_group((own + got.astype(F32)).astype(BF))
    cparts, _, flat = lax.optimization_barrier((cparts, total, flat))
    grads = to_slots(slot, grad_out, cparts)
    total = add_step(total, 7)
    grads, total = lax.optimization_barrier((grads, total))
    arrived = lax.all_to_all(grads.reshape(NOWN, CAP, 128), BOTH, split_axis=0, concat_axis=0, tiled=True)
    grad_in, grad_outw = gather_weights(total)
    layer_out = (
        x.astype(F32)
        + (
            cparts[0][TOK:].astype(F32)
            + cparts[1][TOK:].astype(F32)
            + cparts[2][TOK:].astype(F32)
            + cparts[3][TOK:].astype(F32)
        )
    ).astype(BF)
    table_grad = add_rows(flat, arrived.reshape(SLOTS, 128))
    return layer_out, table_grad, grad_in.reshape(4, D, 128), grad_outw


def solution(mesh):
    in_specs = (
        P(BOTH, "tensor"),
        P(BOTH, None),
        P(BOTH),
        P(BOTH, None),
        P(None, None, "tensor"),
        P("tensor", None),
        P(BOTH, "tensor"),
    )
    out_specs = (
        P(BOTH, "tensor"),
        P(BOTH, "tensor"),
        P(None, None, "tensor"),
        P("tensor", None),
    )
    return jax.shard_map(body, mesh=mesh, in_specs=in_specs, out_specs=out_specs, check_vma=False)
```

```python
import functools

import jax
import jax.numpy as jnp
from jax import lax
from jax.experimental import pallas as pl
from jax.experimental.pallas import tpu as pltpu
from jax.sharding import PartitionSpec as P

HD = 128
SEQ_MOST = 512
TOK = 1024
D = 512
NT = 4
NOWN = 64
CAP = 24
SLOTS = NOWN * CAP
ROWS = 2048
QB = 256
BOTH = ("table", "seq")
BF = jnp.bfloat16
F32 = jnp.float32
I32 = jnp.int32
VM = pl.BlockSpec(memory_space=pltpu.VMEM)
SM = pl.BlockSpec(memory_space=pltpu.SMEM)
ANY = pl.BlockSpec(memory_space=pl.ANY)
PARAMS = pltpu.CompilerParams(vmem_limit_bytes=56 * 1024 * 1024)


def iota(shape, dim):
    return lax.broadcasted_iota(I32, shape, dim)


def begin(pairs, sems):
    copies = [pltpu.make_async_copy(a, b, sems.at[i]) for i, (a, b) in enumerate(pairs)]
    for copy in copies:
        copy.start()
    return copies


def finish(copies):
    for copy in copies:
        copy.wait()


def dot(a, b, ca, cb):
    return lax.dot_general(a, b, (((ca,), (cb,)), ((), ())), preferred_element_type=F32)


def route_kernel(owner_ref, row_ref, req_ref, slot_ref):
    blocks = TOK // 128
    upper = (iota((128, 128), 0) < iota((128, 128), 1)).astype(BF)
    scan = jnp.concatenate([upper, jnp.ones((128, 128), BF)], axis=1)
    hots = [(iota((NOWN, 128), 0) == owner_ref[b : b + 1, :]).astype(F32) for b in range(blocks)]
    sums = dot(jnp.concatenate(hots, axis=0).astype(BF), scan, 1, 0)
    carry = jnp.zeros((NOWN, 128), F32)
    highs, lows = [], []
    for b in range(blocks):
        part = sums[b * NOWN : (b + 1) * NOWN, :]
        rank = jnp.sum(hots[b] * (part[:, :128] + carry), axis=0, keepdims=True).astype(I32)
        carry = carry + part[:, 128:]
        row = row_ref[b : b + 1, :]
        slot_ref[b : b + 1, :] = owner_ref[b : b + 1, :] * CAP + rank
        here = iota((32, 128), 0) == rank
        highs.append(jnp.where(here, (row >> 6).astype(F32), 0.0))
        lows.append(jnp.where(here, (row & 63).astype(F32), 0.0))
    hot = jnp.concatenate(hots, axis=1).astype(BF)
    high = dot(hot, jnp.concatenate(highs, axis=1).astype(BF), 1, 1)
    low = dot(hot, jnp.concatenate(lows, axis=1).astype(BF), 1, 1)
    req_ref[...] = jnp.zeros((NOWN, 128), I32)
    req_ref[:, 0:32] = (high * 64.0 + low).astype(I32)


def route(owner, row):
    return pl.pallas_call(
        route_kernel,
        out_shape=(
            jax.ShapeDtypeStruct((NOWN, 128), I32),
            jax.ShapeDtypeStruct((TOK // 128, 128), I32),
        ),
        in_specs=[VM, VM],
        out_specs=(VM, VM),
        compiler_params=PARAMS,
        name="route",
    )(owner, row)


def hot_where(high, value, low_hot):
    return jnp.where(high == value, low_hot, jnp.zeros_like(low_hot))


def fetch_kernel(req_ref, table_ref, out_ref, got):
    half = ROWS // 2
    both = jnp.concatenate([table_ref[:half, :], table_ref[half:, :]], axis=1)
    for c0 in range(0, CAP, 4):
        hots, uppers = [], []
        for c in range(c0, c0 + 4):
            row = jnp.broadcast_to(req_ref[:, c : c + 1], (NOWN, 128))
            low = ((row & 127) == iota((NOWN, 128), 1)).astype(F32).astype(BF)
            high = ((row >> 7) & 7).astype(F32).astype(BF)
            hots.append(jnp.concatenate([hot_where(high, j, low) for j in range(8)], axis=1))
            uppers.append(row >= half)
        pair = dot(jnp.concatenate(hots, axis=0), both, 1, 0)
        rows = jnp.where(jnp.concatenate(uppers, axis=0), pair[:, 128:], pair[:, :128])
        for i in range(4):
            got[pl.ds(c0 + i, NOWN, stride=CAP), :] = rows[i * NOWN : (i + 1) * NOWN, :]
    out_ref[...] = got[...].astype(BF)


def fetch(req, table):
    return pl.pallas_call(
        fetch_kernel,
        out_shape=jax.ShapeDtypeStruct((SLOTS, 128), BF),
        in_specs=[VM, VM],
        out_specs=VM,
        scratch_shapes=[pltpu.VMEM((SLOTS, 128), F32)],
        compiler_params=PARAMS,
        name="fetch",
    )(req, table)


def column(row_vector):
    wide = jnp.broadcast_to(row_vector.astype(F32), (128, 128))
    return jnp.transpose(wide)


def place_kernel(slot_ref, back_any, x_ref, back_ref, sems):
    half = SLOTS // 2
    finish(begin([(back_any, back_ref)], sems))
    both = jnp.concatenate([back_ref[:half, :], back_ref[half:, :]], axis=1)
    for b0 in range(0, TOK // 128, 2):
        hots, uppers = [], []
        for b in (b0, b0 + 1):
            slot = column(slot_ref[b : b + 1, :]).astype(I32)
            upper = slot >= half
            slot = jnp.where(upper, slot - half, slot)
            low = ((slot & 127) == iota((128, 128), 1)).astype(F32).astype(BF)
            high = (slot >> 7).astype(F32).astype(BF)
            hots.append(jnp.concatenate([hot_where(high, j, low) for j in range(half // 128)], axis=1))
            uppers.append(upper)
        pair = dot(jnp.concatenate(hots, axis=0), both, 1, 0)
        rows = jnp.where(jnp.concatenate(uppers, axis=0), pair[:, 128:], pair[:, :128])
        x_ref[b0 * 128 : b0 * 128 + 256, :] = rows.astype(BF)


def place(slot, back):
    return pl.pallas_call(
        place_kernel,
        out_shape=jax.ShapeDtypeStruct((TOK, 128), BF),
        in_specs=[VM, ANY],
        out_specs=VM,
        scratch_shapes=[pltpu.VMEM((SLOTS, 128), BF), pltpu.SemaphoreType.DMA((1,))],
        compiler_params=PARAMS,
        name="place",
    )(slot, back)


def layer_kernel(
    pos_ref, core_ref, seg_ref, xa0, xa1, xa2, xa3, ga0, ga1, ga2, ga3, win_ref, wout_ref,
    mine_ref, other_ref, ca0, ca1, ca2, ca3,
    w, wo, pre, act, segc, aw, dsil, dkv, du, u_ref, y_ref, dp_ref, dw_ref,
    x_in, g_in, c_out, x_sems, g_sems, d_sems, z_sems,
):
    xs, gs, both = ([ref.at[k] for k in range(NT)] for ref in (x_in, g_in, c_out))
    targets = (ca0, ca1, ca2, ca3)
    x_copies = begin(list(zip((xa0, xa1, xa2, xa3), xs)), x_sems)
    g_copies = begin(list(zip((ga0, ga1, ga2, ga3), gs)), g_sems)
    me, core = pos_ref[0], core_ref[0]
    for k in range(NT):
        at = pl.multiple_of(lax.rem(me + k, NT) * 128, 128)
        for c in range(4):
            w[k * 128 : (k + 1) * 128, c * 128 : (c + 1) * 128] = win_ref[c, pl.ds(at, 128), :]
        wo[:, k * 128 : (k + 1) * 128] = wout_ref[:, pl.ds(at, 128)]
    for b in range(TOK // 128):
        segc[b * 128 : (b + 1) * 128, :] = column(
            seg_ref[0:1, b * 128 : (b + 1) * 128]
        )

    def stats(r0, n):
        x = [r[r0 : r0 + n, :].astype(F32) for r in xs]
        mean = jnp.sum(x[0] + x[1] + x[2] + x[3], axis=1, keepdims=True) * (1.0 / D)
        x = [v - mean for v in x]
        var = jnp.sum(x[0] * x[0] + x[1] * x[1] + x[2] * x[2] + x[3] * x[3], axis=1, keepdims=True)
        scale = lax.rsqrt(var * (1.0 / D) + 1e-05)
        return [v * scale for v in x], scale

    finish(x_copies)
    step = 64
    for q in range(TOK // QB):
        lo = q * QB
        for r0 in range(lo, lo + QB, step):
            n, _ = stats(r0, step)
            for k in range(NT):
                u_ref[r0 : r0 + step, k * 128 : (k + 1) * 128] = n[k].astype(BF)
        pre[lo : lo + QB, :] = dot(u_ref[lo : lo + QB, :], w[...], 1, 0)
        for r0 in range(lo, lo + QB, step):
            p = pre[r0 : r0 + step, :]
            s = 0.5 + 0.5 * jnp.tanh(0.5 * p)
            ps = p * s
            act[r0 : r0 + step, :] = ps.astype(BF)
            pre[r0 : r0 + step, :] = s + ps * (1.0 - s)

    finish(g_copies)
    dkv[...] = jnp.zeros((TOK, 256), F32)
    for q in range(TOK // QB):
        lo = q * QB
        k0 = max(0, lo - SEQ_MOST)
        width = lo + QB - k0
        queries = act[lo : lo + QB, 256:384]
        o = jnp.zeros((QB, HD), F32)
        for kb in range(k0, lo + QB, QB):
            sc = dot(queries, act[kb : kb + QB, 384:512], 1, 1) * (HD ** (-0.5))
            for j in range(0, QB, 128):
                same = segc[lo : lo + QB, :] == seg_ref[0:1, kb + j : kb + j + 128].astype(F32)
                if kb == lo:
                    same = same & (iota((QB, 128), 1) + j <= iota((QB, 128), 0))
                v = sc[:, j : j + 128]
                s = 0.5 + 0.5 * jnp.tanh(0.5 * v)
                vs = v * s
                at = kb - k0 + j
                aw[:, at : at + 128] = jnp.where(same, vs * (1.0 / SEQ_MOST), 0.0).astype(BF)
                dsil[:, at : at + 128] = jnp.where(
                    same, (s + vs * (1.0 - s)) * (HD ** (-0.5) / SEQ_MOST), 0.0
                )
        o = dot(aw[:, 0:width], act[k0 : lo + QB, 128:256], 1, 0)
        gate = act[lo : lo + QB, 0:128].astype(F32)
        mean = jnp.sum(o, axis=1, keepdims=True) * (1.0 / HD)
        o = o - mean
        scale = lax.rsqrt(jnp.sum(o * o, axis=1, keepdims=True) * (1.0 / HD) + 1e-05)
        n = o * scale
        y_ref[lo : lo + QB, :] = (n * gate).astype(BF)
        dy = dot(gs[0][lo : lo + QB, :], wo[:, 0:128], 1, 1)
        for k in range(1, NT):
            dy = dy + dot(gs[k][lo : lo + QB, :], wo[:, k * 128 : (k + 1) * 128], 1, 1)
        dy = dy.astype(BF).astype(F32)
        dgate = (dy * n).astype(BF).astype(F32)
        dn = dy * gate
        m1 = jnp.sum(dn, axis=1, keepdims=True) * (1.0 / HD)
        m2 = jnp.sum(dn * n, axis=1, keepdims=True) * (1.0 / HD)
        do = ((dn - m1 - n * m2) * scale).astype(BF)
        dp_ref[lo : lo + QB, 0:128] = (dgate * pre[lo : lo + QB, 0:128]).astype(BF)
        dq = jnp.zeros((QB, HD), F32)
        for kb in range(k0, lo + QB, QB):
            at = kb - k0
            da = dot(do, act[kb : kb + QB, 128:256], 1, 1).astype(BF).astype(F32)
            ds = (da * dsil[:, at : at + QB]).astype(BF)
            dq = dq + dot(ds, act[kb : kb + QB, 384:512], 1, 0)
            dkv[kb : kb + QB, 0:128] += dot(aw[:, at : at + QB], do, 0, 0)
            dkv[kb : kb + QB, 128:256] += dot(ds, queries, 0, 0)
        dq = dq.astype(BF).astype(F32)
        dp_ref[lo : lo + QB, 256:384] = (dq * pre[lo : lo + QB, 256:384]).astype(BF)

    for q in range(TOK // QB):
        lo = q * QB
        dvb = dkv[lo : lo + QB, 0:128].astype(BF).astype(F32)
        dkb = dkv[lo : lo + QB, 128:256].astype(BF).astype(F32)
        dp_ref[lo : lo + QB, 128:256] = (dvb * pre[lo : lo + QB, 128:256]).astype(BF)
        dp_ref[lo : lo + QB, 384:512] = (dkb * pre[lo : lo + QB, 384:512]).astype(BF)
        du[...] = dot(dp_ref[lo : lo + QB, :], w[...], 1, 1).astype(BF).astype(F32)
        for r in range(0, QB, step):
            n, scale = stats(lo + r, step)
            d = [du[r : r + step, k * 128 : (k + 1) * 128] for k in range(NT)]
            m1 = jnp.sum(d[0] + d[1] + d[2] + d[3], axis=1, keepdims=True) * (1.0 / D)
            m2 = jnp.sum(
                d[0] * n[0] + d[1] * n[1] + d[2] * n[2] + d[3] * n[3], axis=1, keepdims=True
            ) * (1.0 / D)
            for k in range(NT):
                both[k][lo + r : lo + r + step, :] = ((d[k] - m1 - n[k] * m2) * scale).astype(BF)

    out_copies = begin([(both[k].at[0:TOK], targets[k].at[0:TOK]) for k in range(NT)], d_sems)
    for k in range(NT):
        both[k][TOK:, :] = dot(y_ref[...], wo[:, k * 128 : (k + 1) * 128], 1, 0).astype(BF)
    out_copies += begin([(both[k].at[TOK : 2 * TOK], targets[k].at[TOK : 2 * TOK]) for k in range(NT)], z_sems)
    for k in range(NT):
        at = pl.multiple_of(lax.rem(me + k, NT) * 128, 128)
        dw = dot(u_ref[:, k * 128 : (k + 1) * 128], dp_ref[...], 0, 0)
        for c in range(4):
            dw_ref[pl.ds(pl.multiple_of(c * 512 + at, 128), 128), :] = dw[:, c * 128 : (c + 1) * 128]
        dw_ref[pl.ds(pl.multiple_of(2048 + at, 128), 128), :] = dot(y_ref[...], gs[k][...], 0, 0)
    mine_ref[...] = dw_ref[pl.ds(pl.multiple_of(core * 1280, 1280), 1280), :]
    other_ref[...] = dw_ref[pl.ds(pl.multiple_of(1280 - core * 1280, 1280), 1280), :].astype(BF)
    finish(out_copies)


def layer(pos, core, seg, xs, gs, w_in, w_out):
    pair = jax.ShapeDtypeStruct((2 * TOK, 128), BF)
    return pl.pallas_call(
        layer_kernel,
        out_shape=(jax.ShapeDtypeStruct((1280, 128), F32), jax.ShapeDtypeStruct((1280, 128), BF))
        + (pair,) * 4,
        in_specs=[SM, SM, VM] + [ANY] * 8 + [VM] * 2,
        out_specs=(VM,) * 2 + (ANY,) * 4,
        scratch_shapes=[
            pltpu.VMEM((D, 512), BF),
            pltpu.VMEM((HD, D), BF),
            pltpu.VMEM((TOK, 512), F32),
            pltpu.VMEM((TOK, 512), BF),
            pltpu.VMEM((TOK, 128), F32),
            pltpu.VMEM((QB, 768), BF),
            pltpu.VMEM((QB, 768), F32),
            pltpu.VMEM((TOK, 256), F32),
            pltpu.VMEM((QB, 512), F32),
            pltpu.VMEM((TOK, D), BF),
            pltpu.VMEM((TOK, HD), BF),
            pltpu.VMEM((TOK, 512), BF),
            pltpu.VMEM((2560, 128), F32),
            pltpu.VMEM((NT, TOK, 128), BF),
            pltpu.VMEM((NT, TOK, 128), BF),
            pltpu.VMEM((NT, 2 * TOK, 128), BF),
            pltpu.SemaphoreType.DMA((NT,)),
            pltpu.SemaphoreType.DMA((NT,)),
            pltpu.SemaphoreType.DMA((NT,)),
            pltpu.SemaphoreType.DMA((NT,)),
        ],
        compiler_params=PARAMS,
        name="layer",
    )(pos, core, seg, *xs, *gs, w_in, w_out)


def spread(at_ref, blocks, size, values):
    lows, highs, pairs = [], [], []
    for b in range(blocks):
        at = at_ref[b : b + 1, :]
        upper = column((at >= size).astype(F32)) > 0.5
        value = values[b * 128 : (b + 1) * 128, :]
        pairs.append(
            jnp.concatenate([jnp.where(upper, 0.0, value), jnp.where(upper, value, 0.0)], axis=1).astype(BF)
        )
        at = jnp.broadcast_to(jnp.where(at >= size, at - size, at), (128, 128))
        lows.append(((at & 127) == iota((128, 128), 0)).astype(F32).astype(BF))
        highs.append((at >> 7).astype(F32).astype(BF))
    low = jnp.concatenate(lows, axis=1)
    high = jnp.concatenate(highs, axis=1)
    pair = jnp.concatenate(pairs, axis=0)
    return [dot(hot_where(high, s, low), pair, 1, 0) for s in range(size // 128)]


def slots_kernel(slot_ref, grad_ref, c0, c1, c2, c3, out_ref, parts, sems):
    finish(begin([(c.at[0:TOK], parts.at[k]) for k, c in enumerate((c0, c1, c2, c3))], sems))
    d0, d1, d2, d3 = (parts.at[k] for k in range(NT))
    dx = grad_ref[...].astype(F32) + (
        d0[...].astype(F32) + d1[...].astype(F32) + d2[...].astype(F32) + d3[...].astype(F32)
    )
    half = SLOTS // 2
    for s, both in enumerate(spread(slot_ref, TOK // 128, half, dx)):
        out_ref[s * 128 : (s + 1) * 128, :] = both[:, :128].astype(BF)
        out_ref[half + s * 128 : half + (s + 1) * 128, :] = both[:, 128:].astype(BF)


def to_slots(slot, grad, parts):
    return pl.pallas_call(
        slots_kernel,
        out_shape=jax.ShapeDtypeStruct((SLOTS, 128), BF),
        in_specs=[VM, VM] + [ANY] * 4,
        out_specs=VM,
        scratch_shapes=[pltpu.VMEM((NT, TOK, 128), BF), pltpu.SemaphoreType.DMA((NT,))],
        compiler_params=PARAMS,
        name="to_slots",
    )(slot, grad, *parts)


def add_rows_kernel(req_ref, arrived_any, out_ref, arrived_ref, sems):
    half = ROWS // 2
    finish(begin([(arrived_any, arrived_ref)], sems))
    for s, both in enumerate(spread(req_ref, SLOTS // 128, half, arrived_ref[...].astype(F32))):
        out_ref[s * 128 : (s + 1) * 128, :] = both[:, :128]
        out_ref[half + s * 128 : half + (s + 1) * 128, :] = both[:, 128:]


def add_rows(req, arrived):
    return pl.pallas_call(
        add_rows_kernel,
        out_shape=jax.ShapeDtypeStruct((ROWS, 128), F32),
        in_specs=[VM, ANY],
        out_specs=VM,
        scratch_shapes=[pltpu.VMEM((SLOTS, 128), BF), pltpu.SemaphoreType.DMA((1,))],
        compiler_params=PARAMS,
        name="add_rows",
    )(req, arrived)


def unpack_kernel(y_ref, p0, p1, p2, p3, in_ref, out_ref, whole, parts, sems):
    copies = begin([(p, parts.at[k]) for k, p in enumerate((p0, p1, p2, p3))], sems)
    for k in range(NT):
        copies[k].wait()
        p = parts.at[k]
        half, quarter = y_place(lax.rem(y_ref[0] + k, 4))
        for core in range(2):
            at = pl.multiple_of(half * 640 + quarter * 320 + core * 1280, 320)
            whole[pl.ds(at, 320), :] = p[core * 320 : (core + 1) * 320, :].astype(F32)
    in_ref[...] = whole[0:2048, :]
    for k in range(NT):
        out_ref[:, k * 128 : (k + 1) * 128] = whole[2048 + k * 128 : 2176 + k * 128, :]


def unpack(y, parts):
    return pl.pallas_call(
        unpack_kernel,
        out_shape=(jax.ShapeDtypeStruct((2048, 128), F32), jax.ShapeDtypeStruct((HD, D), F32)),
        in_specs=[SM] + [ANY] * 4,
        out_specs=(VM, VM),
        scratch_shapes=[
            pltpu.VMEM((2560, 128), F32),
            pltpu.VMEM((NT, 640, 128), BF),
            pltpu.SemaphoreType.DMA((NT,)),
        ],
        compiler_params=PARAMS,
        name="unpack",
    )(y, *parts)


def shift(x, axis, fn, n):
    return lax.ppermute(x, axis, [(i, fn(i)) for i in range(n)])


def gather_pieces(x):
    return [x] + [shift(x, "tensor", lambda i, k=k: (i - k) % NT, NT) for k in (1, 3, 2)]


def order(pieces):
    own, one, three, two = pieces
    return [own, one, two, three]


def scatter_pieces(parts):
    return [parts[0]] + [shift(parts[k], "tensor", lambda i, k=k: (i + k) % NT, NT) for k in (1, 3, 2)]


def pick(x, i):
    return lax.dynamic_index_in_dim(x, i, 0, keepdims=False)


def y_place(y):
    return ((y == 1) | (y == 2)).astype(I32), (y >= 2).astype(I32)


def reduce_over_chips(mine, other):
    half, quarter = y_place(lax.axis_index("table") // 2)
    other = shift(other, "table", lambda i: i ^ 1, 8)
    mine = (mine + other.astype(F32)).reshape(2, 640, 128)
    got = shift(pick(mine, 1 - half).astype(BF), "table", lambda i: i ^ 2, 8)
    mine = (pick(mine, half) + got.astype(F32)).reshape(2, 320, 128)
    got = shift(pick(mine, 1 - quarter).astype(BF), "table", lambda i: 6 - (i & 6) + (i & 1), 8)
    return pick(mine, quarter), got


def add_step(total, mask):
    return (total.astype(F32) + shift(total, "seq", lambda i: i ^ mask, 8).astype(F32)).astype(BF)


def add_group(total):
    got = [shift(total, "seq", lambda i, k=k: i ^ k, 8) for k in (1, 2, 3)]
    for other in got:
        total = total.astype(F32) + other.astype(F32)
    return total.astype(BF)


def gather_weights(total, add):
    y = (lax.axis_index("table") // 2).astype(I32).reshape(1)
    pairs = [[2 * i, 2 * i + 1] for i in range(4)]
    both = lax.all_gather(total, "table", axis=0, tiled=True, axis_index_groups=pairs)
    parts = [both] + [shift(both, "table", lambda i, k=k: (i - 2 * k) % 8, 8) for k in range(1, 4)]
    table_grad = add()
    parts, table_grad = lax.optimization_barrier((parts, table_grad))
    return unpack(y, parts), table_grad


def body(table, owner, local_row, segment_ids, proj_in, proj_out, grad_out):
    pos = lax.axis_index("tensor").astype(I32).reshape(1)
    core = (lax.axis_index("table") % 2).astype(I32).reshape(1)
    requests, slot = route(owner.reshape(8, 128), local_row.reshape(8, 128))
    gs = order(gather_pieces(grad_out))
    received = lax.all_to_all(requests, BOTH, split_axis=0, concat_axis=0, tiled=True)
    rows = fetch(received, table)
    back = lax.all_to_all(rows.reshape(NOWN, CAP, 128), BOTH, split_axis=0, concat_axis=0, tiled=True)
    x = place(slot, back.reshape(SLOTS, 128))
    xs = order(gather_pieces(x))
    mine, other, c0, c1, c2, c3 = layer(pos, core, segment_ids, xs, gs, proj_in, proj_out)
    cparts = scatter_pieces([c0, c1, c2, c3])
    own, got = reduce_over_chips(mine, other)
    flat = received[:, :CAP].reshape(SLOTS // 128, 128)
    got, cparts[3] = lax.optimization_barrier((got, cparts[3]))
    total = add_group((own + got.astype(F32)).astype(BF))
    cparts, _, flat = lax.optimization_barrier((cparts, total, flat))
    grads = to_slots(slot, grad_out, cparts)
    total = add_step(total, 7)
    grads, total = lax.optimization_barrier((grads, total))
    arrived = lax.all_to_all(grads.reshape(NOWN, CAP, 128), BOTH, split_axis=0, concat_axis=0, tiled=True)
    (grad_in, grad_outw), table_grad = gather_weights(
        total, lambda: add_rows(flat, arrived.reshape(SLOTS, 128))
    )
    layer_out = (
        x.astype(F32)
        + (
            cparts[0][TOK:].astype(F32)
            + cparts[1][TOK:].astype(F32)
            + cparts[2][TOK:].astype(F32)
            + cparts[3][TOK:].astype(F32)
        )
    ).astype(BF)
    return layer_out, table_grad, grad_in.reshape(4, D, 128), grad_outw


def solution(mesh):
    in_specs = (
        P(BOTH, "tensor"),
        P(BOTH, None),
        P(BOTH),
        P(BOTH, None),
        P(None, None, "tensor"),
        P("tensor", None),
        P(BOTH, "tensor"),
    )
    out_specs = (
        P(BOTH, "tensor"),
        P(BOTH, "tensor"),
        P(None, None, "tensor"),
        P("tensor", None),
    )
    return jax.shard_map(body, mesh=mesh, in_specs=in_specs, out_specs=out_specs, check_vma=False)
```

```python
import functools

import jax
import jax.numpy as jnp
from jax import lax
from jax.experimental import pallas as pl
from jax.experimental.pallas import tpu as pltpu
from jax.sharding import PartitionSpec as P

HD = 128
SEQ_MOST = 512
TOK = 1024
D = 512
NT = 4
NOWN = 64
CAP = 24
SLOTS = NOWN * CAP
ROWS = 2048
QB = 256
BOTH = ("table", "seq")
BF = jnp.bfloat16
F32 = jnp.float32
I32 = jnp.int32
VM = pl.BlockSpec(memory_space=pltpu.VMEM)
SM = pl.BlockSpec(memory_space=pltpu.SMEM)
PARAMS = pltpu.CompilerParams(vmem_limit_bytes=56 * 1024 * 1024)


def iota(shape, dim):
    return lax.broadcasted_iota(I32, shape, dim)


def dot(a, b, ca, cb):
    return lax.dot_general(a, b, (((ca,), (cb,)), ((), ())), preferred_element_type=F32)


def route_kernel(owner_ref, row_ref, req_ref, slot_ref):
    blocks = TOK // 128
    upper = (iota((128, 128), 0) < iota((128, 128), 1)).astype(BF)
    scan = jnp.concatenate([upper, jnp.ones((128, 128), BF)], axis=1)
    hots = [(iota((NOWN, 128), 0) == owner_ref[b : b + 1, :]).astype(F32) for b in range(blocks)]
    sums = dot(jnp.concatenate(hots, axis=0).astype(BF), scan, 1, 0)
    carry = jnp.zeros((NOWN, 128), F32)
    highs, lows = [], []
    for b in range(blocks):
        part = sums[b * NOWN : (b + 1) * NOWN, :]
        rank = jnp.sum(hots[b] * (part[:, :128] + carry), axis=0, keepdims=True).astype(I32)
        carry = carry + part[:, 128:]
        row = row_ref[b : b + 1, :]
        slot_ref[b : b + 1, :] = owner_ref[b : b + 1, :] * CAP + rank
        here = iota((32, 128), 0) == rank
        highs.append(jnp.where(here, (row >> 6).astype(F32), 0.0))
        lows.append(jnp.where(here, (row & 63).astype(F32), 0.0))
    hot = jnp.concatenate(hots, axis=1).astype(BF)
    high = dot(hot, jnp.concatenate(highs, axis=1).astype(BF), 1, 1)
    low = dot(hot, jnp.concatenate(lows, axis=1).astype(BF), 1, 1)
    req_ref[...] = jnp.zeros((NOWN, 128), I32)
    req_ref[:, 0:32] = (high * 64.0 + low).astype(I32)


def route(owner, row):
    return pl.pallas_call(
        route_kernel,
        out_shape=(
            jax.ShapeDtypeStruct((NOWN, 128), I32),
            jax.ShapeDtypeStruct((TOK // 128, 128), I32),
        ),
        in_specs=[VM, VM],
        out_specs=(VM, VM),
        compiler_params=PARAMS,
        name="route",
    )(owner, row)


def hot_where(high, value, low_hot):
    return jnp.where(high == value, low_hot, jnp.zeros_like(low_hot))


def fetch_kernel(req_ref, table_ref, out_ref, got):
    half = ROWS // 2
    both = jnp.concatenate([table_ref[:half, :], table_ref[half:, :]], axis=1)
    for c0 in range(0, CAP, 4):
        hots, uppers = [], []
        for c in range(c0, c0 + 4):
            row = jnp.broadcast_to(req_ref[:, c : c + 1], (NOWN, 128))
            low = ((row & 127) == iota((NOWN, 128), 1)).astype(F32).astype(BF)
            high = ((row >> 7) & 7).astype(F32).astype(BF)
            hots.append(jnp.concatenate([hot_where(high, j, low) for j in range(8)], axis=1))
            uppers.append(row >= half)
        pair = dot(jnp.concatenate(hots, axis=0), both, 1, 0)
        rows = jnp.where(jnp.concatenate(uppers, axis=0), pair[:, 128:], pair[:, :128])
        for i in range(4):
            got[pl.ds(c0 + i, NOWN, stride=CAP), :] = rows[i * NOWN : (i + 1) * NOWN, :]
    out_ref[...] = got[...].astype(BF)


def fetch(req, table):
    return pl.pallas_call(
        fetch_kernel,
        out_shape=jax.ShapeDtypeStruct((SLOTS, 128), BF),
        in_specs=[VM, VM],
        out_specs=VM,
        scratch_shapes=[pltpu.VMEM((SLOTS, 128), F32)],
        compiler_params=PARAMS,
        name="fetch",
    )(req, table)


def column(row_vector):
    wide = jnp.broadcast_to(row_vector.astype(F32), (128, 128))
    return jnp.transpose(wide)


def place_kernel(slot_ref, back_ref, x_ref):
    half = SLOTS // 2
    both = jnp.concatenate([back_ref[:half, :], back_ref[half:, :]], axis=1)
    for b0 in range(0, TOK // 128, 2):
        hots, uppers = [], []
        for b in (b0, b0 + 1):
            slot = column(slot_ref[b : b + 1, :]).astype(I32)
            upper = slot >= half
            slot = jnp.where(upper, slot - half, slot)
            low = ((slot & 127) == iota((128, 128), 1)).astype(F32).astype(BF)
            high = (slot >> 7).astype(F32).astype(BF)
            hots.append(jnp.concatenate([hot_where(high, j, low) for j in range(half // 128)], axis=1))
            uppers.append(upper)
        pair = dot(jnp.concatenate(hots, axis=0), both, 1, 0)
        rows = jnp.where(jnp.concatenate(uppers, axis=0), pair[:, 128:], pair[:, :128])
        x_ref[b0 * 128 : b0 * 128 + 256, :] = rows.astype(BF)


def place(slot, back):
    return pl.pallas_call(
        place_kernel,
        out_shape=jax.ShapeDtypeStruct((TOK, 128), BF),
        in_specs=[VM, VM],
        out_specs=VM,
        compiler_params=PARAMS,
        name="place",
    )(slot, back)


def layer_kernel(
    pos_ref, core_ref, seg_ref, x0, x1, x2, x3, g0, g1, g2, g3, win_ref, wout_ref,
    mine_ref, other_ref, c0, c1, c2, c3,
    w, wo, pre, act, segc, aw, dsil, dkv, du, u_ref, y_ref, dp_ref, dw_ref,
):
    xs, gs = (x0, x1, x2, x3), (g0, g1, g2, g3)
    both = (c0, c1, c2, c3)
    me, core = pos_ref[0], core_ref[0]
    for k in range(NT):
        at = pl.multiple_of(lax.rem(me + k, NT) * 128, 128)
        for c in range(4):
            w[k * 128 : (k + 1) * 128, c * 128 : (c + 1) * 128] = win_ref[c, pl.ds(at, 128), :]
        wo[:, k * 128 : (k + 1) * 128] = wout_ref[:, pl.ds(at, 128)]
    for b in range(TOK // 128):
        segc[b * 128 : (b + 1) * 128, :] = column(
            seg_ref[0:1, b * 128 : (b + 1) * 128]
        )

    def stats(r0, n):
        x = [r[r0 : r0 + n, :].astype(F32) for r in xs]
        mean = jnp.sum(x[0] + x[1] + x[2] + x[3], axis=1, keepdims=True) * (1.0 / D)
        x = [v - mean for v in x]
        var = jnp.sum(x[0] * x[0] + x[1] * x[1] + x[2] * x[2] + x[3] * x[3], axis=1, keepdims=True)
        scale = lax.rsqrt(var * (1.0 / D) + 1e-05)
        return [v * scale for v in x], scale

    step = 64
    for q in range(TOK // QB):
        lo = q * QB
        for r0 in range(lo, lo + QB, step):
            n, _ = stats(r0, step)
            for k in range(NT):
                u_ref[r0 : r0 + step, k * 128 : (k + 1) * 128] = n[k].astype(BF)
        pre[lo : lo + QB, :] = dot(u_ref[lo : lo + QB, :], w[...], 1, 0)
        for r0 in range(lo, lo + QB, step):
            p = pre[r0 : r0 + step, :]
            s = 0.5 + 0.5 * jnp.tanh(0.5 * p)
            ps = p * s
            act[r0 : r0 + step, :] = ps.astype(BF)
            pre[r0 : r0 + step, :] = s + ps * (1.0 - s)

    dkv[...] = jnp.zeros((TOK, 256), F32)
    for q in range(TOK // QB):
        lo = q * QB
        k0 = max(0, lo - SEQ_MOST)
        width = lo + QB - k0
        queries = act[lo : lo + QB, 256:384]
        o = jnp.zeros((QB, HD), F32)
        for kb in range(k0, lo + QB, QB):
            sc = dot(queries, act[kb : kb + QB, 384:512], 1, 1) * (HD ** (-0.5))
            for j in range(0, QB, 128):
                at = kb - k0 + j
                first, last = 0, QB
                if kb == lo and j:
                    first = j
                if lo - kb == SEQ_MOST and j + 128 < QB:
                    last = j + 128
                rows = slice(first, last)
                same = segc[lo + first : lo + last, :] == seg_ref[0:1, kb + j : kb + j + 128].astype(F32)
                if kb == lo:
                    shape = (last - first, 128)
                    same = same & (iota(shape, 1) + j <= iota(shape, 0) + first)
                v = sc[rows, j : j + 128]
                s = 0.5 + 0.5 * jnp.tanh(0.5 * v)
                vs = v * s
                aw[rows, at : at + 128] = jnp.where(same, vs * (1.0 / SEQ_MOST), 0.0).astype(BF)
                dsil[rows, at : at + 128] = jnp.where(
                    same, (s + vs * (1.0 - s)) * (HD ** (-0.5) / SEQ_MOST), 0.0
                )
                if first:
                    aw[0:first, at : at + 128] = jnp.zeros((first, 128), BF)
                    dsil[0:first, at : at + 128] = jnp.zeros((first, 128), F32)
                if last < QB:
                    aw[last:QB, at : at + 128] = jnp.zeros((QB - last, 128), BF)
                    dsil[last:QB, at : at + 128] = jnp.zeros((QB - last, 128), F32)
        o = dot(aw[:, 0:width], act[k0 : lo + QB, 128:256], 1, 0)
        gate = act[lo : lo + QB, 0:128].astype(F32)
        mean = jnp.sum(o, axis=1, keepdims=True) * (1.0 / HD)
        o = o - mean
        scale = lax.rsqrt(jnp.sum(o * o, axis=1, keepdims=True) * (1.0 / HD) + 1e-05)
        n = o * scale
        y_ref[lo : lo + QB, :] = (n * gate).astype(BF)
        dy = dot(gs[0][lo : lo + QB, :], wo[:, 0:128], 1, 1)
        for k in range(1, NT):
            dy = dy + dot(gs[k][lo : lo + QB, :], wo[:, k * 128 : (k + 1) * 128], 1, 1)
        dy = dy.astype(BF).astype(F32)
        dgate = (dy * n).astype(BF).astype(F32)
        dn = dy * gate
        m1 = jnp.sum(dn, axis=1, keepdims=True) * (1.0 / HD)
        m2 = jnp.sum(dn * n, axis=1, keepdims=True) * (1.0 / HD)
        do = ((dn - m1 - n * m2) * scale).astype(BF)
        dp_ref[lo : lo + QB, 0:128] = (dgate * pre[lo : lo + QB, 0:128]).astype(BF)
        dq = jnp.zeros((QB, HD), F32)
        for kb in range(k0, lo + QB, QB):
            at = kb - k0
            da = dot(do, act[kb : kb + QB, 128:256], 1, 1).astype(BF).astype(F32)
            ds = (da * dsil[:, at : at + QB]).astype(BF)
            dq = dq + dot(ds, act[kb : kb + QB, 384:512], 1, 0)
            dkv[kb : kb + QB, 0:128] += dot(aw[:, at : at + QB], do, 0, 0)
            dkv[kb : kb + QB, 128:256] += dot(ds, queries, 0, 0)
        dq = dq.astype(BF).astype(F32)
        dp_ref[lo : lo + QB, 256:384] = (dq * pre[lo : lo + QB, 256:384]).astype(BF)

    for q in range(TOK // QB):
        lo = q * QB
        dvb = dkv[lo : lo + QB, 0:128].astype(BF).astype(F32)
        dkb = dkv[lo : lo + QB, 128:256].astype(BF).astype(F32)
        dp_ref[lo : lo + QB, 128:256] = (dvb * pre[lo : lo + QB, 128:256]).astype(BF)
        dp_ref[lo : lo + QB, 384:512] = (dkb * pre[lo : lo + QB, 384:512]).astype(BF)
        du[...] = dot(dp_ref[lo : lo + QB, :], w[...], 1, 1).astype(BF).astype(F32)
        for r in range(0, QB, step):
            n, scale = stats(lo + r, step)
            d = [du[r : r + step, k * 128 : (k + 1) * 128] for k in range(NT)]
            m1 = jnp.sum(d[0] + d[1] + d[2] + d[3], axis=1, keepdims=True) * (1.0 / D)
            m2 = jnp.sum(
                d[0] * n[0] + d[1] * n[1] + d[2] * n[2] + d[3] * n[3], axis=1, keepdims=True
            ) * (1.0 / D)
            for k in range(NT):
                both[k][lo + r : lo + r + step, :] = ((d[k] - m1 - n[k] * m2) * scale).astype(BF)

    for k in range(NT):
        at = pl.multiple_of(lax.rem(me + k, NT) * 128, 128)
        dw = dot(u_ref[:, k * 128 : (k + 1) * 128], dp_ref[...], 0, 0)
        for c in range(4):
            dw_ref[pl.ds(pl.multiple_of(c * 512 + at, 128), 128), :] = dw[:, c * 128 : (c + 1) * 128]
        dw_ref[pl.ds(pl.multiple_of(2048 + at, 128), 128), :] = dot(y_ref[...], gs[k][...], 0, 0)
        both[k][TOK:, :] = dot(y_ref[...], wo[:, k * 128 : (k + 1) * 128], 1, 0).astype(BF)
    mine_ref[...] = dw_ref[pl.ds(pl.multiple_of(core * 1280, 1280), 1280), :]
    other_ref[...] = dw_ref[pl.ds(pl.multiple_of(1280 - core * 1280, 1280), 1280), :].astype(BF)


def layer(pos, core, seg, xs, gs, w_in, w_out):
    pair = jax.ShapeDtypeStruct((2 * TOK, 128), BF)
    return pl.pallas_call(
        layer_kernel,
        out_shape=(jax.ShapeDtypeStruct((1280, 128), F32), jax.ShapeDtypeStruct((1280, 128), BF))
        + (pair,) * 4,
        in_specs=[SM, SM] + [VM] * 11,
        out_specs=(VM,) * 6,
        scratch_shapes=[
            pltpu.VMEM((D, 512), BF),
            pltpu.VMEM((HD, D), BF),
            pltpu.VMEM((TOK, 512), F32),
            pltpu.VMEM((TOK, 512), BF),
            pltpu.VMEM((TOK, 128), F32),
            pltpu.VMEM((QB, 768), BF),
            pltpu.VMEM((QB, 768), F32),
            pltpu.VMEM((TOK, 256), F32),
            pltpu.VMEM((QB, 512), F32),
            pltpu.VMEM((TOK, D), BF),
            pltpu.VMEM((TOK, HD), BF),
            pltpu.VMEM((TOK, 512), BF),
            pltpu.VMEM((2560, 128), F32),
        ],
        compiler_params=PARAMS,
        name="layer",
    )(pos, core, seg, *xs, *gs, w_in, w_out)


def spread(at_ref, blocks, size, values):
    lows, highs, pairs = [], [], []
    for b in range(blocks):
        at = at_ref[b : b + 1, :]
        upper = column((at >= size).astype(F32)) > 0.5
        value = values[b * 128 : (b + 1) * 128, :]
        pairs.append(
            jnp.concatenate([jnp.where(upper, 0.0, value), jnp.where(upper, value, 0.0)], axis=1).astype(BF)
        )
        at = jnp.broadcast_to(jnp.where(at >= size, at - size, at), (128, 128))
        lows.append(((at & 127) == iota((128, 128), 0)).astype(F32).astype(BF))
        highs.append((at >> 7).astype(F32).astype(BF))
    low = jnp.concatenate(lows, axis=1)
    high = jnp.concatenate(highs, axis=1)
    pair = jnp.concatenate(pairs, axis=0)
    return [dot(hot_where(high, s, low), pair, 1, 0) for s in range(size // 128)]


def slots_kernel(slot_ref, grad_ref, d0, d1, d2, d3, out_ref):
    dx = grad_ref[...].astype(F32) + (
        d0[...].astype(F32) + d1[...].astype(F32) + d2[...].astype(F32) + d3[...].astype(F32)
    )
    half = SLOTS // 2
    for s, both in enumerate(spread(slot_ref, TOK // 128, half, dx)):
        out_ref[s * 128 : (s + 1) * 128, :] = both[:, :128].astype(BF)
        out_ref[half + s * 128 : half + (s + 1) * 128, :] = both[:, 128:].astype(BF)


def to_slots(slot, grad, parts):
    top = pl.BlockSpec((TOK, 128), lambda i: (0, 0))
    return pl.pallas_call(
        slots_kernel,
        out_shape=jax.ShapeDtypeStruct((SLOTS, 128), BF),
        grid=(1,),
        in_specs=[pl.BlockSpec((TOK // 128, 128), lambda i: (0, 0))] + [top] * 5,
        out_specs=pl.BlockSpec((SLOTS, 128), lambda i: (0, 0)),
        compiler_params=PARAMS,
        name="to_slots",
    )(slot, grad, *parts)


def add_rows_kernel(req_ref, arrived_ref, out_ref):
    half = ROWS // 2
    for s, both in enumerate(spread(req_ref, SLOTS // 128, half, arrived_ref[...].astype(F32))):
        out_ref[s * 128 : (s + 1) * 128, :] = both[:, :128]
        out_ref[half + s * 128 : half + (s + 1) * 128, :] = both[:, 128:]


def add_rows(req, arrived):
    return pl.pallas_call(
        add_rows_kernel,
        out_shape=jax.ShapeDtypeStruct((ROWS, 128), F32),
        in_specs=[VM, VM],
        out_specs=VM,
        compiler_params=PARAMS,
        name="add_rows",
    )(req, arrived)


def unpack_kernel(y_ref, p0, p1, p2, p3, in_ref, out_ref, whole):
    for k, p in enumerate((p0, p1, p2, p3)):
        half, quarter = y_place(lax.rem(y_ref[0] + k, 4))
        for core in range(2):
            at = pl.multiple_of(half * 640 + quarter * 320 + core * 1280, 320)
            whole[pl.ds(at, 320), :] = p[core * 320 : (core + 1) * 320, :].astype(F32)
    in_ref[...] = whole[0:2048, :]
    for k in range(NT):
        out_ref[:, k * 128 : (k + 1) * 128] = whole[2048 + k * 128 : 2176 + k * 128, :]


def unpack(y, parts):
    return pl.pallas_call(
        unpack_kernel,
        out_shape=(jax.ShapeDtypeStruct((2048, 128), F32), jax.ShapeDtypeStruct((HD, D), F32)),
        in_specs=[SM] + [VM] * 4,
        out_specs=(VM, VM),
        scratch_shapes=[pltpu.VMEM((2560, 128), F32)],
        compiler_params=PARAMS,
        name="unpack",
    )(y, *parts)


def shift(x, axis, fn, n):
    return lax.ppermute(x, axis, [(i, fn(i)) for i in range(n)])


def gather_pieces(x):
    return [x] + [shift(x, "tensor", lambda i, k=k: (i - k) % NT, NT) for k in (1, 3, 2)]


def order(pieces):
    own, one, three, two = pieces
    return [own, one, two, three]


def scatter_pieces(parts):
    return [parts[0]] + [shift(parts[k], "tensor", lambda i, k=k: (i + k) % NT, NT) for k in (1, 3, 2)]


def pick(x, i):
    return lax.dynamic_index_in_dim(x, i, 0, keepdims=False)


def y_place(y):
    return ((y == 1) | (y == 2)).astype(I32), (y >= 2).astype(I32)


def reduce_over_chips(mine, other):
    half, quarter = y_place(lax.axis_index("table") // 2)
    other = shift(other, "table", lambda i: i ^ 1, 8)
    mine = (mine + other.astype(F32)).reshape(2, 640, 128)
    got = shift(pick(mine, 1 - half).astype(BF), "table", lambda i: i ^ 2, 8)
    mine = (pick(mine, half) + got.astype(F32)).reshape(2, 320, 128)
    got = shift(pick(mine, 1 - quarter).astype(BF), "table", lambda i: 6 - (i & 6) + (i & 1), 8)
    return pick(mine, quarter), got


def add_step(total, mask):
    return (total.astype(F32) + shift(total, "seq", lambda i: i ^ mask, 8).astype(F32)).astype(BF)


def add_group(total):
    got = [shift(total, "seq", lambda i, k=k: i ^ k, 8) for k in (1, 2, 3)]
    for other in got:
        total = total.astype(F32) + other.astype(F32)
    return total.astype(BF)


def gather_weights(total, add):
    y = (lax.axis_index("table") // 2).astype(I32).reshape(1)
    pairs = [[2 * i, 2 * i + 1] for i in range(4)]
    both = lax.all_gather(total, "table", axis=0, tiled=True, axis_index_groups=pairs)
    parts = [both] + [shift(both, "table", lambda i, k=k: (i - 2 * k) % 8, 8) for k in range(1, 4)]
    table_grad = add()
    parts, table_grad = lax.optimization_barrier((parts, table_grad))
    return unpack(y, parts), table_grad


def body(table, owner, local_row, segment_ids, proj_in, proj_out, grad_out):
    pos = lax.axis_index("tensor").astype(I32).reshape(1)
    core = (lax.axis_index("table") % 2).astype(I32).reshape(1)
    requests, slot = route(owner.reshape(8, 128), local_row.reshape(8, 128))
    gs = order(gather_pieces(grad_out))
    received = lax.all_to_all(requests, BOTH, split_axis=0, concat_axis=0, tiled=True)
    rows = fetch(received, table)
    back = lax.all_to_all(rows.reshape(NOWN, CAP, 128), BOTH, split_axis=0, concat_axis=0, tiled=True)
    x = place(slot, back.reshape(SLOTS, 128))
    xs = order(gather_pieces(x))
    mine, other, c0, c1, c2, c3 = layer(pos, core, segment_ids, xs, gs, proj_in, proj_out)
    cparts = scatter_pieces([c0, c1, c2, c3])
    own, got = reduce_over_chips(mine, other)
    flat = received[:, :CAP].reshape(SLOTS // 128, 128)
    got, cparts[1] = lax.optimization_barrier((got, cparts[1]))
    total = add_group((own + got.astype(F32)).astype(BF))
    cparts, _, flat = lax.optimization_barrier((cparts, total, flat))
    grads = to_slots(slot, grad_out, cparts)
    total = add_step(total, 7)
    grads, total = lax.optimization_barrier((grads, total))
    arrived = lax.all_to_all(grads.reshape(NOWN, CAP, 128), BOTH, split_axis=0, concat_axis=0, tiled=True)
    (grad_in, grad_outw), table_grad = gather_weights(
        total, lambda: add_rows(flat, arrived.reshape(SLOTS, 128))
    )
    layer_out = (
        x.astype(F32)
        + (
            cparts[0][TOK:].astype(F32)
            + cparts[1][TOK:].astype(F32)
            + cparts[2][TOK:].astype(F32)
            + cparts[3][TOK:].astype(F32)
        )
    ).astype(BF)
    return layer_out, table_grad, grad_in.reshape(4, D, 128), grad_outw


def solution(mesh):
    in_specs = (
        P(BOTH, "tensor"),
        P(BOTH, None),
        P(BOTH),
        P(BOTH, None),
        P(None, None, "tensor"),
        P("tensor", None),
        P(BOTH, "tensor"),
    )
    out_specs = (
        P(BOTH, "tensor"),
        P(BOTH, "tensor"),
        P(None, None, "tensor"),
        P("tensor", None),
    )
    return jax.shard_map(body, mesh=mesh, in_specs=in_specs, out_specs=out_specs, check_vma=False)
```

```python
import functools

import jax
import jax.numpy as jnp
from jax import lax
from jax.experimental import pallas as pl
from jax.experimental.pallas import tpu as pltpu
from jax.sharding import PartitionSpec as P

HD = 128
SEQ_MOST = 512
TOK = 1024
D = 512
NT = 4
NOWN = 64
CAP = 24
SLOTS = NOWN * CAP
ROWS = 2048
QB = 256
BOTH = ("table", "seq")
FAR = (0, 1, 3, 2)
BF = jnp.bfloat16
F32 = jnp.float32
I32 = jnp.int32
VM = pl.BlockSpec(memory_space=pltpu.VMEM)
SM = pl.BlockSpec(memory_space=pltpu.SMEM)
PARAMS = pltpu.CompilerParams(vmem_limit_bytes=56 * 1024 * 1024)


def iota(shape, dim):
    return lax.broadcasted_iota(I32, shape, dim)


def dot(a, b, ca, cb):
    return lax.dot_general(a, b, (((ca,), (cb,)), ((), ())), preferred_element_type=F32)


def route_kernel(owner_ref, row_ref, req_ref, slot_ref):
    blocks = TOK // 128
    upper = (iota((128, 128), 0) < iota((128, 128), 1)).astype(BF)
    scan = jnp.concatenate([upper, jnp.ones((128, 128), BF)], axis=1)
    hots = [(iota((NOWN, 128), 0) == owner_ref[b : b + 1, :]).astype(F32) for b in range(blocks)]
    sums = dot(jnp.concatenate(hots, axis=0).astype(BF), scan, 1, 0)
    carry = jnp.zeros((NOWN, 128), F32)
    highs, lows = [], []
    for b in range(blocks):
        part = sums[b * NOWN : (b + 1) * NOWN, :]
        rank = jnp.sum(hots[b] * (part[:, :128] + carry), axis=0, keepdims=True).astype(I32)
        carry = carry + part[:, 128:]
        row = row_ref[b : b + 1, :]
        slot_ref[b : b + 1, :] = owner_ref[b : b + 1, :] * CAP + rank
        here = iota((32, 128), 0) == rank
        highs.append(jnp.where(here, (row >> 6).astype(F32), 0.0))
        lows.append(jnp.where(here, (row & 63).astype(F32), 0.0))
    hot = jnp.concatenate(hots, axis=1).astype(BF)
    high = dot(hot, jnp.concatenate(highs, axis=1).astype(BF), 1, 1)
    low = dot(hot, jnp.concatenate(lows, axis=1).astype(BF), 1, 1)
    req_ref[...] = jnp.zeros((NOWN, 128), I32)
    req_ref[:, 0:32] = (high * 64.0 + low).astype(I32)


def route(owner, row):
    return pl.pallas_call(
        route_kernel,
        out_shape=(
            jax.ShapeDtypeStruct((NOWN, 128), I32),
            jax.ShapeDtypeStruct((TOK // 128, 128), I32),
        ),
        in_specs=[VM, VM],
        out_specs=(VM, VM),
        compiler_params=PARAMS,
        name="route",
    )(owner, row)


def hot_where(high, value, low_hot):
    return jnp.where(high == value, low_hot, jnp.zeros_like(low_hot))


def fetch_kernel(req_ref, table_ref, out_ref, got):
    half = ROWS // 2
    both = jnp.concatenate([table_ref[:half, :], table_ref[half:, :]], axis=1)
    for c0 in range(0, CAP, 4):
        hots, uppers = [], []
        for c in range(c0, c0 + 4):
            row = jnp.broadcast_to(req_ref[:, c : c + 1], (NOWN, 128))
            low = ((row & 127) == iota((NOWN, 128), 1)).astype(F32).astype(BF)
            high = ((row >> 7) & 7).astype(F32).astype(BF)
            hots.append(jnp.concatenate([hot_where(high, j, low) for j in range(8)], axis=1))
            uppers.append(row >= half)
        pair = dot(jnp.concatenate(hots, axis=0), both, 1, 0)
        rows = jnp.where(jnp.concatenate(uppers, axis=0), pair[:, 128:], pair[:, :128])
        for i in range(4):
            got[pl.ds(c0 + i, NOWN, stride=CAP), :] = rows[i * NOWN : (i + 1) * NOWN, :]
    out_ref[...] = got[...].astype(BF)


def fetch(req, table):
    return pl.pallas_call(
        fetch_kernel,
        out_shape=jax.ShapeDtypeStruct((SLOTS, 128), BF),
        in_specs=[VM, VM],
        out_specs=VM,
        scratch_shapes=[pltpu.VMEM((SLOTS, 128), F32)],
        compiler_params=PARAMS,
        name="fetch",
    )(req, table)


def column(row_vector):
    wide = jnp.broadcast_to(row_vector.astype(F32), (128, 128))
    return jnp.transpose(wide)


def place_kernel(slot_ref, back_ref, x_ref):
    half = SLOTS // 2
    both = jnp.concatenate([back_ref[:half, :], back_ref[half:, :]], axis=1)
    for b0 in range(0, TOK // 128, 2):
        hots, uppers = [], []
        for b in (b0, b0 + 1):
            slot = column(slot_ref[b : b + 1, :]).astype(I32)
            upper = slot >= half
            slot = jnp.where(upper, slot - half, slot)
            low = ((slot & 127) == iota((128, 128), 1)).astype(F32).astype(BF)
            high = (slot >> 7).astype(F32).astype(BF)
            hots.append(jnp.concatenate([hot_where(high, j, low) for j in range(half // 128)], axis=1))
            uppers.append(upper)
        pair = dot(jnp.concatenate(hots, axis=0), both, 1, 0)
        rows = jnp.where(jnp.concatenate(uppers, axis=0), pair[:, 128:], pair[:, :128])
        x_ref[b0 * 128 : b0 * 128 + 256, :] = rows.astype(BF)


def place(slot, back):
    return pl.pallas_call(
        place_kernel,
        out_shape=jax.ShapeDtypeStruct((TOK, 128), BF),
        in_specs=[VM, VM],
        out_specs=VM,
        compiler_params=PARAMS,
        name="place",
    )(slot, back)


def layer_kernel(
    pos_ref, core_ref, seg_ref, x0, x1, x2, x3, g0, g1, g2, g3, win_ref, wout_ref,
    mine_ref, other_ref, c0, c1, c2, c3,
    w, wo, pre, act, segc, aw, dsil, dkv, du, u_ref, y_ref, dp_ref, dw_ref,
):
    xs, gs = (x0, x1, x2, x3), (g0, g1, g2, g3)
    both = (c0, c1, c2, c3)
    me, core = pos_ref[0], core_ref[0]
    for k in range(NT):
        at = pl.multiple_of(lax.rem(me + FAR[k], NT) * 128, 128)
        for c in range(4):
            w[k * 128 : (k + 1) * 128, c * 128 : (c + 1) * 128] = win_ref[c, pl.ds(at, 128), :]
        wo[:, k * 128 : (k + 1) * 128] = wout_ref[:, pl.ds(at, 128)]
    for b in range(TOK // 128):
        segc[b * 128 : (b + 1) * 128, :] = column(
            seg_ref[0:1, b * 128 : (b + 1) * 128]
        )

    def stats(r0, n):
        x = [r[r0 : r0 + n, :].astype(F32) for r in xs]
        mean = jnp.sum(x[0] + x[1] + x[2] + x[3], axis=1, keepdims=True) * (1.0 / D)
        x = [v - mean for v in x]
        var = jnp.sum(x[0] * x[0] + x[1] * x[1] + x[2] * x[2] + x[3] * x[3], axis=1, keepdims=True)
        scale = lax.rsqrt(var * (1.0 / D) + 1e-05)
        return [v * scale for v in x], scale

    step = 64
    for q in range(TOK // QB):
        lo = q * QB
        for r0 in range(lo, lo + QB, step):
            n, _ = stats(r0, step)
            for k in range(NT):
                u_ref[r0 : r0 + step, k * 128 : (k + 1) * 128] = n[k].astype(BF)
        pre[lo : lo + QB, :] = dot(u_ref[lo : lo + QB, :], w[...], 1, 0)
        for r0 in range(lo, lo + QB, step):
            p = pre[r0 : r0 + step, :]
            s = 0.5 + 0.5 * jnp.tanh(0.5 * p)
            ps = p * s
            act[r0 : r0 + step, :] = ps.astype(BF)
            pre[r0 : r0 + step, :] = s + ps * (1.0 - s)

    dkv[...] = jnp.zeros((TOK, 256), F32)
    for q in range(TOK // QB):
        lo = q * QB
        k0 = max(0, lo - SEQ_MOST)
        width = lo + QB - k0
        queries = act[lo : lo + QB, 256:384]
        o = jnp.zeros((QB, HD), F32)
        for kb in range(k0, lo + QB, QB):
            sc = dot(queries, act[kb : kb + QB, 384:512], 1, 1) * (HD ** (-0.5))
            for j in range(0, QB, 128):
                at = kb - k0 + j
                first, last = 0, QB
                if kb == lo and j:
                    first = j
                if lo - kb == SEQ_MOST and j + 128 < QB:
                    last = j + 128
                rows = slice(first, last)
                same = segc[lo + first : lo + last, :] == seg_ref[0:1, kb + j : kb + j + 128].astype(F32)
                if kb == lo:
                    shape = (last - first, 128)
                    same = same & (iota(shape, 1) + j <= iota(shape, 0) + first)
                v = sc[rows, j : j + 128]
                s = 0.5 + 0.5 * jnp.tanh(0.5 * v)
                vs = v * s
                aw[rows, at : at + 128] = jnp.where(same, vs * (1.0 / SEQ_MOST), 0.0).astype(BF)
                dsil[rows, at : at + 128] = jnp.where(
                    same, (s + vs * (1.0 - s)) * (HD ** (-0.5) / SEQ_MOST), 0.0
                )
                if first:
                    aw[0:first, at : at + 128] = jnp.zeros((first, 128), BF)
                    dsil[0:first, at : at + 128] = jnp.zeros((first, 128), F32)
                if last < QB:
                    aw[last:QB, at : at + 128] = jnp.zeros((QB - last, 128), BF)
                    dsil[last:QB, at : at + 128] = jnp.zeros((QB - last, 128), F32)
        o = dot(aw[:, 0:width], act[k0 : lo + QB, 128:256], 1, 0)
        gate = act[lo : lo + QB, 0:128].astype(F32)
        mean = jnp.sum(o, axis=1, keepdims=True) * (1.0 / HD)
        o = o - mean
        scale = lax.rsqrt(jnp.sum(o * o, axis=1, keepdims=True) * (1.0 / HD) + 1e-05)
        n = o * scale
        y_ref[lo : lo + QB, :] = (n * gate).astype(BF)
        dy = dot(gs[0][lo : lo + QB, :], wo[:, 0:128], 1, 1)
        for k in range(1, NT):
            dy = dy + dot(gs[k][lo : lo + QB, :], wo[:, k * 128 : (k + 1) * 128], 1, 1)
        dy = dy.astype(BF).astype(F32)
        dgate = (dy * n).astype(BF).astype(F32)
        dn = dy * gate
        m1 = jnp.sum(dn, axis=1, keepdims=True) * (1.0 / HD)
        m2 = jnp.sum(dn * n, axis=1, keepdims=True) * (1.0 / HD)
        do = ((dn - m1 - n * m2) * scale).astype(BF)
        dp_ref[lo : lo + QB, 0:128] = (dgate * pre[lo : lo + QB, 0:128]).astype(BF)
        dq = jnp.zeros((QB, HD), F32)
        for kb in range(k0, lo + QB, QB):
            at = kb - k0
            da = dot(do, act[kb : kb + QB, 128:256], 1, 1).astype(BF).astype(F32)
            ds = (da * dsil[:, at : at + QB]).astype(BF)
            dq = dq + dot(ds, act[kb : kb + QB, 384:512], 1, 0)
            dkv[kb : kb + QB, 0:128] += dot(aw[:, at : at + QB], do, 0, 0)
            dkv[kb : kb + QB, 128:256] += dot(ds, queries, 0, 0)
        dq = dq.astype(BF).astype(F32)
        dp_ref[lo : lo + QB, 256:384] = (dq * pre[lo : lo + QB, 256:384]).astype(BF)

    for q in range(TOK // QB):
        lo = q * QB
        dvb = dkv[lo : lo + QB, 0:128].astype(BF).astype(F32)
        dkb = dkv[lo : lo + QB, 128:256].astype(BF).astype(F32)
        dp_ref[lo : lo + QB, 128:256] = (dvb * pre[lo : lo + QB, 128:256]).astype(BF)
        dp_ref[lo : lo + QB, 384:512] = (dkb * pre[lo : lo + QB, 384:512]).astype(BF)
        du[...] = dot(dp_ref[lo : lo + QB, :], w[...], 1, 1).astype(BF).astype(F32)
        for r in range(0, QB, step):
            n, scale = stats(lo + r, step)
            d = [du[r : r + step, k * 128 : (k + 1) * 128] for k in range(NT)]
            m1 = jnp.sum(d[0] + d[1] + d[2] + d[3], axis=1, keepdims=True) * (1.0 / D)
            m2 = jnp.sum(
                d[0] * n[0] + d[1] * n[1] + d[2] * n[2] + d[3] * n[3], axis=1, keepdims=True
            ) * (1.0 / D)
            for k in range(NT):
                both[k][lo + r : lo + r + step, :] = ((d[k] - m1 - n[k] * m2) * scale).astype(BF)

    for k in range(NT):
        at = pl.multiple_of(lax.rem(me + FAR[k], NT) * 128, 128)
        dw = dot(u_ref[:, k * 128 : (k + 1) * 128], dp_ref[...], 0, 0)
        for c in range(4):
            dw_ref[pl.ds(pl.multiple_of(c * 512 + at, 128), 128), :] = dw[:, c * 128 : (c + 1) * 128]
        dw_ref[pl.ds(pl.multiple_of(2048 + at, 128), 128), :] = dot(y_ref[...], gs[k][...], 0, 0)
        both[k][TOK:, :] = dot(y_ref[...], wo[:, k * 128 : (k + 1) * 128], 1, 0).astype(BF)
    mine_ref[...] = dw_ref[pl.ds(pl.multiple_of(core * 1280, 1280), 1280), :]
    other_ref[...] = dw_ref[pl.ds(pl.multiple_of(1280 - core * 1280, 1280), 1280), :].astype(BF)


def layer(pos, core, seg, xs, gs, w_in, w_out):
    pair = jax.ShapeDtypeStruct((2 * TOK, 128), BF)
    return pl.pallas_call(
        layer_kernel,
        out_shape=(jax.ShapeDtypeStruct((1280, 128), F32), jax.ShapeDtypeStruct((1280, 128), BF))
        + (pair,) * 4,
        in_specs=[SM, SM] + [VM] * 11,
        out_specs=(VM,) * 6,
        scratch_shapes=[
            pltpu.VMEM((D, 512), BF),
            pltpu.VMEM((HD, D), BF),
            pltpu.VMEM((TOK, 512), F32),
            pltpu.VMEM((TOK, 512), BF),
            pltpu.VMEM((TOK, 128), F32),
            pltpu.VMEM((QB, 768), BF),
            pltpu.VMEM((QB, 768), F32),
            pltpu.VMEM((TOK, 256), F32),
            pltpu.VMEM((QB, 512), F32),
            pltpu.VMEM((TOK, D), BF),
            pltpu.VMEM((TOK, HD), BF),
            pltpu.VMEM((TOK, 512), BF),
            pltpu.VMEM((2560, 128), F32),
        ],
        compiler_params=PARAMS,
        name="layer",
    )(pos, core, seg, *xs, *gs, w_in, w_out)


def spread(at_ref, blocks, size, values):
    lows, highs, pairs = [], [], []
    for b in range(blocks):
        at = at_ref[b : b + 1, :]
        upper = column((at >= size).astype(F32)) > 0.5
        value = values[b * 128 : (b + 1) * 128, :]
        pairs.append(
            jnp.concatenate([jnp.where(upper, 0.0, value), jnp.where(upper, value, 0.0)], axis=1).astype(BF)
        )
        at = jnp.broadcast_to(jnp.where(at >= size, at - size, at), (128, 128))
        lows.append(((at & 127) == iota((128, 128), 0)).astype(F32).astype(BF))
        highs.append((at >> 7).astype(F32).astype(BF))
    low = jnp.concatenate(lows, axis=1)
    high = jnp.concatenate(highs, axis=1)
    pair = jnp.concatenate(pairs, axis=0)
    return [dot(hot_where(high, s, low), pair, 1, 0) for s in range(size // 128)]


def slots_kernel(slot_ref, grad_ref, d0, d1, d2, d3, out_ref):
    dx = grad_ref[...].astype(F32) + (
        d0[...].astype(F32) + d1[...].astype(F32) + d2[...].astype(F32) + d3[...].astype(F32)
    )
    half = SLOTS // 2
    for s, both in enumerate(spread(slot_ref, TOK // 128, half, dx)):
        out_ref[s * 128 : (s + 1) * 128, :] = both[:, :128].astype(BF)
        out_ref[half + s * 128 : half + (s + 1) * 128, :] = both[:, 128:].astype(BF)


def to_slots(slot, grad, parts):
    top = pl.BlockSpec((TOK, 128), lambda i: (0, 0))
    return pl.pallas_call(
        slots_kernel,
        out_shape=jax.ShapeDtypeStruct((SLOTS, 128), BF),
        grid=(1,),
        in_specs=[pl.BlockSpec((TOK // 128, 128), lambda i: (0, 0))] + [top] * 5,
        out_specs=pl.BlockSpec((SLOTS, 128), lambda i: (0, 0)),
        compiler_params=PARAMS,
        name="to_slots",
    )(slot, grad, *parts)


def add_rows_kernel(req_ref, arrived_ref, out_ref):
    half = ROWS // 2
    for s, both in enumerate(spread(req_ref, SLOTS // 128, half, arrived_ref[...].astype(F32))):
        out_ref[s * 128 : (s + 1) * 128, :] = both[:, :128]
        out_ref[half + s * 128 : half + (s + 1) * 128, :] = both[:, 128:]


def add_rows(req, arrived):
    return pl.pallas_call(
        add_rows_kernel,
        out_shape=jax.ShapeDtypeStruct((ROWS, 128), F32),
        in_specs=[VM, VM],
        out_specs=VM,
        compiler_params=PARAMS,
        name="add_rows",
    )(req, arrived)


def unpack_kernel(y_ref, p0, p1, p2, p3, in_ref, out_ref, whole):
    for k, p in enumerate((p0, p1, p2, p3)):
        half, quarter = y_place(lax.rem(y_ref[0] + FAR[k], 4))
        for core in range(2):
            at = pl.multiple_of(half * 640 + quarter * 320 + core * 1280, 320)
            whole[pl.ds(at, 320), :] = p[core * 320 : (core + 1) * 320, :].astype(F32)
    in_ref[...] = whole[0:2048, :]
    for k in range(NT):
        out_ref[:, k * 128 : (k + 1) * 128] = whole[2048 + k * 128 : 2176 + k * 128, :]


def unpack(y, parts):
    return pl.pallas_call(
        unpack_kernel,
        out_shape=(jax.ShapeDtypeStruct((2048, 128), F32), jax.ShapeDtypeStruct((HD, D), F32)),
        in_specs=[SM] + [VM] * 4,
        out_specs=(VM, VM),
        scratch_shapes=[pltpu.VMEM((2560, 128), F32)],
        compiler_params=PARAMS,
        name="unpack",
    )(y, *parts)


def shift(x, axis, fn, n):
    return lax.ppermute(x, axis, [(i, fn(i)) for i in range(n)])


def gather_pieces(x):
    return [x] + [shift(x, "tensor", lambda i, k=k: (i - k) % NT, NT) for k in FAR[1:]]


def scatter_pieces(parts):
    return [parts[0]] + [
        shift(parts[i], "tensor", lambda j, k=FAR[i]: (j + k) % NT, NT) for i in range(1, NT)
    ]


def pick(x, i):
    return lax.dynamic_index_in_dim(x, i, 0, keepdims=False)


def y_place(y):
    return ((y == 1) | (y == 2)).astype(I32), (y >= 2).astype(I32)


def reduce_over_chips(mine, other):
    half, quarter = y_place(lax.axis_index("table") // 2)
    other = shift(other, "table", lambda i: i ^ 1, 8)
    mine = (mine + other.astype(F32)).reshape(2, 640, 128)
    got = shift(pick(mine, 1 - half).astype(BF), "table", lambda i: i ^ 2, 8)
    mine = (pick(mine, half) + got.astype(F32)).reshape(2, 320, 128)
    got = shift(pick(mine, 1 - quarter).astype(BF), "table", lambda i: 6 - (i & 6) + (i & 1), 8)
    return pick(mine, quarter), got


def add_step(total, mask):
    return (total.astype(F32) + shift(total, "seq", lambda i: i ^ mask, 8).astype(F32)).astype(BF)


def add_group(total):
    got = [shift(total, "seq", lambda i, k=k: i ^ k, 8) for k in (1, 2, 3)]
    for other in got:
        total = total.astype(F32) + other.astype(F32)
    return total.astype(BF)


def gather_weights(total, add):
    y = (lax.axis_index("table") // 2).astype(I32).reshape(1)
    pairs = [[2 * i, 2 * i + 1] for i in range(4)]
    both = lax.all_gather(total, "table", axis=0, tiled=True, axis_index_groups=pairs)
    parts = [both] + [shift(both, "table", lambda i, k=k: (i - 2 * k) % 8, 8) for k in FAR[1:]]
    table_grad = add()
    parts, table_grad = lax.optimization_barrier((parts, table_grad))
    return unpack(y, parts), table_grad


def body(table, owner, local_row, segment_ids, proj_in, proj_out, grad_out):
    pos = lax.axis_index("tensor").astype(I32).reshape(1)
    core = (lax.axis_index("table") % 2).astype(I32).reshape(1)
    requests, slot = route(owner.reshape(8, 128), local_row.reshape(8, 128))
    gs = gather_pieces(grad_out)
    received = lax.all_to_all(requests, BOTH, split_axis=0, concat_axis=0, tiled=True)
    rows = fetch(received, table)
    back = lax.all_to_all(rows.reshape(NOWN, CAP, 128), BOTH, split_axis=0, concat_axis=0, tiled=True)
    x = place(slot, back.reshape(SLOTS, 128))
    xs = gather_pieces(x)
    mine, other, c0, c1, c2, c3 = layer(pos, core, segment_ids, xs, gs, proj_in, proj_out)
    cparts = scatter_pieces([c0, c1, c2, c3])
    own, got = reduce_over_chips(mine, other)
    flat = received[:, :CAP].reshape(SLOTS // 128, 128)
    got, cparts[3] = lax.optimization_barrier((got, cparts[3]))
    total = add_group((own + got.astype(F32)).astype(BF))
    cparts, _, flat = lax.optimization_barrier((cparts, total, flat))
    grads = to_slots(slot, grad_out, cparts)
    total = add_step(total, 7)
    grads, total = lax.optimization_barrier((grads, total))
    arrived = lax.all_to_all(grads.reshape(NOWN, CAP, 128), BOTH, split_axis=0, concat_axis=0, tiled=True)
    (grad_in, grad_outw), table_grad = gather_weights(
        total, lambda: add_rows(flat, arrived.reshape(SLOTS, 128))
    )
    layer_out = (
        x.astype(F32)
        + (
            cparts[0][TOK:].astype(F32)
            + cparts[1][TOK:].astype(F32)
            + cparts[2][TOK:].astype(F32)
            + cparts[3][TOK:].astype(F32)
        )
    ).astype(BF)
    return layer_out, table_grad, grad_in.reshape(4, D, 128), grad_outw


def solution(mesh):
    in_specs = (
        P(BOTH, "tensor"),
        P(BOTH, None),
        P(BOTH),
        P(BOTH, None),
        P(None, None, "tensor"),
        P("tensor", None),
        P(BOTH, "tensor"),
    )
    out_specs = (
        P(BOTH, "tensor"),
        P(BOTH, "tensor"),
        P(None, None, "tensor"),
        P("tensor", None),
    )
    return jax.shard_map(body, mesh=mesh, in_specs=in_specs, out_specs=out_specs, check_vma=False)
```

```python
import functools

import jax
import jax.numpy as jnp
from jax import lax
from jax.experimental import pallas as pl
from jax.experimental.pallas import tpu as pltpu
from jax.sharding import PartitionSpec as P

HD = 128
SEQ_MOST = 512
TOK = 1024
D = 512
NT = 4
NOWN = 64
CAP = 24
SLOTS = NOWN * CAP
ROWS = 2048
QB = 256
BOTH = ("table", "seq")
FAR = (0, 1, 3, 2)
BF = jnp.bfloat16
F32 = jnp.float32
I32 = jnp.int32
VM = pl.BlockSpec(memory_space=pltpu.VMEM)
SM = pl.BlockSpec(memory_space=pltpu.SMEM)
PARAMS = pltpu.CompilerParams(vmem_limit_bytes=56 * 1024 * 1024)


def iota(shape, dim):
    return lax.broadcasted_iota(I32, shape, dim)


def dot(a, b, ca, cb):
    return lax.dot_general(a, b, (((ca,), (cb,)), ((), ())), preferred_element_type=F32)


def route_kernel(owner_ref, row_ref, req_ref, slot_ref):
    blocks = TOK // 128
    upper = (iota((128, 128), 0) < iota((128, 128), 1)).astype(BF)
    scan = jnp.concatenate([upper, jnp.ones((128, 128), BF)], axis=1)
    hots = [(iota((NOWN, 128), 0) == owner_ref[b : b + 1, :]).astype(F32) for b in range(blocks)]
    sums = dot(jnp.concatenate(hots, axis=0).astype(BF), scan, 1, 0)
    carry = jnp.zeros((NOWN, 128), F32)
    highs, lows = [], []
    for b in range(blocks):
        part = sums[b * NOWN : (b + 1) * NOWN, :]
        rank = jnp.sum(hots[b] * (part[:, :128] + carry), axis=0, keepdims=True).astype(I32)
        carry = carry + part[:, 128:]
        row = row_ref[b : b + 1, :]
        slot_ref[b : b + 1, :] = owner_ref[b : b + 1, :] * CAP + rank
        here = iota((32, 128), 0) == rank
        highs.append(jnp.where(here, (row >> 6).astype(F32), 0.0))
        lows.append(jnp.where(here, (row & 63).astype(F32), 0.0))
    hot = jnp.concatenate(hots, axis=1).astype(BF)
    high = dot(hot, jnp.concatenate(highs, axis=1).astype(BF), 1, 1)
    low = dot(hot, jnp.concatenate(lows, axis=1).astype(BF), 1, 1)
    req_ref[...] = jnp.zeros((NOWN, 128), I32)
    req_ref[:, 0:32] = (high * 64.0 + low).astype(I32)


def route(owner, row):
    return pl.pallas_call(
        route_kernel,
        out_shape=(
            jax.ShapeDtypeStruct((NOWN, 128), I32),
            jax.ShapeDtypeStruct((TOK // 128, 128), I32),
        ),
        in_specs=[VM, VM],
        out_specs=(VM, VM),
        compiler_params=PARAMS,
        name="route",
    )(owner, row)


def hot_where(high, value, low_hot):
    return jnp.where(high == value, low_hot, jnp.zeros_like(low_hot))


def fetch_kernel(req_ref, table_ref, out_ref, got):
    half = ROWS // 2
    both = jnp.concatenate([table_ref[:half, :], table_ref[half:, :]], axis=1)
    for c0 in range(0, CAP, 4):
        hots, uppers = [], []
        for c in range(c0, c0 + 4):
            row = jnp.broadcast_to(req_ref[:, c : c + 1], (NOWN, 128))
            low = ((row & 127) == iota((NOWN, 128), 1)).astype(F32).astype(BF)
            high = ((row >> 7) & 7).astype(F32).astype(BF)
            hots.append(jnp.concatenate([hot_where(high, j, low) for j in range(8)], axis=1))
            uppers.append(row >= half)
        pair = dot(jnp.concatenate(hots, axis=0), both, 1, 0)
        rows = jnp.where(jnp.concatenate(uppers, axis=0), pair[:, 128:], pair[:, :128])
        for i in range(4):
            got[pl.ds(c0 + i, NOWN, stride=CAP), :] = rows[i * NOWN : (i + 1) * NOWN, :]
    out_ref[...] = got[...].astype(BF)


def fetch(req, table):
    return pl.pallas_call(
        fetch_kernel,
        out_shape=jax.ShapeDtypeStruct((SLOTS, 128), BF),
        in_specs=[VM, VM],
        out_specs=VM,
        scratch_shapes=[pltpu.VMEM((SLOTS, 128), F32)],
        compiler_params=PARAMS,
        name="fetch",
    )(req, table)


def column(row_vector):
    wide = jnp.broadcast_to(row_vector.astype(F32), (128, 128))
    return jnp.transpose(wide)


def place_kernel(slot_ref, back_ref, x_ref):
    half = SLOTS // 2
    both = jnp.concatenate([back_ref[:half, :], back_ref[half:, :]], axis=1)
    for b0 in range(0, TOK // 128, 2):
        hots, uppers = [], []
        for b in (b0, b0 + 1):
            slot = column(slot_ref[b : b + 1, :]).astype(I32)
            upper = slot >= half
            slot = jnp.where(upper, slot - half, slot)
            low = ((slot & 127) == iota((128, 128), 1)).astype(F32).astype(BF)
            high = (slot >> 7).astype(F32).astype(BF)
            hots.append(jnp.concatenate([hot_where(high, j, low) for j in range(half // 128)], axis=1))
            uppers.append(upper)
        pair = dot(jnp.concatenate(hots, axis=0), both, 1, 0)
        rows = jnp.where(jnp.concatenate(uppers, axis=0), pair[:, 128:], pair[:, :128])
        x_ref[b0 * 128 : b0 * 128 + 256, :] = rows.astype(BF)


def place(slot, back):
    return pl.pallas_call(
        place_kernel,
        out_shape=jax.ShapeDtypeStruct((TOK, 128), BF),
        in_specs=[VM, VM],
        out_specs=VM,
        compiler_params=PARAMS,
        name="place",
    )(slot, back)


def layer_kernel(
    pos_ref, core_ref, seg_ref, x0, x1, x2, x3, g0, g1, g2, g3, win_ref, wout_ref,
    mine_ref, other_ref, c0, c1, c2, c3,
    w, wo, pre, act, segc, aw, dsil, dkv, du, u_ref, y_ref, dp_ref, dw_ref,
):
    xs, gs = (x0, x1, x2, x3), (g0, g1, g2, g3)
    both = (c0, c1, c2, c3)
    me, core = pos_ref[0], core_ref[0]
    for k in range(NT):
        at = pl.multiple_of(lax.rem(me + FAR[k], NT) * 128, 128)
        for c in range(4):
            w[k * 128 : (k + 1) * 128, c * 128 : (c + 1) * 128] = win_ref[c, pl.ds(at, 128), :]
        wo[:, k * 128 : (k + 1) * 128] = wout_ref[:, pl.ds(at, 128)]
    for b in range(TOK // 128):
        segc[b * 128 : (b + 1) * 128, :] = column(
            seg_ref[0:1, b * 128 : (b + 1) * 128]
        )

    def stats(r0, n):
        x = [r[r0 : r0 + n, :].astype(F32) for r in xs]
        mean = jnp.sum(x[0] + x[1] + x[2] + x[3], axis=1, keepdims=True) * (1.0 / D)
        x = [v - mean for v in x]
        var = jnp.sum(x[0] * x[0] + x[1] * x[1] + x[2] * x[2] + x[3] * x[3], axis=1, keepdims=True)
        scale = lax.rsqrt(var * (1.0 / D) + 1e-05)
        return [v * scale for v in x], scale

    step = 64
    for q in range(TOK // QB):
        lo = q * QB
        for r0 in range(lo, lo + QB, step):
            n, _ = stats(r0, step)
            for k in range(NT):
                u_ref[r0 : r0 + step, k * 128 : (k + 1) * 128] = n[k].astype(BF)
        pre[lo : lo + QB, :] = dot(u_ref[lo : lo + QB, :], w[...], 1, 0)
        for r0 in range(lo, lo + QB, step):
            p = pre[r0 : r0 + step, :]
            s = 0.5 + 0.5 * jnp.tanh(0.5 * p)
            ps = p * s
            act[r0 : r0 + step, :] = ps.astype(BF)
            pre[r0 : r0 + step, :] = s + ps * (1.0 - s)

    dkv[...] = jnp.zeros((TOK, 256), F32)
    for q in range(TOK // QB):
        lo = q * QB
        k0 = max(0, lo - SEQ_MOST)
        width = lo + QB - k0
        queries = act[lo : lo + QB, 256:384]
        o = jnp.zeros((QB, HD), F32)
        for kb in range(k0, lo + QB, QB):
            sc = dot(queries, act[kb : kb + QB, 384:512], 1, 1) * (HD ** (-0.5))
            for j in range(0, QB, 128):
                at = kb - k0 + j
                first, last = 0, QB
                if kb == lo and j:
                    first = j
                if lo - kb == SEQ_MOST and j + 128 < QB:
                    last = j + 128
                rows = slice(first, last)
                same = segc[lo + first : lo + last, :] == seg_ref[0:1, kb + j : kb + j + 128].astype(F32)
                if kb == lo:
                    shape = (last - first, 128)
                    same = same & (iota(shape, 1) + j <= iota(shape, 0) + first)
                v = sc[rows, j : j + 128]
                s = 0.5 + 0.5 * jnp.tanh(0.5 * v)
                vs = v * s
                aw[rows, at : at + 128] = jnp.where(same, vs * (1.0 / SEQ_MOST), 0.0).astype(BF)
                dsil[rows, at : at + 128] = jnp.where(
                    same, (s + vs * (1.0 - s)) * (HD ** (-0.5) / SEQ_MOST), 0.0
                )
                if first:
                    aw[0:first, at : at + 128] = jnp.zeros((first, 128), BF)
                    dsil[0:first, at : at + 128] = jnp.zeros((first, 128), F32)
                if last < QB:
                    aw[last:QB, at : at + 128] = jnp.zeros((QB - last, 128), BF)
                    dsil[last:QB, at : at + 128] = jnp.zeros((QB - last, 128), F32)
        o = dot(aw[:, 0:width], act[k0 : lo + QB, 128:256], 1, 0)
        gate = act[lo : lo + QB, 0:128].astype(F32)
        mean = jnp.sum(o, axis=1, keepdims=True) * (1.0 / HD)
        o = o - mean
        scale = lax.rsqrt(jnp.sum(o * o, axis=1, keepdims=True) * (1.0 / HD) + 1e-05)
        n = o * scale
        y_ref[lo : lo + QB, :] = (n * gate).astype(BF)
        dy = dot(gs[0][lo : lo + QB, :], wo[:, 0:128], 1, 1)
        for k in range(1, NT):
            dy = dy + dot(gs[k][lo : lo + QB, :], wo[:, k * 128 : (k + 1) * 128], 1, 1)
        dy = dy.astype(BF).astype(F32)
        dgate = (dy * n).astype(BF).astype(F32)
        dn = dy * gate
        m1 = jnp.sum(dn, axis=1, keepdims=True) * (1.0 / HD)
        m2 = jnp.sum(dn * n, axis=1, keepdims=True) * (1.0 / HD)
        do = ((dn - m1 - n * m2) * scale).astype(BF)
        dp_ref[lo : lo + QB, 0:128] = (dgate * pre[lo : lo + QB, 0:128]).astype(BF)
        dq = jnp.zeros((QB, HD), F32)
        for kb in range(k0, lo + QB, QB):
            at = kb - k0
            da = dot(do, act[kb : kb + QB, 128:256], 1, 1).astype(BF).astype(F32)
            ds = (da * dsil[:, at : at + QB]).astype(BF)
            dq = dq + dot(ds, act[kb : kb + QB, 384:512], 1, 0)
            dkv[kb : kb + QB, 0:128] += dot(aw[:, at : at + QB], do, 0, 0)
            dkv[kb : kb + QB, 128:256] += dot(ds, queries, 0, 0)
        dq = dq.astype(BF).astype(F32)
        dp_ref[lo : lo + QB, 256:384] = (dq * pre[lo : lo + QB, 256:384]).astype(BF)

    for q in range(TOK // QB):
        lo = q * QB
        dvb = dkv[lo : lo + QB, 0:128].astype(BF).astype(F32)
        dkb = dkv[lo : lo + QB, 128:256].astype(BF).astype(F32)
        dp_ref[lo : lo + QB, 128:256] = (dvb * pre[lo : lo + QB, 128:256]).astype(BF)
        dp_ref[lo : lo + QB, 384:512] = (dkb * pre[lo : lo + QB, 384:512]).astype(BF)
        du[...] = dot(dp_ref[lo : lo + QB, :], w[...], 1, 1).astype(BF).astype(F32)
        for r in range(0, QB, step):
            n, scale = stats(lo + r, step)
            d = [du[r : r + step, k * 128 : (k + 1) * 128] for k in range(NT)]
            m1 = jnp.sum(d[0] + d[1] + d[2] + d[3], axis=1, keepdims=True) * (1.0 / D)
            m2 = jnp.sum(
                d[0] * n[0] + d[1] * n[1] + d[2] * n[2] + d[3] * n[3], axis=1, keepdims=True
            ) * (1.0 / D)
            for k in range(NT):
                both[k][lo + r : lo + r + step, :] = ((d[k] - m1 - n[k] * m2) * scale).astype(BF)

    for k in range(NT):
        at = pl.multiple_of(lax.rem(me + FAR[k], NT) * 128, 128)
        dw = dot(u_ref[:, k * 128 : (k + 1) * 128], dp_ref[...], 0, 0)
        for c in range(4):
            dw_ref[pl.ds(pl.multiple_of(c * 512 + at, 128), 128), :] = dw[:, c * 128 : (c + 1) * 128]
        dw_ref[pl.ds(pl.multiple_of(2048 + at, 128), 128), :] = dot(y_ref[...], gs[k][...], 0, 0)
        both[k][TOK:, :] = dot(y_ref[...], wo[:, k * 128 : (k + 1) * 128], 1, 0).astype(BF)
    mine_ref[...] = dw_ref[pl.ds(pl.multiple_of(core * 1280, 1280), 1280), :]
    other_ref[...] = dw_ref[pl.ds(pl.multiple_of(1280 - core * 1280, 1280), 1280), :].astype(BF)


def layer(pos, core, seg, xs, gs, w_in, w_out):
    pair = jax.ShapeDtypeStruct((2 * TOK, 128), BF)
    return pl.pallas_call(
        layer_kernel,
        out_shape=(jax.ShapeDtypeStruct((1280, 128), F32), jax.ShapeDtypeStruct((1280, 128), BF))
        + (pair,) * 4,
        in_specs=[SM, SM] + [VM] * 11,
        out_specs=(VM,) * 6,
        scratch_shapes=[
            pltpu.VMEM((D, 512), BF),
            pltpu.VMEM((HD, D), BF),
            pltpu.VMEM((TOK, 512), F32),
            pltpu.VMEM((TOK, 512), BF),
            pltpu.VMEM((TOK, 128), F32),
            pltpu.VMEM((QB, 768), BF),
            pltpu.VMEM((QB, 768), F32),
            pltpu.VMEM((TOK, 256), F32),
            pltpu.VMEM((QB, 512), F32),
            pltpu.VMEM((TOK, D), BF),
            pltpu.VMEM((TOK, HD), BF),
            pltpu.VMEM((TOK, 512), BF),
            pltpu.VMEM((2560, 128), F32),
        ],
        compiler_params=PARAMS,
        name="layer",
    )(pos, core, seg, *xs, *gs, w_in, w_out)


def spread(at_ref, blocks, size, values):
    lows, highs, pairs = [], [], []
    for b in range(blocks):
        at = at_ref[b : b + 1, :]
        upper = column((at >= size).astype(F32)) > 0.5
        value = values[b * 128 : (b + 1) * 128, :]
        pairs.append(
            jnp.concatenate([jnp.where(upper, 0.0, value), jnp.where(upper, value, 0.0)], axis=1).astype(BF)
        )
        at = jnp.broadcast_to(jnp.where(at >= size, at - size, at), (128, 128))
        lows.append(((at & 127) == iota((128, 128), 0)).astype(F32).astype(BF))
        highs.append((at >> 7).astype(F32).astype(BF))
    low = jnp.concatenate(lows, axis=1)
    high = jnp.concatenate(highs, axis=1)
    pair = jnp.concatenate(pairs, axis=0)
    return [dot(hot_where(high, s, low), pair, 1, 0) for s in range(size // 128)]


def slots_kernel(slot_ref, grad_ref, d0, d1, d2, d3, out_ref):
    dx = grad_ref[...].astype(F32) + (
        d0[...].astype(F32) + d1[...].astype(F32) + d2[...].astype(F32) + d3[...].astype(F32)
    )
    half = SLOTS // 2
    for s, both in enumerate(spread(slot_ref, TOK // 128, half, dx)):
        out_ref[s * 128 : (s + 1) * 128, :] = both[:, :128].astype(BF)
        out_ref[half + s * 128 : half + (s + 1) * 128, :] = both[:, 128:].astype(BF)


def to_slots(slot, grad, parts):
    top = pl.BlockSpec((TOK, 128), lambda i: (0, 0))
    return pl.pallas_call(
        slots_kernel,
        out_shape=jax.ShapeDtypeStruct((SLOTS, 128), BF),
        grid=(1,),
        in_specs=[pl.BlockSpec((TOK // 128, 128), lambda i: (0, 0))] + [top] * 5,
        out_specs=pl.BlockSpec((SLOTS, 128), lambda i: (0, 0)),
        compiler_params=PARAMS,
        name="to_slots",
    )(slot, grad, *parts)


def add_rows_kernel(req_ref, arrived_ref, out_ref):
    half = ROWS // 2
    for s, both in enumerate(spread(req_ref, SLOTS // 128, half, arrived_ref[...].astype(F32))):
        out_ref[s * 128 : (s + 1) * 128, :] = both[:, :128]
        out_ref[half + s * 128 : half + (s + 1) * 128, :] = both[:, 128:]


def add_rows(req, arrived):
    return pl.pallas_call(
        add_rows_kernel,
        out_shape=jax.ShapeDtypeStruct((ROWS, 128), F32),
        in_specs=[VM, VM],
        out_specs=VM,
        compiler_params=PARAMS,
        name="add_rows",
    )(req, arrived)


def unpack_kernel(y_ref, p0, p1, p2, p3, in_ref, out_ref, whole):
    for k, p in enumerate((p0, p1, p2, p3)):
        half, quarter = y_place(lax.rem(y_ref[0] + FAR[k], 4))
        for core in range(2):
            at = pl.multiple_of(half * 640 + quarter * 320 + core * 1280, 320)
            whole[pl.ds(at, 320), :] = p[core * 320 : (core + 1) * 320, :].astype(F32)
    in_ref[...] = whole[0:2048, :]
    for k in range(NT):
        out_ref[:, k * 128 : (k + 1) * 128] = whole[2048 + k * 128 : 2176 + k * 128, :]


def unpack(y, parts):
    return pl.pallas_call(
        unpack_kernel,
        out_shape=(jax.ShapeDtypeStruct((2048, 128), F32), jax.ShapeDtypeStruct((HD, D), F32)),
        in_specs=[SM] + [VM] * 4,
        out_specs=(VM, VM),
        scratch_shapes=[pltpu.VMEM((2560, 128), F32)],
        compiler_params=PARAMS,
        name="unpack",
    )(y, *parts)


def shift(x, axis, fn, n):
    return lax.ppermute(x, axis, [(i, fn(i)) for i in range(n)])


def gather_pieces(x):
    return [x] + [shift(x, "tensor", lambda i, k=k: (i - k) % NT, NT) for k in FAR[1:]]


def scatter_pieces(parts):
    return [parts[0]] + [
        shift(parts[i], "tensor", lambda j, k=FAR[i]: (j + k) % NT, NT) for i in range(1, NT)
    ]


def pick(x, i):
    return lax.dynamic_index_in_dim(x, i, 0, keepdims=False)


def y_place(y):
    return ((y == 1) | (y == 2)).astype(I32), (y >= 2).astype(I32)


def reduce_over_chips(mine, other, far):
    half, quarter = y_place(lax.axis_index("table") // 2)
    other = shift(other, "table", lambda i: i ^ 1, 8)
    mine = (mine + other.astype(F32)).reshape(2, 640, 128)
    got = shift(pick(mine, 1 - half).astype(BF), "table", lambda i: i ^ 2, 8)
    got, far = lax.optimization_barrier((got, far))
    mine = (pick(mine, half) + got.astype(F32)).reshape(2, 320, 128)
    got = shift(pick(mine, 1 - quarter).astype(BF), "table", lambda i: 6 - (i & 6) + (i & 1), 8)
    return pick(mine, quarter), got, far


def add_step(total, mask):
    return (total.astype(F32) + shift(total, "seq", lambda i: i ^ mask, 8).astype(F32)).astype(BF)


def add_group(total):
    got = [shift(total, "seq", lambda i, k=k: i ^ k, 8) for k in (1, 2, 3)]
    for other in got:
        total = total.astype(F32) + other.astype(F32)
    return total.astype(BF)


def gather_weights(total, add):
    y = (lax.axis_index("table") // 2).astype(I32).reshape(1)
    pairs = [[2 * i, 2 * i + 1] for i in range(4)]
    both = lax.all_gather(total, "table", axis=0, tiled=True, axis_index_groups=pairs)
    parts = [both] + [shift(both, "table", lambda i, k=k: (i - 2 * k) % 8, 8) for k in FAR[1:]]
    table_grad = add()
    parts, table_grad = lax.optimization_barrier((parts, table_grad))
    return unpack(y, parts), table_grad


def body(table, owner, local_row, segment_ids, proj_in, proj_out, grad_out):
    pos = lax.axis_index("tensor").astype(I32).reshape(1)
    core = (lax.axis_index("table") % 2).astype(I32).reshape(1)
    requests, slot = route(owner.reshape(8, 128), local_row.reshape(8, 128))
    gs = gather_pieces(grad_out)
    received = lax.all_to_all(requests, BOTH, split_axis=0, concat_axis=0, tiled=True)
    rows = fetch(received, table)
    back = lax.all_to_all(rows.reshape(NOWN, CAP, 128), BOTH, split_axis=0, concat_axis=0, tiled=True)
    x = place(slot, back.reshape(SLOTS, 128))
    xs = gather_pieces(x)
    mine, other, c0, c1, c2, c3 = layer(pos, core, segment_ids, xs, gs, proj_in, proj_out)
    cparts = scatter_pieces([c0, c1, c2, c3])
    own, got, cparts[3] = reduce_over_chips(mine, other, cparts[3])
    flat = received[:, :CAP].reshape(SLOTS // 128, 128)
    total = add_group((own + got.astype(F32)).astype(BF))
    cparts, _, flat = lax.optimization_barrier((cparts, total, flat))
    grads = to_slots(slot, grad_out, cparts)
    total = add_step(total, 7)
    grads, total = lax.optimization_barrier((grads, total))
    arrived = lax.all_to_all(grads.reshape(NOWN, CAP, 128), BOTH, split_axis=0, concat_axis=0, tiled=True)
    (grad_in, grad_outw), table_grad = gather_weights(
        total, lambda: add_rows(flat, arrived.reshape(SLOTS, 128))
    )
    layer_out = (
        x.astype(F32)
        + (
            cparts[0][TOK:].astype(F32)
            + cparts[1][TOK:].astype(F32)
            + cparts[2][TOK:].astype(F32)
            + cparts[3][TOK:].astype(F32)
        )
    ).astype(BF)
    return layer_out, table_grad, grad_in.reshape(4, D, 128), grad_outw


def solution(mesh):
    in_specs = (
        P(BOTH, "tensor"),
        P(BOTH, None),
        P(BOTH),
        P(BOTH, None),
        P(None, None, "tensor"),
        P("tensor", None),
        P(BOTH, "tensor"),
    )
    out_specs = (
        P(BOTH, "tensor"),
        P(BOTH, "tensor"),
        P(None, None, "tensor"),
        P("tensor", None),
    )
    return jax.shard_map(body, mesh=mesh, in_specs=in_specs, out_specs=out_specs, check_vma=False)
```

```python
import functools

import jax
import jax.numpy as jnp
from jax import lax
from jax.experimental import pallas as pl
from jax.experimental.pallas import tpu as pltpu
from jax.sharding import PartitionSpec as P

HD = 128
SEQ_MOST = 512
TOK = 1024
D = 512
NT = 4
NOWN = 64
CAP = 24
SLOTS = NOWN * CAP
ROWS = 2048
QB = 256
BOTH = ("table", "seq")
FAR = (0, 1, 3, 2)
BF = jnp.bfloat16
F32 = jnp.float32
I32 = jnp.int32
VM = pl.BlockSpec(memory_space=pltpu.VMEM)
SM = pl.BlockSpec(memory_space=pltpu.SMEM)
PARAMS = pltpu.CompilerParams(vmem_limit_bytes=56 * 1024 * 1024)


def iota(shape, dim):
    return lax.broadcasted_iota(I32, shape, dim)


def dot(a, b, ca, cb):
    return lax.dot_general(a, b, (((ca,), (cb,)), ((), ())), preferred_element_type=F32)


def route_kernel(owner_ref, row_ref, req_ref, slot_ref):
    blocks = TOK // 128
    upper = (iota((128, 128), 0) < iota((128, 128), 1)).astype(BF)
    scan = jnp.concatenate([upper, jnp.ones((128, 128), BF)], axis=1)
    hots = [(iota((NOWN, 128), 0) == owner_ref[b : b + 1, :]).astype(F32) for b in range(blocks)]
    sums = dot(jnp.concatenate(hots, axis=0).astype(BF), scan, 1, 0)
    carry = jnp.zeros((NOWN, 128), F32)
    highs, lows = [], []
    for b in range(blocks):
        part = sums[b * NOWN : (b + 1) * NOWN, :]
        rank = jnp.sum(hots[b] * (part[:, :128] + carry), axis=0, keepdims=True).astype(I32)
        carry = carry + part[:, 128:]
        row = row_ref[b : b + 1, :]
        slot_ref[b : b + 1, :] = owner_ref[b : b + 1, :] * CAP + rank
        here = iota((32, 128), 0) == rank
        highs.append(jnp.where(here, (row >> 6).astype(F32), 0.0))
        lows.append(jnp.where(here, (row & 63).astype(F32), 0.0))
    hot = jnp.concatenate(hots, axis=1).astype(BF)
    high = dot(hot, jnp.concatenate(highs, axis=1).astype(BF), 1, 1)
    low = dot(hot, jnp.concatenate(lows, axis=1).astype(BF), 1, 1)
    req_ref[...] = jnp.zeros((NOWN, 128), I32)
    req_ref[:, 0:32] = (high * 64.0 + low).astype(I32)


def route(owner, row):
    return pl.pallas_call(
        route_kernel,
        out_shape=(
            jax.ShapeDtypeStruct((NOWN, 128), I32),
            jax.ShapeDtypeStruct((TOK // 128, 128), I32),
        ),
        in_specs=[VM, VM],
        out_specs=(VM, VM),
        compiler_params=PARAMS,
        name="route",
    )(owner, row)


def hot_where(high, value, low_hot):
    return jnp.where(high == value, low_hot, jnp.zeros_like(low_hot))


def fetch_kernel(req_ref, table_ref, out_ref, got):
    half = ROWS // 2
    both = jnp.concatenate([table_ref[:half, :], table_ref[half:, :]], axis=1)
    for c0 in range(0, CAP, 4):
        hots, uppers = [], []
        for c in range(c0, c0 + 4):
            row = jnp.broadcast_to(req_ref[:, c : c + 1], (NOWN, 128))
            low = ((row & 127) == iota((NOWN, 128), 1)).astype(F32).astype(BF)
            high = ((row >> 7) & 7).astype(F32).astype(BF)
            hots.append(jnp.concatenate([hot_where(high, j, low) for j in range(8)], axis=1))
            uppers.append(row >= half)
        pair = dot(jnp.concatenate(hots, axis=0), both, 1, 0)
        rows = jnp.where(jnp.concatenate(uppers, axis=0), pair[:, 128:], pair[:, :128])
        for i in range(4):
            got[pl.ds(c0 + i, NOWN, stride=CAP), :] = rows[i * NOWN : (i + 1) * NOWN, :]
    out_ref[...] = got[...].astype(BF)


def fetch(req, table):
    return pl.pallas_call(
        fetch_kernel,
        out_shape=jax.ShapeDtypeStruct((SLOTS, 128), BF),
        in_specs=[VM, VM],
        out_specs=VM,
        scratch_shapes=[pltpu.VMEM((SLOTS, 128), F32)],
        compiler_params=PARAMS,
        name="fetch",
    )(req, table)


def column(row_vector):
    wide = jnp.broadcast_to(row_vector.astype(F32), (128, 128))
    return jnp.transpose(wide)


def place_kernel(slot_ref, back_ref, x_ref):
    half = SLOTS // 2
    both = jnp.concatenate([back_ref[:half, :], back_ref[half:, :]], axis=1)
    for b0 in range(0, TOK // 128, 2):
        hots, uppers = [], []
        for b in (b0, b0 + 1):
            slot = column(slot_ref[b : b + 1, :]).astype(I32)
            upper = slot >= half
            slot = jnp.where(upper, slot - half, slot)
            low = ((slot & 127) == iota((128, 128), 1)).astype(F32).astype(BF)
            high = (slot >> 7).astype(F32).astype(BF)
            hots.append(jnp.concatenate([hot_where(high, j, low) for j in range(half // 128)], axis=1))
            uppers.append(upper)
        pair = dot(jnp.concatenate(hots, axis=0), both, 1, 0)
        rows = jnp.where(jnp.concatenate(uppers, axis=0), pair[:, 128:], pair[:, :128])
        x_ref[b0 * 128 : b0 * 128 + 256, :] = rows.astype(BF)


def place(slot, back):
    return pl.pallas_call(
        place_kernel,
        out_shape=jax.ShapeDtypeStruct((TOK, 128), BF),
        in_specs=[VM, VM],
        out_specs=VM,
        compiler_params=PARAMS,
        name="place",
    )(slot, back)


def layer_kernel(
    pos_ref, core_ref, seg_ref, x0, x1, x2, x3, g0, g1, g2, g3, win_ref, wout_ref,
    mine_ref, other_ref, c0, c1, c2, c3,
    w, wo, pre, act, segc, aw, dsil, dkv, du, u_ref, y_ref, dp_ref, dw_ref,
):
    xs, gs = (x0, x1, x2, x3), (g0, g1, g2, g3)
    both = (c0, c1, c2, c3)
    me, core = pos_ref[0], core_ref[0]
    for k in range(NT):
        at = pl.multiple_of(lax.rem(me + FAR[k], NT) * 128, 128)
        for c in range(4):
            w[k * 128 : (k + 1) * 128, c * 128 : (c + 1) * 128] = win_ref[c, pl.ds(at, 128), :]
        wo[:, k * 128 : (k + 1) * 128] = wout_ref[:, pl.ds(at, 128)]
    for b in range(TOK // 128):
        segc[b * 128 : (b + 1) * 128, :] = column(
            seg_ref[0:1, b * 128 : (b + 1) * 128]
        )

    def stats(r0, n):
        x = [r[r0 : r0 + n, :].astype(F32) for r in xs]
        mean = jnp.sum(x[0] + x[1] + x[2] + x[3], axis=1, keepdims=True) * (1.0 / D)
        x = [v - mean for v in x]
        var = jnp.sum(x[0] * x[0] + x[1] * x[1] + x[2] * x[2] + x[3] * x[3], axis=1, keepdims=True)
        scale = lax.rsqrt(var * (1.0 / D) + 1e-05)
        return [v * scale for v in x], scale

    step = 64
    for q in range(TOK // QB):
        lo = q * QB
        for r0 in range(lo, lo + QB, step):
            n, _ = stats(r0, step)
            for k in range(NT):
                u_ref[r0 : r0 + step, k * 128 : (k + 1) * 128] = n[k].astype(BF)
        pre[lo : lo + QB, :] = dot(u_ref[lo : lo + QB, :], w[...], 1, 0)
        for r0 in range(lo, lo + QB, step):
            p = pre[r0 : r0 + step, :]
            s = 0.5 + 0.5 * jnp.tanh(0.5 * p)
            ps = p * s
            act[r0 : r0 + step, :] = ps.astype(BF)
            pre[r0 : r0 + step, :] = s + ps * (1.0 - s)

    dkv[...] = jnp.zeros((TOK, 256), F32)
    for q in range(TOK // QB):
        lo = q * QB
        k0 = max(0, lo - SEQ_MOST)
        width = lo + QB - k0
        queries = act[lo : lo + QB, 256:384]
        o = jnp.zeros((QB, HD), F32)
        for kb in range(k0, lo + QB, QB):
            sc = dot(queries, act[kb : kb + QB, 384:512], 1, 1) * (HD ** (-0.5))
            for j in range(0, QB, 128):
                at = kb - k0 + j
                first, last = 0, QB
                if kb == lo and j:
                    first = j
                if lo - kb == SEQ_MOST and j + 128 < QB:
                    last = j + 128
                rows = slice(first, last)
                same = segc[lo + first : lo + last, :] == seg_ref[0:1, kb + j : kb + j + 128].astype(F32)
                if kb == lo:
                    shape = (last - first, 128)
                    same = same & (iota(shape, 1) + j <= iota(shape, 0) + first)
                v = sc[rows, j : j + 128]
                s = 0.5 + 0.5 * jnp.tanh(0.5 * v)
                vs = v * s
                aw[rows, at : at + 128] = jnp.where(same, vs * (1.0 / SEQ_MOST), 0.0).astype(BF)
                dsil[rows, at : at + 128] = jnp.where(
                    same, (s + vs * (1.0 - s)) * (HD ** (-0.5) / SEQ_MOST), 0.0
                )
                if first:
                    aw[0:first, at : at + 128] = jnp.zeros((first, 128), BF)
                    dsil[0:first, at : at + 128] = jnp.zeros((first, 128), F32)
                if last < QB:
                    aw[last:QB, at : at + 128] = jnp.zeros((QB - last, 128), BF)
                    dsil[last:QB, at : at + 128] = jnp.zeros((QB - last, 128), F32)
        o = dot(aw[:, 0:width], act[k0 : lo + QB, 128:256], 1, 0)
        gate = act[lo : lo + QB, 0:128].astype(F32)
        mean = jnp.sum(o, axis=1, keepdims=True) * (1.0 / HD)
        o = o - mean
        scale = lax.rsqrt(jnp.sum(o * o, axis=1, keepdims=True) * (1.0 / HD) + 1e-05)
        n = o * scale
        y_ref[lo : lo + QB, :] = (n * gate).astype(BF)
        dy = dot(gs[0][lo : lo + QB, :], wo[:, 0:128], 1, 1)
        for k in range(1, NT):
            dy = dy + dot(gs[k][lo : lo + QB, :], wo[:, k * 128 : (k + 1) * 128], 1, 1)
        dy = dy.astype(BF).astype(F32)
        dgate = (dy * n).astype(BF).astype(F32)
        dn = dy * gate
        m1 = jnp.sum(dn, axis=1, keepdims=True) * (1.0 / HD)
        m2 = jnp.sum(dn * n, axis=1, keepdims=True) * (1.0 / HD)
        do = ((dn - m1 - n * m2) * scale).astype(BF)
        dp_ref[lo : lo + QB, 0:128] = (dgate * pre[lo : lo + QB, 0:128]).astype(BF)
        dq = jnp.zeros((QB, HD), F32)
        for kb in range(k0, lo + QB, QB):
            at = kb - k0
            da = dot(do, act[kb : kb + QB, 128:256], 1, 1).astype(BF).astype(F32)
            ds = (da * dsil[:, at : at + QB]).astype(BF)
            dq = dq + dot(ds, act[kb : kb + QB, 384:512], 1, 0)
            dkv[kb : kb + QB, 0:128] += dot(aw[:, at : at + QB], do, 0, 0)
            dkv[kb : kb + QB, 128:256] += dot(ds, queries, 0, 0)
        dq = dq.astype(BF).astype(F32)
        dp_ref[lo : lo + QB, 256:384] = (dq * pre[lo : lo + QB, 256:384]).astype(BF)

    for q in range(TOK // QB):
        lo = q * QB
        dvb = dkv[lo : lo + QB, 0:128].astype(BF).astype(F32)
        dkb = dkv[lo : lo + QB, 128:256].astype(BF).astype(F32)
        dp_ref[lo : lo + QB, 128:256] = (dvb * pre[lo : lo + QB, 128:256]).astype(BF)
        dp_ref[lo : lo + QB, 384:512] = (dkb * pre[lo : lo + QB, 384:512]).astype(BF)
        du[...] = dot(dp_ref[lo : lo + QB, :], w[...], 1, 1).astype(BF).astype(F32)
        for r in range(0, QB, step):
            n, scale = stats(lo + r, step)
            d = [du[r : r + step, k * 128 : (k + 1) * 128] for k in range(NT)]
            m1 = jnp.sum(d[0] + d[1] + d[2] + d[3], axis=1, keepdims=True) * (1.0 / D)
            m2 = jnp.sum(
                d[0] * n[0] + d[1] * n[1] + d[2] * n[2] + d[3] * n[3], axis=1, keepdims=True
            ) * (1.0 / D)
            for k in range(NT):
                both[k][lo + r : lo + r + step, :] = ((d[k] - m1 - n[k] * m2) * scale).astype(BF)

    for k in range(NT):
        at = pl.multiple_of(lax.rem(me + FAR[k], NT) * 128, 128)
        dw = dot(u_ref[:, k * 128 : (k + 1) * 128], dp_ref[...], 0, 0)
        for c in range(4):
            dw_ref[pl.ds(pl.multiple_of(c * 512 + at, 128), 128), :] = dw[:, c * 128 : (c + 1) * 128]
        dw_ref[pl.ds(pl.multiple_of(2048 + at, 128), 128), :] = dot(y_ref[...], gs[k][...], 0, 0)
        both[k][TOK:, :] = dot(y_ref[...], wo[:, k * 128 : (k + 1) * 128], 1, 0).astype(BF)
    mine_ref[...] = dw_ref[pl.ds(pl.multiple_of(core * 1280, 1280), 1280), :]
    other_ref[...] = dw_ref[pl.ds(pl.multiple_of(1280 - core * 1280, 1280), 1280), :].astype(BF)


def layer(pos, core, seg, xs, gs, w_in, w_out):
    pair = jax.ShapeDtypeStruct((2 * TOK, 128), BF)
    return pl.pallas_call(
        layer_kernel,
        out_shape=(jax.ShapeDtypeStruct((1280, 128), F32), jax.ShapeDtypeStruct((1280, 128), BF))
        + (pair,) * 4,
        in_specs=[SM, SM] + [VM] * 11,
        out_specs=(VM,) * 6,
        scratch_shapes=[
            pltpu.VMEM((D, 512), BF),
            pltpu.VMEM((HD, D), BF),
            pltpu.VMEM((TOK, 512), F32),
            pltpu.VMEM((TOK, 512), BF),
            pltpu.VMEM((TOK, 128), F32),
            pltpu.VMEM((QB, 768), BF),
            pltpu.VMEM((QB, 768), F32),
            pltpu.VMEM((TOK, 256), F32),
            pltpu.VMEM((QB, 512), F32),
            pltpu.VMEM((TOK, D), BF),
            pltpu.VMEM((TOK, HD), BF),
            pltpu.VMEM((TOK, 512), BF),
            pltpu.VMEM((2560, 128), F32),
        ],
        compiler_params=PARAMS,
        name="layer",
    )(pos, core, seg, *xs, *gs, w_in, w_out)


def spread(at_ref, blocks, size, values):
    lows, highs, pairs = [], [], []
    for b in range(blocks):
        at = at_ref[b : b + 1, :]
        upper = column((at >= size).astype(F32)) > 0.5
        value = values[b * 128 : (b + 1) * 128, :]
        pairs.append(
            jnp.concatenate([jnp.where(upper, 0.0, value), jnp.where(upper, value, 0.0)], axis=1).astype(BF)
        )
        at = jnp.broadcast_to(jnp.where(at >= size, at - size, at), (128, 128))
        lows.append(((at & 127) == iota((128, 128), 0)).astype(F32).astype(BF))
        highs.append((at >> 7).astype(F32).astype(BF))
    low = jnp.concatenate(lows, axis=1)
    high = jnp.concatenate(highs, axis=1)
    pair = jnp.concatenate(pairs, axis=0)
    return [dot(hot_where(high, s, low), pair, 1, 0) for s in range(size // 128)]


def slots_kernel(slot_ref, grad_ref, d0, d1, d2, d3, out_ref):
    dx = grad_ref[...].astype(F32) + (
        d0[...].astype(F32) + d1[...].astype(F32) + d2[...].astype(F32) + d3[...].astype(F32)
    )
    half = SLOTS // 2
    for s, both in enumerate(spread(slot_ref, TOK // 128, half, dx)):
        out_ref[s * 128 : (s + 1) * 128, :] = both[:, :128].astype(BF)
        out_ref[half + s * 128 : half + (s + 1) * 128, :] = both[:, 128:].astype(BF)


def to_slots(slot, grad, parts):
    top = pl.BlockSpec((TOK, 128), lambda i: (0, 0))
    return pl.pallas_call(
        slots_kernel,
        out_shape=jax.ShapeDtypeStruct((SLOTS, 128), BF),
        grid=(1,),
        in_specs=[pl.BlockSpec((TOK // 128, 128), lambda i: (0, 0))] + [top] * 5,
        out_specs=pl.BlockSpec((SLOTS, 128), lambda i: (0, 0)),
        compiler_params=PARAMS,
        name="to_slots",
    )(slot, grad, *parts)


def add_rows_kernel(req_ref, arrived_ref, out_ref):
    half = ROWS // 2
    for s, both in enumerate(spread(req_ref, SLOTS // 128, half, arrived_ref[...].astype(F32))):
        out_ref[s * 128 : (s + 1) * 128, :] = both[:, :128]
        out_ref[half + s * 128 : half + (s + 1) * 128, :] = both[:, 128:]


def add_rows(req, arrived):
    return pl.pallas_call(
        add_rows_kernel,
        out_shape=jax.ShapeDtypeStruct((ROWS, 128), F32),
        in_specs=[VM, VM],
        out_specs=VM,
        compiler_params=PARAMS,
        name="add_rows",
    )(req, arrived)


def unpack_kernel(y_ref, p0, p1, p2, p3, in_ref, out_ref, whole):
    for k, p in enumerate((p0, p1, p2, p3)):
        half, quarter = y_place(lax.rem(y_ref[0] + FAR[k], 4))
        for core in range(2):
            at = pl.multiple_of(half * 640 + quarter * 320 + core * 1280, 320)
            whole[pl.ds(at, 320), :] = p[core * 320 : (core + 1) * 320, :].astype(F32)
    in_ref[...] = whole[0:2048, :]
    for k in range(NT):
        out_ref[:, k * 128 : (k + 1) * 128] = whole[2048 + k * 128 : 2176 + k * 128, :]


def unpack(y, parts):
    return pl.pallas_call(
        unpack_kernel,
        out_shape=(jax.ShapeDtypeStruct((2048, 128), F32), jax.ShapeDtypeStruct((HD, D), F32)),
        in_specs=[SM] + [VM] * 4,
        out_specs=(VM, VM),
        scratch_shapes=[pltpu.VMEM((2560, 128), F32)],
        compiler_params=PARAMS,
        name="unpack",
    )(y, *parts)


def shift(x, axis, fn, n):
    return lax.ppermute(x, axis, [(i, fn(i)) for i in range(n)])


def gather_pieces(x):
    return [x] + [shift(x, "tensor", lambda i, k=k: (i - k) % NT, NT) for k in FAR[1:]]


def scatter_pieces(parts):
    return [parts[0]] + [
        shift(parts[i], "tensor", lambda j, k=FAR[i]: (j + k) % NT, NT) for i in range(1, NT)
    ]


def pick(x, i):
    return lax.dynamic_index_in_dim(x, i, 0, keepdims=False)


def y_place(y):
    return ((y == 1) | (y == 2)).astype(I32), (y >= 2).astype(I32)


def reduce_over_chips(mine, other):
    half, quarter = y_place(lax.axis_index("table") // 2)
    other = shift(other, "table", lambda i: i ^ 1, 8)
    mine = (mine + other.astype(F32)).reshape(2, 640, 128)
    got = shift(pick(mine, 1 - half).astype(BF), "table", lambda i: i ^ 2, 8)
    mine = (pick(mine, half) + got.astype(F32)).reshape(2, 320, 128)
    got = shift(pick(mine, 1 - quarter).astype(BF), "table", lambda i: 6 - (i & 6) + (i & 1), 8)
    return pick(mine, quarter), got


def add_step(total, mask):
    return (total.astype(F32) + shift(total, "seq", lambda i: i ^ mask, 8).astype(F32)).astype(BF)


def add_group(total):
    got = [shift(total, "seq", lambda i, k=k: i ^ k, 8) for k in (1, 2, 3)]
    for other in got:
        total = total.astype(F32) + other.astype(F32)
    return total.astype(BF)


def gather_weights(total, add):
    y = (lax.axis_index("table") // 2).astype(I32).reshape(1)
    pairs = [[2 * i, 2 * i + 1] for i in range(4)]
    both = lax.all_gather(total, "table", axis=0, tiled=True, axis_index_groups=pairs)
    parts = [both] + [shift(both, "table", lambda i, k=k: (i - 2 * k) % 8, 8) for k in FAR[1:]]
    table_grad = add()
    parts, table_grad = lax.optimization_barrier((parts, table_grad))
    return unpack(y, parts), table_grad


def body(table, owner, local_row, segment_ids, proj_in, proj_out, grad_out):
    pos = lax.axis_index("tensor").astype(I32).reshape(1)
    core = (lax.axis_index("table") % 2).astype(I32).reshape(1)
    requests, slot = route(owner.reshape(8, 128), local_row.reshape(8, 128))
    gs = gather_pieces(grad_out)
    received = lax.all_to_all(requests, BOTH, split_axis=0, concat_axis=0, tiled=True)
    rows = fetch(received, table)
    flat = received[:, :CAP].reshape(SLOTS // 128, 128)
    back = lax.all_to_all(rows.reshape(NOWN, CAP, 128), BOTH, split_axis=0, concat_axis=0, tiled=True)
    back, flat = lax.optimization_barrier((back, flat))
    x = place(slot, back.reshape(SLOTS, 128))
    xs = gather_pieces(x)
    mine, other, c0, c1, c2, c3 = layer(pos, core, segment_ids, xs, gs, proj_in, proj_out)
    cparts = scatter_pieces([c0, c1, c2, c3])
    own, got = reduce_over_chips(mine, other)
    got, cparts[3] = lax.optimization_barrier((got, cparts[3]))
    total = add_group((own + got.astype(F32)).astype(BF))
    cparts, _ = lax.optimization_barrier((cparts, total))
    grads = to_slots(slot, grad_out, cparts)
    total = add_step(total, 7)
    grads, total = lax.optimization_barrier((grads, total))
    arrived = lax.all_to_all(grads.reshape(NOWN, CAP, 128), BOTH, split_axis=0, concat_axis=0, tiled=True)
    (grad_in, grad_outw), table_grad = gather_weights(
        total, lambda: add_rows(flat, arrived.reshape(SLOTS, 128))
    )
    layer_out = (
        x.astype(F32)
        + (
            cparts[0][TOK:].astype(F32)
            + cparts[1][TOK:].astype(F32)
            + cparts[2][TOK:].astype(F32)
            + cparts[3][TOK:].astype(F32)
        )
    ).astype(BF)
    return layer_out, table_grad, grad_in.reshape(4, D, 128), grad_outw


def solution(mesh):
    in_specs = (
        P(BOTH, "tensor"),
        P(BOTH, None),
        P(BOTH),
        P(BOTH, None),
        P(None, None, "tensor"),
        P("tensor", None),
        P(BOTH, "tensor"),
    )
    out_specs = (
        P(BOTH, "tensor"),
        P(BOTH, "tensor"),
        P(None, None, "tensor"),
        P("tensor", None),
    )
    return jax.shard_map(body, mesh=mesh, in_specs=in_specs, out_specs=out_specs, check_vma=False)
```
